32 devices in a mesh: member: 4 (over y, core), dx: 4 (over z), dy: 2 (over x).
Axes of the slice: x: 2, y: 2, z: 4, core: 2. Of those that a mesh axis runs over, the one named last changes fastest.
Arguments:
- perturbed_states: float32 [4, 4, 8, 64, 256], P('member', None, None, 'dx', 'dy'), may hold values from -6 to 6
- control: float32 [4, 4, 8, 64, 256], P('member', None, None, 'dx', 'dy'), may hold values from -6 to 6
- owner: int32 [4], replicated, may hold values from 0 to 3, each once
- map_factor: float32 [64, 256], P('dx', 'dy'), may hold values from 0.5 to 2
- terrain: int32 [64, 256], P('dx', 'dy'), may hold values from 0 to 3
Outputs:
- forecast: float32 [4, 4, 8, 64, 256], P('member', None, None, 'dx', 'dy')
The draws below stay inside these ranges and needn't reach their ends.
Inputs may be any that keep to these rules, and one draw needn't show every extreme that they name: `owner`: a permutation of the member indices.
All inputs are finite; a program needn't handle non-finite values.
Results may differ from the reference program's by a relative error of at most 0.0003.
Values sent between devices are 32-bit elements; how exact they have to be, the bound alone decides.
No kernel may reach another device: no remote copies, remote signals or barrier semaphores. Data moves between devices by JAX's collectives and lax.ppermute only.
A program may use at most 64 MiB of HBM per device.

```python
import math
import jax
import jax.numpy as jnp
from jax import lax

PROGNOSTIC_VARS = 4
LEV = 8
STEPS = 4
ENS = 4
NX = 64
NY = 256


def touch_ends(drawn, own_key, low, top_value):
    spot = [jax.random.randint(jax.random.fold_in(own_key, axis), (), 0, length) for axis, length in enumerate(drawn.shape)]
    longest = drawn.shape.index(max(drawn.shape))
    beside = spot[:longest] + [(spot[longest] + 1) % drawn.shape[longest]] + spot[longest + 1:]
    return drawn.at[tuple(spot)].set(low).at[tuple(beside)].set(top_value)


def steps_of(rng, dims, shards, least, top_value):
    def one(dim, blocks):
        steps = jax.random.uniform(jax.random.fold_in(jax.random.fold_in(rng, 6), dim), (blocks,), jnp.float32, least / len(shards), top_value / len(shards))
        return jnp.repeat(jnp.exp(steps), dims[dim] // blocks).reshape((-1,) + (1,) * (len(dims) - dim - 1))

    gain = one(*shards[0])
    for cut in shards[1:]:
        gain = gain * one(*cut)
    return gain


def scatter_about(rng, shape, scale, most, shards=(), held_as=jnp.bfloat16):
    array = scale * jax.random.normal(rng, shape, jnp.float32)
    if shards:
        array = array * steps_of(rng, shape, shards, -0.22, 0.18)
    return jnp.clip(array, -most, most).astype(held_as)


def setup_inputs(seed: int = 0) -> dict:
    seeds = jax.random.split(jax.random.key(seed), 6)
    perturbed_states = scatter_about(seeds[0], (ENS, PROGNOSTIC_VARS, LEV, NX, NY), 1.0, 6.0, ((0, 4), (3, 4), (4, 2)), jnp.float32)
    control = scatter_about(seeds[1], (ENS, PROGNOSTIC_VARS, LEV, NX, NY), 1.0, 6.0, ((0, 4), (3, 4), (4, 2)), jnp.float32)
    owner = jax.random.permutation(seeds[2], ENS).astype(jnp.int32)
    map_factor = jnp.clip(jnp.exp(math.log(2.0) - 1.3862944 * jax.random.uniform(seeds[3], (NX, NY), jnp.float32) ** steps_of(seeds[3], (NX, NY), ((0, 4), (1, 2)), -0.2, 0.2)), 0.5, 2.0)
    terrain = touch_ends(jax.random.randint(seeds[4], (NX, NY), 0, LEV // 2), jax.random.fold_in(seeds[4], 1), 0, (LEV // 2) - 1).astype(jnp.int32)
    return dict(perturbed_states=perturbed_states, control=control, owner=owner, map_factor=map_factor, terrain=terrain)


integration_step = 0.2
diffusion = 0.1


def advance(padded, metric, vertical_level_mask):
    middle_point = padded[:, :, 1:-1, 1:-1]
    east = padded[:, :, 2:, 1:-1]
    west = padded[:, :, :-2, 1:-1]
    north = padded[:, :, 1:-1, 2:]
    south = padded[:, :, 1:-1, :-2]
    gradient_along_x = (east - west) * 0.5
    grad_y = (north - south) * 0.5
    stacked = jnp.pad(middle_point, ((0, 0), (1, 1), (0, 0), (0, 0)))
    laplace = east + west + north + south + stacked[:, 2:] + stacked[:, :-2] - 6.0 * middle_point
    wind_x = middle_point[0]
    meridional_velocity = middle_point[1]
    trend = -metric * (wind_x * gradient_along_x + meridional_velocity * grad_y) + diffusion * laplace
    extra = jnp.stack([-metric * gradient_along_x[2], -metric * grad_y[2], -metric * (gradient_along_x[0] + grad_y[1]), jnp.zeros_like(wind_x)])
    return vertical_level_mask * (middle_point + integration_step * (trend + extra))


def rank_weights(owner):
    ranks = lax.broadcasted_iota(jnp.int32, (ENS, ENS), 0)
    members = lax.broadcasted_iota(jnp.int32, (ENS, ENS), 1)
    per_rank = 2.0 * (ENS - ranks.astype(jnp.float32)) / (ENS * (ENS + 1.0))
    hits = owner[:, None].astype(jnp.int32) == members
    return jnp.sum(jnp.where(hits, per_rank, jnp.zeros_like(per_rank)), axis=0)


def reference(perturbed_states, control, owner, map_factor, terrain):
    mean = jnp.sum(perturbed_states, axis=0) / ENS
    weight = rank_weights(owner)
    chosen = jnp.tensordot(weight, control, axes=1)
    levels = lax.broadcasted_iota(jnp.int32, (LEV, NX, NY), 0)
    vertical_level_mask = (levels >= terrain[None].astype(jnp.int32)).astype(jnp.float32)

    def predict_sample_state(sample_state):
        state = chosen + sample_state - mean
        for number in range(STEPS):
            padded = jnp.pad(state, ((0, 0), (0, 0), (1, 1), (1, 1)))
            state = advance(padded, map_factor, vertical_level_mask)
        return state

    return lax.map(predict_sample_state, perturbed_states)
```

```python
import functools

import jax
import jax.numpy as jnp
from jax import lax
from jax.experimental import pallas as pl
from jax.experimental.pallas import tpu as pltpu
from jax.sharding import PartitionSpec as P

STEPS = 4

integration_step = 0.2
diffusion = 0.1

OUTSIDE = 1.0e6
AXES = ("member", "dx", "dy")
VMEM = pl.BlockSpec(memory_space=pltpu.VMEM)
SMEM = pl.BlockSpec(memory_space=pltpu.SMEM)


def send(value, target):
    sizes = [lax.axis_size(axis) for axis in AXES]
    pairs = []
    for member in range(sizes[0]):
        for i in range(sizes[1]):
            for j in range(sizes[2]):
                k, l, m = target(member, i, j)
                pairs.append(
                    (
                        (member * sizes[1] + i) * sizes[2] + j,
                        (k * sizes[1] + l) * sizes[2] + m,
                    )
                )
    return lax.ppermute(value, AXES, pairs)


def loop_target(rows, forward):
    def target(member, i, j):
        step = 1 if (member % 2 == 0) == forward else -1
        if 0 <= i + step < rows:
            return member, i + step, j
        return member ^ 1, i, j

    return target


def lanes_of(shape):
    return lax.broadcasted_iota(jnp.int32, shape, len(shape) - 1)


def turn(tile, by, axis=1):
    return pltpu.roll(tile, by % tile.shape[axis], axis)


def edges_of(tiles, width):
    lane = lanes_of(tiles[0].shape)
    total = None
    for x, tile in enumerate(tiles):
        moved = turn(tile, 2 * width * x + width)
        total = moved if total is None else jnp.where(lane < 2 * width * x, total, moved)
    return total


def split_kernel(p_ref, c_ref, owner_ref, m_ref, t_ref, pt_ref, keep_ref, send_ref, more_ref):
    fields, _, cols = p_ref.shape
    rows = m_ref.shape[0]
    levels = p_ref.shape[1] // rows
    half = rows // 2
    member = lax.axis_index("member")
    members = owner_ref.shape[0]
    first = lax.rem(member, 2) == 0
    weight = jnp.float32(0.0)
    for rank in range(members):
        per_rank = 2.0 * (members - rank) / (members * (members + 1.0))
        weight = weight + jnp.where(owner_ref[rank] == member, per_rank, 0.0)
    for f in range(fields):
        states, parts = [], []
        for x in range(rows):
            state = p_ref[f, pl.ds(x, levels, stride=rows), :]
            analysis = c_ref[f, pl.ds(x, levels, stride=rows), :]
            pt_ref[x * fields + f] = state
            states.append(state)
            parts.append(weight * analysis - state * (1.0 / members))
        for x in range(half):
            keep_ref[x * fields + f] = jnp.where(first, parts[x], parts[x + half])
            send_ref[x * fields + f] = jnp.where(first, parts[x + half], parts[x])
        send_ref[half * fields + f] = edges_of(parts, STEPS)
        more_ref[f] = edges_of(states, STEPS)
    level = lax.broadcasted_iota(jnp.int32, (levels, cols), 0)
    columns = []
    for x in range(rows):
        scale = jnp.broadcast_to(m_ref[pl.ds(x, 1), :], (levels, cols))
        ground = jnp.broadcast_to(t_ref[pl.ds(x, 1), :].astype(jnp.float32), (levels, cols))
        columns.append(jnp.where(level == 0, scale, ground))
    more_ref[fields] = edges_of(columns, STEPS)


def join_kernel(
    sizes, n_left, pt_ref, mine_ref, other_ref, m_ref, t_ref, more_ref, *refs
):
    left, rest = refs[:n_left], refs[n_left:]
    right, rest = rest[:n_left], rest[n_left:]
    start_ref, strip_ref, first_ref, second_ref = rest
    rows, cols = m_ref.shape
    levels = pt_ref.shape[1]
    fields = pt_ref.shape[0] // rows
    half, wide = rows // 2, STEPS
    parity = lax.rem(lax.axis_index("member"), 2)
    place = lax.axis_index("dy")
    has_left, has_right = place > 0, place < sizes[2] - 1
    for r in range(half):
        for f in range(fields):
            near = (parity * half + r) * fields + f
            far = ((1 - parity) * half + r) * fields + f
            start_ref[near] = pt_ref[near] + mine_ref[r * fields + f]
            start_ref[far] = pt_ref[far] + other_ref[r * fields + f]
    lane = lanes_of((levels, cols))
    early = lax.rem(lane, 2 * wide) < wide
    quarter = 2 * wide * wide

    def strips(own, before, after):
        a = jnp.where(early, before, own)
        b = jnp.where(early, own, after)
        ends = jnp.where(
            lane < quarter,
            a,
            jnp.where(
                lane < 2 * quarter,
                turn(b, quarter),
                jnp.where(lane < cols - quarter, turn(b, -quarter), a),
            ),
        )
        return a, b, ends

    def beside(parts, f):
        total = parts[0][fields + f] + parts[0][f]
        for part in parts[1:]:
            total = total + part[f]
        return total

    ends = []
    for f in range(fields):
        own = edges_of([start_ref[x * fields + f] for x in range(rows)], wide)
        before = jnp.where(has_left, beside(left, f), 0.0)
        after = jnp.where(has_right, beside(right, f), 0.0)
        a, b, end = strips(own, before, after)
        strip_ref[f] = a
        strip_ref[fields + 1 + f] = b
        ends.append(end)
    a, b, end = strips(
        more_ref[fields],
        jnp.where(has_left, left[0][2 * fields], OUTSIDE),
        jnp.where(has_right, right[0][2 * fields], OUTSIDE),
    )
    strip_ref[fields] = a
    strip_ref[2 * fields + 1] = b
    ends.append(end)
    scale, ground = m_ref[...], t_ref[...].astype(jnp.float32)
    tops = jnp.concatenate([scale[rows - wide :], ground[rows - wide :]], axis=0)
    bottoms = jnp.concatenate([scale[:wide], ground[:wide]], axis=0)
    for message, up in ((first_ref, parity == 0), (second_ref, parity == 1)):
        base = jnp.where(up, rows - wide, 0) * fields
        for k in range(wide * fields):
            message[k] = start_ref[base + k]
        for k, end in enumerate(ends):
            message[wide * fields + k] = end
        message[wide * fields + fields + 1] = jnp.where(up, tops, bottoms)


def forecast_kernel(
    sizes, start_ref, strip_ref, m_ref, t_ref, first_ref, second_ref, out_ref, a_ref, b_ref, coef_ref
):
    rows, cols = m_ref.shape
    levels = start_ref.shape[1]
    fields = start_ref.shape[0] // rows
    wide = STEPS
    group = 2 * wide
    tall = rows + 2 * wide
    parity = lax.rem(lax.axis_index("member"), 2)
    place = lax.axis_index("dx")
    has_low, has_high = place > 0, place < sizes[1] - 1
    lane = lanes_of((levels, cols))
    level = lax.broadcasted_iota(jnp.int32, (levels, cols), 0)
    quarter = group * wide
    even = parity == 0

    def low(k):
        return jnp.where(even, first_ref[k], second_ref[k])

    def high(k):
        return jnp.where(even, second_ref[k], first_ref[k])

    def coefficients(scale, ground):
        mask = (level.astype(jnp.float32) >= ground).astype(jnp.float32)
        return (
            mask * (1.0 - 6.0 * integration_step * diffusion),
            mask * (integration_step * diffusion),
            mask * (scale * (0.5 * integration_step)),
        )

    def wide_row(row):
        return jnp.broadcast_to(row, (levels, cols))

    for k in range(wide * fields):
        a_ref[k] = jnp.where(has_low, low(k), 0.0)
        a_ref[(rows + wide) * fields + k] = jnp.where(has_high, high(k), 0.0)
    for k in range(rows * fields):
        a_ref[wide * fields + k] = start_ref[k]
    metric = wide * fields + fields + 1
    below, above = low(metric), high(metric)
    below = jnp.where(has_low, below, OUTSIDE)
    above = jnp.where(has_high, above, OUTSIDE)
    for x in range(tall):
        if x < wide:
            scale, ground = below[x : x + 1], below[wide + x : wide + x + 1]
        elif x < wide + rows:
            scale = m_ref[pl.ds(x - wide, 1), :]
            ground = t_ref[pl.ds(x - wide, 1), :].astype(jnp.float32)
        else:
            r = x - wide - rows
            scale, ground = above[r : r + 1], above[wide + r : wide + r + 1]
        for k, value in enumerate(coefficients(wide_row(scale), wide_row(ground))):
            coef_ref[3 * x + k] = value

    def stretched(k, empty):
        mine_a = turn(strip_ref[k], quarter)
        mine_b = turn(strip_ref[fields + 1 + k], quarter)
        under, over = low(wide * fields + k), high(wide * fields + k)
        under = jnp.where(has_low, under, empty)
        over = jnp.where(has_high, over, empty)
        blank = jnp.full((levels, cols), empty, jnp.float32)

        def end(own, other):
            return jnp.where(
                lane < quarter, own, jnp.where(lane < 2 * quarter, other, blank)
            )

        return (
            (
                jnp.where(lane < quarter, turn(under, quarter), mine_a),
                end(mine_a, turn(over, quarter)),
            ),
            (
                jnp.where(lane < quarter, turn(under, 2 * quarter), mine_b),
                end(mine_b, over),
            ),
        )

    strips = [stretched(f, 0.0) for f in range(fields)]
    strip_coefs = [
        [coefficients(wide_row(tile[0:1]), wide_row(tile[1:2])) for tile in side]
        for side in stretched(fields, OUTSIDE)
    ]

    def updated(coefs, cur, dx, sx, dy, sy):
        new = []
        for f in range(fields):
            advected = cur[0] * dx[f] + cur[1] * dy[f]
            if f == 0:
                advected = advected + dx[2]
            elif f == 1:
                advected = advected + dy[2]
            elif f == 2:
                advected = advected + (dx[0] + dy[1])
            upper = jnp.where(level < levels - 1, turn(cur[f], -1, 0), 0.0)
            lower = jnp.where(level > 0, turn(cur[f], 1, 0), 0.0)
            total = (sx[f] + sy[f]) + (upper + lower)
            new.append(coefs[0] * cur[f] + coefs[1] * total - coefs[2] * advected)
        return new

    def strip_step(tiles):
        new = [[[None, None], [None, None]] for _ in range(fields)]
        for side in range(2):
            for v in range(2):
                cur, dx, sx, dy, sy = [], [], [], [], []
                for f in range(fields):
                    one, two = tiles[f][side]
                    if v == 0:
                        east = jnp.where(lane < cols - group, turn(one, -group), turn(two, -group))
                        west = turn(one, group)
                    else:
                        east = turn(two, -group)
                        west = jnp.where(lane < group, turn(one, group), turn(two, group))
                    here = (one, two)[v]
                    north, south = turn(here, -1), turn(here, 1)
                    cur.append(here)
                    dx.append(east - west)
                    sx.append(east + west)
                    dy.append(north - south)
                    sy.append(north + south)
                result = updated(strip_coefs[side][v], cur, dx, sx, dy, sy)
                for f in range(fields):
                    new[f][side][v] = result[f]
        return new

    for number in range(STEPS):
        source = a_ref if number % 2 == 0 else b_ref
        sink = b_ref if number % 2 == 0 else a_ref
        beyond = [
            [
                jnp.where(lax.rem(lane, group) == wide - 1, a, turn(b, -2))
                for a, b in zip(strips[f][0], strips[f][1])
            ]
            for f in range(fields)
        ]
        bottom, top = number + 1, tall - number - 1
        rows_at = lambda x: [source[x * fields + f] for f in range(fields)]
        before, cur = rows_at(bottom - 1), rows_at(bottom)
        for x in range(bottom, top):
            after = rows_at(x + 1)
            dx, sx, dy, sy = [], [], [], []
            for f in range(fields):
                spot = group * x + wide - 1
                outer = turn(beyond[f][spot // cols], -(spot % cols))
                north = jnp.where(lane == cols - 1, outer, turn(cur[f], -1))
                south = jnp.where(lane == 0, outer, turn(cur[f], 1))
                dx.append(after[f] - before[f])
                sx.append(after[f] + before[f])
                dy.append(north - south)
                sy.append(north + south)
            coefs = [coef_ref[3 * x + k] for k in range(3)]
            new = updated(coefs, cur, dx, sx, dy, sy)
            for f in range(fields):
                if number == STEPS - 1:
                    out_ref[f, pl.ds(x - wide, levels, stride=rows), :] = new[f]
                else:
                    sink[x * fields + f] = new[f]
            before, cur = cur, after
        if number < STEPS - 1:
            strips = strip_step(strips)


def on_device(perturbed_states, control, owner, map_factor, terrain):
    _, fields, levels, rows, cols = perturbed_states.shape
    sizes = tuple(lax.axis_size(axis) for axis in AXES)
    members = sizes[0]
    half = rows // 2
    tile = (levels, cols)

    def tiles(count):
        return jax.ShapeDtypeStruct((count, *tile), jnp.float32)

    flat = (fields, levels * rows, cols)
    states, keep, give, more = pl.pallas_call(
        split_kernel,
        out_shape=(
            tiles(rows * fields),
            tiles(half * fields),
            tiles(half * fields + fields),
            tiles(fields + 1),
        ),
        in_specs=[VMEM, VMEM, SMEM, VMEM, VMEM],
        out_specs=(VMEM,) * 4,
        name="split",
    )(perturbed_states.reshape(flat), control.reshape(flat), owner, map_factor, terrain)

    given = send(give, lambda k, i, j: (k ^ 1, i, j))
    total = keep + given[: half * fields]
    edges = give[half * fields :] + given[half * fields :]

    chips = [b for b in range(2, members, 2)]
    bit = 2
    got = []
    while bit < members:
        got.append(send(total, lambda k, i, j, bit=bit: (k ^ bit, i, j)))
        total = total + got[-1]
        bit *= 2
    along = sizes[2]

    def from_side(step):
        there = lambda b: lambda k, i, j: (k ^ b, i, (j + step) % along)
        near = send(jnp.concatenate([edges, more], axis=0), there(0))
        return [near] + [send(edges, there(b)) for b in chips]

    left = from_side(1)
    right = left if along == 2 else from_side(-1)

    other = send(total, lambda k, i, j: (k ^ 1, i, j))
    count = STEPS * fields + fields + 2
    start, strips, first, second = pl.pallas_call(
        functools.partial(join_kernel, sizes, len(left)),
        out_shape=(tiles(rows * fields), tiles(2 * (fields + 1)), tiles(count), tiles(count)),
        in_specs=[VMEM] * (6 + 2 * len(left)),
        out_specs=(VMEM,) * 4,
        name="join",
    )(states, total, other, map_factor, terrain, more, *left, *right)
    first = send(first, loop_target(sizes[1], True))
    second = send(second, loop_target(sizes[1], False))
    out = pl.pallas_call(
        functools.partial(forecast_kernel, sizes),
        out_shape=jax.ShapeDtypeStruct(flat, jnp.float32),
        in_specs=[VMEM] * 6,
        out_specs=VMEM,
        scratch_shapes=[
            pltpu.VMEM(((rows + 2 * STEPS) * fields, *tile), jnp.float32),
            pltpu.VMEM(((rows + 2 * STEPS) * fields, *tile), jnp.float32),
            pltpu.VMEM(((rows + 2 * STEPS) * 3, *tile), jnp.float32),
        ],
        name="forecast",
    )(start, strips, map_factor, terrain, first, second)
    return out.reshape(perturbed_states.shape)


def solution(mesh):
    placed = (
        P("member", None, None, "dx", "dy"),
        P("member", None, None, "dx", "dy"),
        P(),
        P("dx", "dy"),
        P("dx", "dy"),
    )
    return jax.shard_map(
        on_device,
        mesh=mesh,
        in_specs=placed,
        out_specs=P("member", None, None, "dx", "dy"),
        check_vma=False,
    )
```

```python
import functools

import jax
import jax.numpy as jnp
from jax import lax
from jax.experimental import pallas as pl
from jax.experimental.pallas import tpu as pltpu
from jax.sharding import PartitionSpec as P

STEPS = 4

integration_step = 0.2
diffusion = 0.1

OUTSIDE = 1.0e6
AXES = ("member", "dx", "dy")
VMEM = pl.BlockSpec(memory_space=pltpu.VMEM)
HBM = pl.BlockSpec(memory_space=pltpu.HBM)
MODEST = pltpu.CompilerParams(vmem_limit_bytes=8 * 2**20)


def send(value, target):
    sizes = [lax.axis_size(axis) for axis in AXES]
    pairs = []
    for member in range(sizes[0]):
        for i in range(sizes[1]):
            for j in range(sizes[2]):
                k, l, m = target(member, i, j)
                pairs.append(
                    (
                        (member * sizes[1] + i) * sizes[2] + j,
                        (k * sizes[1] + l) * sizes[2] + m,
                    )
                )
    return lax.ppermute(value, AXES, pairs)


def loop_target(rows, forward):
    def target(member, i, j):
        step = 1 if (member % 2 == 0) == forward else -1
        if 0 <= i + step < rows:
            return member, i + step, j
        return member ^ 1, i, j

    return target


def lanes_of(shape):
    return lax.broadcasted_iota(jnp.int32, shape, len(shape) - 1)


def turn(tile, by, axis=1):
    return pltpu.roll(tile, by % tile.shape[axis], axis)


def edges_of(tiles, width):
    lane = lanes_of(tiles[0].shape)
    total = None
    for x, tile in enumerate(tiles):
        moved = turn(tile, 2 * width * x + width)
        total = moved if total is None else jnp.where(lane < 2 * width * x, total, moved)
    return total


def split_kernel(
    p_hbm, c_hbm, owner_hbm, m_hbm, t_hbm,
    pt_ref, keep_ref, send_ref, more_ref, metric_ref,
    p_ref, c_ref, owner_ref, t_ref, sems,
):
    fields, _, cols = p_ref.shape
    rows = t_ref.shape[0]
    levels = p_ref.shape[1] // rows
    half = rows // 2
    member = lax.axis_index("member")
    members = owner_ref.shape[0]
    first = lax.rem(member, 2) == 0
    copies = [pltpu.make_async_copy(owner_hbm, owner_ref, sems.at[0])]
    for f in range(fields):
        copies.append(pltpu.make_async_copy(p_hbm.at[f], p_ref.at[f], sems.at[1 + 2 * f]))
        copies.append(pltpu.make_async_copy(c_hbm.at[f], c_ref.at[f], sems.at[2 + 2 * f]))
    copies.append(
        pltpu.make_async_copy(m_hbm, metric_ref.at[pl.ds(0, rows), :], sems.at[1 + 2 * fields])
    )
    copies.append(pltpu.make_async_copy(t_hbm, t_ref, sems.at[2 + 2 * fields]))
    for copy in copies:
        copy.start()
    copies[0].wait()
    weight = jnp.float32(0.0)
    for rank in range(members):
        per_rank = 2.0 * (members - rank) / (members * (members + 1.0))
        weight = weight + jnp.where(owner_ref[rank] == member, per_rank, 0.0)
    for f in range(fields):
        copies[1 + 2 * f].wait()
        copies[2 + 2 * f].wait()
        states, parts = [], []
        for x in range(rows):
            state = p_ref[f, pl.ds(x, levels, stride=rows), :]
            analysis = c_ref[f, pl.ds(x, levels, stride=rows), :]
            pt_ref[x * fields + f] = state
            states.append(state)
            parts.append(weight * analysis - state * (1.0 / members))
        for x in range(half):
            keep_ref[x * fields + f] = jnp.where(first, parts[x], parts[x + half])
            send_ref[x * fields + f] = jnp.where(first, parts[x + half], parts[x])
        send_ref[half * fields + f] = edges_of(parts, STEPS)
        more_ref[f] = edges_of(states, STEPS)
    copies[-2].wait()
    copies[-1].wait()
    metric_ref[pl.ds(rows, rows), :] = t_ref[...].astype(jnp.float32)
    level = lax.broadcasted_iota(jnp.int32, (levels, cols), 0)
    columns = []
    for x in range(rows):
        scale = jnp.broadcast_to(metric_ref[pl.ds(x, 1), :], (levels, cols))
        ground = jnp.broadcast_to(metric_ref[pl.ds(rows + x, 1), :], (levels, cols))
        columns.append(jnp.where(level == 0, scale, ground))
    more_ref[fields] = edges_of(columns, STEPS)


def join_kernel(
    sizes, n_left, pt_ref, mine_ref, other_ref, metric_ref, more_ref, *refs
):
    left, rest = refs[:n_left], refs[n_left:]
    right, rest = rest[:n_left], rest[n_left:]
    start_ref, strip_ref, first_ref, second_ref = rest
    rows, cols = metric_ref.shape[0] // 2, metric_ref.shape[1]
    levels = pt_ref.shape[1]
    fields = pt_ref.shape[0] // rows
    half, wide = rows // 2, STEPS
    parity = lax.rem(lax.axis_index("member"), 2)
    place = lax.axis_index("dy")
    has_left, has_right = place > 0, place < sizes[2] - 1
    for r in range(half):
        for f in range(fields):
            near = (parity * half + r) * fields + f
            far = ((1 - parity) * half + r) * fields + f
            start_ref[near] = pt_ref[near] + mine_ref[r * fields + f]
            start_ref[far] = pt_ref[far] + other_ref[r * fields + f]
    lane = lanes_of((levels, cols))
    early = lax.rem(lane, 2 * wide) < wide
    quarter = 2 * wide * wide

    def strips(own, before, after):
        a = jnp.where(early, before, own)
        b = jnp.where(early, own, after)
        ends = jnp.where(
            lane < quarter,
            a,
            jnp.where(
                lane < 2 * quarter,
                turn(b, quarter),
                jnp.where(lane < cols - quarter, turn(b, -quarter), a),
            ),
        )
        return a, b, ends

    def beside(parts, f):
        total = parts[0][fields + f] + parts[0][f]
        for part in parts[1:]:
            total = total + part[f]
        return total

    ends = []
    for f in range(fields):
        own = edges_of([start_ref[x * fields + f] for x in range(rows)], wide)
        before = jnp.where(has_left, beside(left, f), 0.0)
        after = jnp.where(has_right, beside(right, f), 0.0)
        a, b, end = strips(own, before, after)
        strip_ref[f] = a
        strip_ref[fields + 1 + f] = b
        ends.append(end)
    a, b, end = strips(
        more_ref[fields],
        jnp.where(has_left, left[0][2 * fields], OUTSIDE),
        jnp.where(has_right, right[0][2 * fields], OUTSIDE),
    )
    strip_ref[fields] = a
    strip_ref[2 * fields + 1] = b
    ends.append(end)
    scale, ground = metric_ref[pl.ds(0, rows), :], metric_ref[pl.ds(rows, rows), :]
    tops = jnp.concatenate([scale[rows - wide :], ground[rows - wide :]], axis=0)
    bottoms = jnp.concatenate([scale[:wide], ground[:wide]], axis=0)
    for message, up in ((first_ref, parity == 0), (second_ref, parity == 1)):
        base = jnp.where(up, rows - wide, 0) * fields
        for k in range(wide * fields):
            message[k] = start_ref[base + k]
        for k, end in enumerate(ends):
            message[wide * fields + k] = end
        message[wide * fields + fields + 1] = jnp.where(up, tops, bottoms)


def forecast_kernel(
    sizes, start_ref, strip_ref, metric_ref, first_ref, second_ref, out_ref, a_ref, b_ref, coef_ref
):
    rows, cols = metric_ref.shape[0] // 2, metric_ref.shape[1]
    levels = start_ref.shape[1]
    fields = start_ref.shape[0] // rows
    wide = STEPS
    group = 2 * wide
    tall = rows + 2 * wide
    parity = lax.rem(lax.axis_index("member"), 2)
    place = lax.axis_index("dx")
    has_low, has_high = place > 0, place < sizes[1] - 1
    lane = lanes_of((levels, cols))
    level = lax.broadcasted_iota(jnp.int32, (levels, cols), 0)
    quarter = group * wide
    even = parity == 0

    def low(k):
        return jnp.where(even, first_ref[k], second_ref[k])

    def high(k):
        return jnp.where(even, second_ref[k], first_ref[k])

    def coefficients(scale, ground):
        mask = (level.astype(jnp.float32) >= ground).astype(jnp.float32)
        return (
            mask * (1.0 - 6.0 * integration_step * diffusion),
            mask * (integration_step * diffusion),
            mask * (scale * (0.5 * integration_step)),
        )

    def wide_row(row):
        return jnp.broadcast_to(row, (levels, cols))

    for k in range(wide * fields):
        a_ref[k] = jnp.where(has_low, low(k), 0.0)
        a_ref[(rows + wide) * fields + k] = jnp.where(has_high, high(k), 0.0)
    for k in range(rows * fields):
        a_ref[wide * fields + k] = start_ref[k]
    metric = wide * fields + fields + 1
    below, above = low(metric), high(metric)
    below = jnp.where(has_low, below, OUTSIDE)
    above = jnp.where(has_high, above, OUTSIDE)
    for x in range(tall):
        if x < wide:
            scale, ground = below[x : x + 1], below[wide + x : wide + x + 1]
        elif x < wide + rows:
            scale = metric_ref[pl.ds(x - wide, 1), :]
            ground = metric_ref[pl.ds(rows + x - wide, 1), :]
        else:
            r = x - wide - rows
            scale, ground = above[r : r + 1], above[wide + r : wide + r + 1]
        for k, value in enumerate(coefficients(wide_row(scale), wide_row(ground))):
            coef_ref[3 * x + k] = value

    def stretched(k, empty):
        mine_a = turn(strip_ref[k], quarter)
        mine_b = turn(strip_ref[fields + 1 + k], quarter)
        under, over = low(wide * fields + k), high(wide * fields + k)
        under = jnp.where(has_low, under, empty)
        over = jnp.where(has_high, over, empty)
        blank = jnp.full((levels, cols), empty, jnp.float32)

        def end(own, other):
            return jnp.where(
                lane < quarter, own, jnp.where(lane < 2 * quarter, other, blank)
            )

        return (
            (
                jnp.where(lane < quarter, turn(under, quarter), mine_a),
                end(mine_a, turn(over, quarter)),
            ),
            (
                jnp.where(lane < quarter, turn(under, 2 * quarter), mine_b),
                end(mine_b, over),
            ),
        )

    strips = [stretched(f, 0.0) for f in range(fields)]
    strip_coefs = [
        [coefficients(wide_row(tile[0:1]), wide_row(tile[1:2])) for tile in side]
        for side in stretched(fields, OUTSIDE)
    ]

    def updated(coefs, cur, dx, sx, dy, sy):
        new = []
        for f in range(fields):
            advected = cur[0] * dx[f] + cur[1] * dy[f]
            if f == 0:
                advected = advected + dx[2]
            elif f == 1:
                advected = advected + dy[2]
            elif f == 2:
                advected = advected + (dx[0] + dy[1])
            upper = jnp.where(level < levels - 1, turn(cur[f], -1, 0), 0.0)
            lower = jnp.where(level > 0, turn(cur[f], 1, 0), 0.0)
            total = (sx[f] + sy[f]) + (upper + lower)
            new.append(coefs[0] * cur[f] + coefs[1] * total - coefs[2] * advected)
        return new

    def strip_step(tiles):
        new = [[[None, None], [None, None]] for _ in range(fields)]
        for side in range(2):
            for v in range(2):
                cur, dx, sx, dy, sy = [], [], [], [], []
                for f in range(fields):
                    one, two = tiles[f][side]
                    if v == 0:
                        east = jnp.where(lane < cols - group, turn(one, -group), turn(two, -group))
                        west = turn(one, group)
                    else:
                        east = turn(two, -group)
                        west = jnp.where(lane < group, turn(one, group), turn(two, group))
                    here = (one, two)[v]
                    north, south = turn(here, -1), turn(here, 1)
                    cur.append(here)
                    dx.append(east - west)
                    sx.append(east + west)
                    dy.append(north - south)
                    sy.append(north + south)
                result = updated(strip_coefs[side][v], cur, dx, sx, dy, sy)
                for f in range(fields):
                    new[f][side][v] = result[f]
        return new

    for number in range(STEPS):
        source = a_ref if number % 2 == 0 else b_ref
        sink = b_ref if number % 2 == 0 else a_ref
        beyond = [
            [
                jnp.where(lax.rem(lane, group) == wide - 1, a, turn(b, -2))
                for a, b in zip(strips[f][0], strips[f][1])
            ]
            for f in range(fields)
        ]
        bottom, top = number + 1, tall - number - 1
        rows_at = lambda x: [source[x * fields + f] for f in range(fields)]
        before, cur = rows_at(bottom - 1), rows_at(bottom)
        for x in range(bottom, top):
            after = rows_at(x + 1)
            dx, sx, dy, sy = [], [], [], []
            for f in range(fields):
                spot = group * x + wide - 1
                outer = turn(beyond[f][spot // cols], -(spot % cols))
                north = jnp.where(lane == cols - 1, outer, turn(cur[f], -1))
                south = jnp.where(lane == 0, outer, turn(cur[f], 1))
                dx.append(after[f] - before[f])
                sx.append(after[f] + before[f])
                dy.append(north - south)
                sy.append(north + south)
            coefs = [coef_ref[3 * x + k] for k in range(3)]
            new = updated(coefs, cur, dx, sx, dy, sy)
            for f in range(fields):
                if number == STEPS - 1:
                    out_ref[f, pl.ds(x - wide, levels, stride=rows), :] = new[f]
                else:
                    sink[x * fields + f] = new[f]
            before, cur = cur, after
        if number < STEPS - 1:
            strips = strip_step(strips)


def on_device(perturbed_states, control, owner, map_factor, terrain):
    _, fields, levels, rows, cols = perturbed_states.shape
    sizes = tuple(lax.axis_size(axis) for axis in AXES)
    members = sizes[0]
    half = rows // 2
    tile = (levels, cols)

    def tiles(count):
        return jax.ShapeDtypeStruct((count, *tile), jnp.float32)

    flat = (fields, levels * rows, cols)
    states, keep, give, more, metric = pl.pallas_call(
        split_kernel,
        out_shape=(
            tiles(rows * fields),
            tiles(half * fields),
            tiles(half * fields + fields),
            tiles(fields + 1),
            jax.ShapeDtypeStruct((2 * rows, cols), jnp.float32),
        ),
        in_specs=[HBM] * 5,
        out_specs=(VMEM,) * 5,
        scratch_shapes=[
            pltpu.VMEM(flat, jnp.float32),
            pltpu.VMEM(flat, jnp.float32),
            pltpu.SMEM(owner.shape, jnp.int32),
            pltpu.VMEM((rows, cols), jnp.int32),
            pltpu.SemaphoreType.DMA((2 * fields + 3,)),
        ],
        compiler_params=MODEST,
        name="split",
    )(
        *(
            pltpu.with_memory_space_constraint(value, pltpu.HBM)
            for value in (
                perturbed_states.reshape(flat), control.reshape(flat), owner, map_factor, terrain
            )
        )
    )

    given = send(give, lambda k, i, j: (k ^ 1, i, j))
    total = keep + given[: half * fields]
    edges = give[half * fields :] + given[half * fields :]

    chips = [b for b in range(2, members, 2)]
    bit = 2
    got = []
    while bit < members:
        got.append(send(total, lambda k, i, j, bit=bit: (k ^ bit, i, j)))
        total = total + got[-1]
        bit *= 2
    along = sizes[2]

    def from_side(step):
        there = lambda b: lambda k, i, j: (k ^ b, i, (j + step) % along)
        near = send(jnp.concatenate([edges, more], axis=0), there(0))
        return [near] + [send(edges, there(b)) for b in chips]

    left = from_side(1)
    right = from_side(-1) if along > 2 else []

    total, left, right = lax.optimization_barrier((total, left, right))
    other = send(total, lambda k, i, j: (k ^ 1, i, j))
    right = right or left
    count = STEPS * fields + fields + 2
    start, strips, first, second = pl.pallas_call(
        functools.partial(join_kernel, sizes, len(left)),
        out_shape=(tiles(rows * fields), tiles(2 * (fields + 1)), tiles(count), tiles(count)),
        in_specs=[VMEM] * (5 + 2 * len(left)),
        out_specs=(VMEM,) * 4,
        compiler_params=MODEST,
        name="join",
    )(states, total, other, metric, more, *left, *right)
    first = send(first, loop_target(sizes[1], True))
    second = send(second, loop_target(sizes[1], False))
    out = pl.pallas_call(
        functools.partial(forecast_kernel, sizes),
        out_shape=jax.ShapeDtypeStruct(flat, jnp.float32),
        in_specs=[VMEM] * 5,
        out_specs=VMEM,
        scratch_shapes=[
            pltpu.VMEM(((rows + 2 * STEPS) * fields, *tile), jnp.float32),
            pltpu.VMEM(((rows + 2 * STEPS) * fields, *tile), jnp.float32),
            pltpu.VMEM(((rows + 2 * STEPS) * 3, *tile), jnp.float32),
        ],
        compiler_params=MODEST,
        name="forecast",
    )(start, strips, metric, first, second)
    return out.reshape(perturbed_states.shape)


def solution(mesh):
    placed = (
        P("member", None, None, "dx", "dy"),
        P("member", None, None, "dx", "dy"),
        P(),
        P("dx", "dy"),
        P("dx", "dy"),
    )
    return jax.shard_map(
        on_device,
        mesh=mesh,
        in_specs=placed,
        out_specs=P("member", None, None, "dx", "dy"),
        check_vma=False,
    )
```

```python
import functools

import jax
import jax.numpy as jnp
from jax import lax
from jax.experimental import pallas as pl
from jax.experimental.pallas import tpu as pltpu
from jax.sharding import PartitionSpec as P

STEPS = 4

integration_step = 0.2
diffusion = 0.1

OUTSIDE = 1.0e6
AXES = ("member", "dx", "dy")
VMEM = pl.BlockSpec(memory_space=pltpu.VMEM)
HBM = pl.BlockSpec(memory_space=pltpu.HBM)
MODEST = pltpu.CompilerParams(vmem_limit_bytes=8 * 2**20)


def send(value, target):
    sizes = [lax.axis_size(axis) for axis in AXES]
    pairs = []
    for member in range(sizes[0]):
        for i in range(sizes[1]):
            for j in range(sizes[2]):
                k, l, m = target(member, i, j)
                pairs.append(
                    (
                        (member * sizes[1] + i) * sizes[2] + j,
                        (k * sizes[1] + l) * sizes[2] + m,
                    )
                )
    return lax.ppermute(value, AXES, pairs)


def loop_target(rows, forward):
    def target(member, i, j):
        step = 1 if (member % 2 == 0) == forward else -1
        if 0 <= i + step < rows:
            return member, i + step, j
        return member ^ 1, i, j

    return target


def lanes_of(shape):
    return lax.broadcasted_iota(jnp.int32, shape, len(shape) - 1)


def turn(tile, by, axis=1):
    return pltpu.roll(tile, by % tile.shape[axis], axis)


def edges_of(tiles, width):
    lane = lanes_of(tiles[0].shape)
    total = None
    for x, tile in enumerate(tiles):
        moved = turn(tile, 2 * width * x + width)
        total = moved if total is None else jnp.where(lane < 2 * width * x, total, moved)
    return total


def split_kernel(
    p_hbm, c_hbm, owner_hbm, m_hbm, t_hbm,
    pt_ref, keep_ref, send_ref, edge_ref, side_ref, metric_ref,
    p_ref, c_ref, owner_ref, t_ref, sems,
):
    fields, _, cols = p_ref.shape
    rows = t_ref.shape[0]
    levels = p_ref.shape[1] // rows
    half = rows // 2
    member = lax.axis_index("member")
    members = owner_ref.shape[0]
    first = lax.rem(member, 2) == 0
    copies = [pltpu.make_async_copy(owner_hbm, owner_ref, sems.at[0])]
    for f in range(fields):
        copies.append(pltpu.make_async_copy(p_hbm.at[f], p_ref.at[f], sems.at[1 + 2 * f]))
        copies.append(pltpu.make_async_copy(c_hbm.at[f], c_ref.at[f], sems.at[2 + 2 * f]))
    copies.append(
        pltpu.make_async_copy(m_hbm, metric_ref.at[pl.ds(0, rows), :], sems.at[1 + 2 * fields])
    )
    copies.append(pltpu.make_async_copy(t_hbm, t_ref, sems.at[2 + 2 * fields]))
    for copy in copies:
        copy.start()
    copies[0].wait()
    weight = jnp.float32(0.0)
    for rank in range(members):
        per_rank = 2.0 * (members - rank) / (members * (members + 1.0))
        weight = weight + jnp.where(owner_ref[rank] == member, per_rank, 0.0)
    for f in range(fields):
        copies[1 + 2 * f].wait()
        copies[2 + 2 * f].wait()
        states, parts = [], []
        for x in range(rows):
            state = p_ref[f, pl.ds(x, levels, stride=rows), :]
            analysis = c_ref[f, pl.ds(x, levels, stride=rows), :]
            pt_ref[x * fields + f] = state
            states.append(state)
            parts.append(weight * analysis - state * (1.0 / members))
        for r in range(half):
            keep_ref[r * fields + f] = jnp.where(first, parts[r], parts[rows - 1 - r])
            send_ref[r * fields + f] = jnp.where(first, parts[rows - 1 - r], parts[r])
        edge_ref[f] = edges_of(parts, STEPS)
        side_ref[f] = edge_ref[f]
        side_ref[fields + f] = edges_of(states, STEPS)
    copies[-2].wait()
    copies[-1].wait()
    metric_ref[pl.ds(rows, rows), :] = t_ref[...].astype(jnp.float32)
    level = lax.broadcasted_iota(jnp.int32, (levels, cols), 0)
    columns = []
    for x in range(rows):
        scale = jnp.broadcast_to(metric_ref[pl.ds(x, 1), :], (levels, cols))
        ground = jnp.broadcast_to(metric_ref[pl.ds(rows + x, 1), :], (levels, cols))
        columns.append(jnp.where(level == 0, scale, ground))
    side_ref[2 * fields] = edges_of(columns, STEPS)


def has_neighbours(axis, size):
    place = lax.axis_index(axis)
    return place > 0, place < size - 1


def coefficients(level, scale, ground):
    scale = jnp.broadcast_to(scale, level.shape)
    ground = jnp.broadcast_to(ground, level.shape)
    mask = (level.astype(jnp.float32) >= ground).astype(jnp.float32)
    return (
        mask * (1.0 - 6.0 * integration_step * diffusion),
        mask * (integration_step * diffusion),
        mask * (scale * (0.5 * integration_step)),
    )


def updated(level, coefs, cur, dx, sx, dy, sy):
    levels = level.shape[0]
    new = []
    for f, here in enumerate(cur):
        advected = cur[0] * dx[f] + cur[1] * dy[f]
        if f == 0:
            advected = advected + dx[2]
        elif f == 1:
            advected = advected + dy[2]
        elif f == 2:
            advected = advected + (dx[0] + dy[1])
        upper = jnp.where(level < levels - 1, turn(here, -1, 0), 0.0)
        lower = jnp.where(level > 0, turn(here, 1, 0), 0.0)
        total = (sx[f] + sy[f]) + (upper + lower)
        new.append(coefs[0] * here + coefs[1] * total - coefs[2] * advected)
    return new


def row_step(level, lane, coefs, before, cur, after, beyond, spot):
    cols = lane.shape[1]
    dx, sx, dy, sy = [], [], [], []
    for f, here in enumerate(cur):
        outer = turn(beyond[f], -spot)
        north = jnp.where(lane == cols - 1, outer, turn(here, -1))
        south = jnp.where(lane == 0, outer, turn(here, 1))
        dx.append(after[f] - before[f])
        sx.append(after[f] + before[f])
        dy.append(north - south)
        sy.append(north + south)
    return updated(level, coefs, cur, dx, sx, dy, sy)


def strip_step(level, coefs, here, east, west):
    dx, sx, dy, sy = [], [], [], []
    for f, tile in enumerate(here):
        north, south = turn(tile, -1), turn(tile, 1)
        dx.append(east[f] - west[f])
        sx.append(east[f] + west[f])
        dy.append(north - south)
        sy.append(north + south)
    return updated(level, coefs, here, dx, sx, dy, sy)


def outside_columns(lane, width, left, right):
    return [
        jnp.where(lax.rem(lane, 2 * width) == width - 1, a, turn(b, -2))
        for a, b in zip(left, right)
    ]


def join_kernel(
    sizes, n_sides, pt_ref, mine_ref, edge_ref, other_ref, metric_ref, side_ref, *refs
):
    near, (start_ref, beside_ref, first_ref, second_ref) = refs[:n_sides], refs[n_sides:]
    rows, cols = metric_ref.shape[0] // 2, metric_ref.shape[1]
    levels = pt_ref.shape[1]
    fields = pt_ref.shape[0] // rows
    wide = STEPS
    parity = lax.rem(lax.axis_index("member"), 2)
    has_left, has_right = has_neighbours("dy", sizes[2])
    lane = lanes_of((levels, cols))
    early = lax.rem(lane, 2 * wide) < wide
    quarter = 2 * wide * wide

    for r in range(wide):
        for f in range(fields):
            mine, other = mine_ref[r * fields + f], other_ref[r * fields + f]
            low, high = jnp.where(parity == 0, mine, other), jnp.where(parity == 0, other, mine)
            start_ref[r * fields + f] = pt_ref[r * fields + f] + low
            end = 2 * wide - 1 - r
            start_ref[end * fields + f] = pt_ref[(rows - 1 - r) * fields + f] + high

    def ends_of(a, b):
        return jnp.where(
            lane < quarter,
            a,
            jnp.where(
                lane < 2 * quarter,
                turn(b, quarter),
                jnp.where(lane < cols - quarter, turn(b, -quarter), a),
            ),
        )

    ends = []
    far = 0 if n_sides == 1 else 1
    for f in range(fields + 1):
        if f < fields:
            own_rows = {}
            for r in range(wide):
                own_rows[r] = start_ref[r * fields + f]
                own_rows[rows - 1 - r] = start_ref[(2 * wide - 1 - r) * fields + f]
            own = None
            for x in sorted(own_rows):
                moved = turn(own_rows[x], 2 * wide * x + wide)
                own = moved if own is None else jnp.where(lane < 2 * wide * x, own, moved)
            sums = []
            for side in (0, far):
                k = side * fields + f
                total = edge_ref[k] + other_ref[wide * fields + k]
                sums.append(near[side][fields + f] + total)
            before = jnp.where(has_left, sums[0], 0.0)
            after = jnp.where(has_right, sums[1], 0.0)
        else:
            own = side_ref[2 * fields]
            before = jnp.where(has_left, near[0][2 * fields], OUTSIDE)
            after = jnp.where(has_right, near[far][2 * fields], OUTSIDE)
        beside_ref[f] = before
        beside_ref[fields + 1 + f] = after
        ends.append(ends_of(jnp.where(early, before, own), jnp.where(early, own, after)))
    scale, ground = metric_ref[pl.ds(0, rows), :], metric_ref[pl.ds(rows, rows), :]
    tops = jnp.concatenate([scale[rows - wide :], ground[rows - wide :]], axis=0)
    bottoms = jnp.concatenate([scale[:wide], ground[:wide]], axis=0)
    for message, up in ((first_ref, parity == 0), (second_ref, parity == 1)):
        base = jnp.where(up, wide, 0) * fields
        for k in range(wide * fields):
            message[k] = start_ref[base + k]
        for k, end in enumerate(ends):
            message[wide * fields + k] = end
        message[wide * fields + fields + 1] = jnp.where(up, tops, bottoms)


def middle_kernel(
    pt_ref, outer_ref, mine_ref, other_ref, metric_ref, side_ref, beside_ref,
    strip_ref, saved_ref, done_ref, a_ref, b_ref,
):
    rows, cols = metric_ref.shape[0] // 2, metric_ref.shape[1]
    levels = pt_ref.shape[1]
    fields = pt_ref.shape[0] // rows
    wide = STEPS
    group = 2 * wide
    half = rows // 2
    parity = lax.rem(lax.axis_index("member"), 2)
    lane = lanes_of((levels, cols))
    level = lax.broadcasted_iota(jnp.int32, (levels, cols), 0)
    early = lax.rem(lane, group) < wide
    for r in range(wide):
        for f in range(fields):
            a_ref[r * fields + f] = outer_ref[r * fields + f]
            a_ref[(rows - 1 - r) * fields + f] = outer_ref[(group - 1 - r) * fields + f]
    for r in range(wide, half):
        for f in range(fields):
            k = (r - wide) * fields + f
            mine, other = mine_ref[k], other_ref[k]
            low, high = jnp.where(parity == 0, mine, other), jnp.where(parity == 0, other, mine)
            a_ref[r * fields + f] = pt_ref[r * fields + f] + low
            mirrored = (rows - 1 - r) * fields + f
            a_ref[mirrored] = pt_ref[mirrored] + high
    left, right = [], []
    for f in range(fields + 1):
        if f < fields:
            own = edges_of([a_ref[x * fields + f] for x in range(rows)], wide)
        else:
            own = side_ref[2 * fields]
        left.append(jnp.where(early, beside_ref[f], own))
        right.append(jnp.where(early, own, beside_ref[fields + 1 + f]))
        strip_ref[f] = left[f]
        strip_ref[fields + 1 + f] = right[f]
    strip_coefs = [coefficients(level, side[fields][0:1], side[fields][1:2]) for side in (left, right)]
    left, right = left[:fields], right[:fields]
    coefs = [
        coefficients(level, metric_ref[pl.ds(x, 1), :], metric_ref[pl.ds(rows + x, 1), :])
        for x in range(rows)
    ]
    for number in range(STEPS):
        source, sink = (a_ref, b_ref) if number % 2 == 0 else (b_ref, a_ref)
        beyond = outside_columns(lane, wide, left, right)
        bottom, top = number + 1, rows - 1 - number
        row = lambda x: [source[x * fields + f] for f in range(fields)]
        before, cur = row(bottom - 1), row(bottom)
        for x in range(bottom, top):
            after = row(x + 1)
            new = row_step(
                level, lane, coefs[x], before, cur, after, beyond, group * x + wide - 1
            )
            edge = {bottom: 0, bottom + 1: 1, top - 2: 2, top - 1: 3}.get(x)
            for f in range(fields):
                if number == STEPS - 1:
                    done_ref[(x - wide) * fields + f] = new[f]
                else:
                    sink[x * fields + f] = new[f]
                    if edge is not None:
                        saved_ref[(4 * number + edge) * fields + f] = new[f]
            before, cur = cur, after
        if number < STEPS - 1:
            left, right = [
                strip_step(
                    level,
                    strip_coefs[side],
                    tiles,
                    [turn(tile, -group) for tile in tiles],
                    [turn(tile, group) for tile in tiles],
                )
                for side, tiles in enumerate((left, right))
            ]


def outer_kernel(
    sizes, outer_ref, strip_ref, saved_ref, done_ref, metric_ref, first_ref, second_ref,
    out_hbm, out_ref, sems,
):
    rows, cols = metric_ref.shape[0] // 2, metric_ref.shape[1]
    levels = outer_ref.shape[1]
    wide = STEPS
    group = 2 * wide
    fields = outer_ref.shape[0] // group
    half = rows // 2
    even = lax.rem(lax.axis_index("member"), 2) == 0
    has_low, has_high = has_neighbours("dx", sizes[1])
    lane = lanes_of((levels, cols))
    level = lax.broadcasted_iota(jnp.int32, (levels, cols), 0)
    quarter = group * wide

    def low(k, empty=0.0):
        return jnp.where(has_low, jnp.where(even, first_ref[k], second_ref[k]), empty)

    def high(k, empty=0.0):
        return jnp.where(has_high, jnp.where(even, second_ref[k], first_ref[k]), empty)

    def stretched(k, empty):
        mine_a = turn(strip_ref[k], quarter)
        mine_b = turn(strip_ref[fields + 1 + k], quarter)
        under, over = low(wide * fields + k, empty), high(wide * fields + k, empty)

        def end(own, other):
            return jnp.where(lane < quarter, own, jnp.where(lane < 2 * quarter, other, empty))

        return (
            (
                jnp.where(lane < quarter, turn(under, quarter), mine_a),
                end(mine_a, turn(over, quarter)),
            ),
            (
                jnp.where(lane < quarter, turn(under, 2 * quarter), mine_b),
                end(mine_b, over),
            ),
        )

    by_field = [stretched(f, 0.0) for f in range(fields)]
    strips = [[[by_field[f][side][v] for f in range(fields)] for v in range(2)] for side in range(2)]
    strip_coefs = [
        [coefficients(level, tile[0:1], tile[1:2]) for tile in side]
        for side in stretched(fields, OUTSIDE)
    ]
    beyond = []
    for number in range(STEPS):
        beyond.append(
            [outside_columns(lane, wide, strips[0][v], strips[1][v]) for v in range(2)]
        )
        if number == STEPS - 1:
            break
        new = []
        for side, (one, two) in enumerate(strips):
            ahead = [
                [jnp.where(lane < cols - group, turn(p, -group), turn(q, -group)) for p, q in zip(one, two)],
                [turn(q, -group) for q in two],
            ]
            behind = [
                [turn(p, group) for p in one],
                [jnp.where(lane < group, turn(p, group), turn(q, group)) for p, q in zip(one, two)],
            ]
            new.append(
                [
                    strip_step(level, strip_coefs[side][v], (one, two)[v], ahead[v], behind[v])
                    for v in range(2)
                ]
            )
        strips = new

    for x in range(wide, rows - wide):
        for f in range(fields):
            out_ref[f, pl.ds(x, levels, stride=rows), :] = done_ref[(x - wide) * fields + f]

    def saved(number, edge):
        return [saved_ref[(4 * (number - 1) + edge) * fields + f] for f in range(fields)]

    def finish(is_low):
        metric = wide * fields + fields + 1
        halo = low(metric, OUTSIDE) if is_low else high(metric, OUTSIDE)
        coefs, state = {}, {}
        for r in range(wide):
            message = [(low if is_low else high)(r * fields + f) for f in range(fields)]
            state[r - wide if is_low else rows + r] = message
            coefs[r - wide if is_low else rows + r] = coefficients(
                level, halo[r : r + 1], halo[wide + r : wide + r + 1]
            )
            x = r if is_low else rows - wide + r
            k = r if is_low else wide + r
            state[x] = [outer_ref[k * fields + f] for f in range(fields)]
            coefs[x] = coefficients(
                level, metric_ref[pl.ds(x, 1), :], metric_ref[pl.ds(rows + x, 1), :]
            )
        for number in range(STEPS):
            if number > 0:
                if is_low:
                    state[number], state[number + 1] = saved(number, 0), saved(number, 1)
                else:
                    state[rows - 2 - number], state[rows - 1 - number] = saved(number, 2), saved(number, 3)
            bottom = number + 1 - wide if is_low else rows - 1 - number
            new = {}
            for x in range(bottom, bottom + wide):
                spot = group * (x + wide) + wide - 1
                outside = beyond[number][spot // cols]
                new[x] = row_step(
                    level, lane, coefs[x], state[x - 1], state[x], state[x + 1], outside, spot % cols
                )
            state = new
        for x, tiles in state.items():
            for f in range(fields):
                out_ref[f, pl.ds(x, levels, stride=rows), :] = tiles[f]

    copies = []
    for n, is_low in enumerate((True, False)):
        finish(is_low)
        part = pl.ds(n * half, half)
        source = out_ref.reshape(fields * levels, rows, cols)
        copies.append(
            pltpu.make_async_copy(source.at[:, part, :], out_hbm.at[:, part, :], sems.at[n])
        )
        copies[-1].start()
    for copy in copies:
        copy.wait()


def on_device(perturbed_states, control, owner, map_factor, terrain):
    _, fields, levels, rows, cols = perturbed_states.shape
    sizes = tuple(lax.axis_size(axis) for axis in AXES)
    members, along = sizes[0], sizes[2]
    half = rows // 2
    tile = (levels, cols)

    def tiles(count):
        return jax.ShapeDtypeStruct((count, *tile), jnp.float32)

    def room(count):
        return pltpu.VMEM((count, *tile), jnp.float32)

    flat = (fields, levels * rows, cols)
    states, keep, give, edge, side, metric = pl.pallas_call(
        split_kernel,
        out_shape=(
            tiles(rows * fields),
            tiles(half * fields),
            tiles(half * fields),
            tiles(fields),
            tiles(2 * fields + 1),
            jax.ShapeDtypeStruct((2 * rows, cols), jnp.float32),
        ),
        in_specs=[HBM] * 5,
        out_specs=(VMEM,) * 6,
        scratch_shapes=[
            pltpu.VMEM(flat, jnp.float32),
            pltpu.VMEM(flat, jnp.float32),
            pltpu.SMEM(owner.shape, jnp.int32),
            pltpu.VMEM((rows, cols), jnp.int32),
            pltpu.SemaphoreType.DMA((2 * fields + 3,)),
        ],
        compiler_params=MODEST,
        name="split",
    )(
        *(
            pltpu.with_memory_space_constraint(value, pltpu.HBM)
            for value in (
                perturbed_states.reshape(flat), control.reshape(flat), owner, map_factor, terrain
            )
        )
    )

    def over_members(value, bit):
        return send(value, lambda k, i, j: (k ^ bit, i, j))

    def over_chips(value):
        bit = 2
        while bit < members:
            value = value + over_members(value, bit)
            bit *= 2
        return value

    given = over_members(give, 1)
    def from_beside(value, step, bit):
        return send(value, lambda k, i, j: (k ^ bit, i, (j + step) % along))

    steps = (1, -1) if along > 2 else (1,)
    near = [from_beside(side, step, 0) for step in steps]
    edges = []
    for step, n in zip(steps, near):
        total = n[:fields]
        for bit in range(2, members, 2):
            total = total + from_beside(edge, step, bit)
        edges.append(total)
    edges = jnp.concatenate(edges, axis=0)
    cut = STEPS * fields
    outer = over_chips(keep[:cut] + given[:cut])
    inner = over_chips(keep[cut:] + given[cut:])

    other = over_members(jnp.concatenate([outer, edges], axis=0), 1)
    count = cut + fields + 2
    start, beside, first, second = pl.pallas_call(
        functools.partial(join_kernel, sizes, len(near)),
        out_shape=(tiles(2 * cut), tiles(2 * (fields + 1)), tiles(count), tiles(count)),
        in_specs=[VMEM] * (6 + len(near)),
        out_specs=(VMEM,) * 4,
        compiler_params=MODEST,
        name="join",
    )(states, outer, edges, other, metric, side, *near)
    first_in = send(first, loop_target(sizes[1], True))
    second_in = send(second, loop_target(sizes[1], False))
    inner, _ = lax.optimization_barrier((inner, first))
    other = over_members(inner, 1)
    strips, saved, done = pl.pallas_call(
        middle_kernel,
        out_shape=(
            tiles(2 * (fields + 1)),
            tiles(4 * (STEPS - 1) * fields),
            tiles((rows - 2 * STEPS) * fields),
        ),
        in_specs=[VMEM] * 7,
        out_specs=(VMEM,) * 3,
        scratch_shapes=[room(rows * fields), room(rows * fields)],
        compiler_params=MODEST,
        cost_estimate=pl.CostEstimate(
            flops=30 * rows * fields * levels * cols * STEPS, bytes_accessed=2**20, transcendentals=0
        ),
        name="middle",
    )(states, start, inner, other, metric, side, beside)
    out = pl.pallas_call(
        functools.partial(outer_kernel, sizes),
        out_shape=jax.ShapeDtypeStruct((fields * levels, rows, cols), jnp.float32),
        in_specs=[VMEM] * 7,
        out_specs=HBM,
        scratch_shapes=[pltpu.VMEM(flat, jnp.float32), pltpu.SemaphoreType.DMA((2,))],
        compiler_params=MODEST,
        name="outer",
    )(start, strips, saved, done, metric, first_in, second_in)
    return out.reshape(perturbed_states.shape)


def solution(mesh):
    placed = (
        P("member", None, None, "dx", "dy"),
        P("member", None, None, "dx", "dy"),
        P(),
        P("dx", "dy"),
        P("dx", "dy"),
    )
    return jax.shard_map(
        on_device,
        mesh=mesh,
        in_specs=placed,
        out_specs=P("member", None, None, "dx", "dy"),
        check_vma=False,
    )
```

```python
import functools

import jax
import jax.numpy as jnp
from jax import lax
from jax.experimental import pallas as pl
from jax.experimental.pallas import tpu as pltpu
from jax.sharding import PartitionSpec as P

STEPS = 4

integration_step = 0.2
diffusion = 0.1

OUTSIDE = 1.0e6
AXES = ("member", "dx", "dy")
VMEM = pl.BlockSpec(memory_space=pltpu.VMEM)
HBM = pl.BlockSpec(memory_space=pltpu.HBM)
MODEST = pltpu.CompilerParams(vmem_limit_bytes=8 * 2**20)


def send(value, target):
    sizes = [lax.axis_size(axis) for axis in AXES]
    pairs = []
    for member in range(sizes[0]):
        for i in range(sizes[1]):
            for j in range(sizes[2]):
                k, l, m = target(member, i, j)
                pairs.append(
                    (
                        (member * sizes[1] + i) * sizes[2] + j,
                        (k * sizes[1] + l) * sizes[2] + m,
                    )
                )
    return lax.ppermute(value, AXES, pairs)


def loop_target(rows, forward):
    def target(member, i, j):
        step = 1 if (member % 2 == 0) == forward else -1
        if 0 <= i + step < rows:
            return member, i + step, j
        return member ^ 1, i, j

    return target


def lanes_of(shape):
    return lax.broadcasted_iota(jnp.int32, shape, len(shape) - 1)


def turn(tile, by, axis=1):
    size = tile.shape[axis]
    return pltpu.roll(tile, by % size if isinstance(by, int) else lax.rem(by, size), axis)


def edges_of(tiles, width):
    lane = lanes_of(tiles[0].shape)
    total = None
    for x, tile in enumerate(tiles):
        moved = turn(tile, 2 * width * x + width)
        total = moved if total is None else jnp.where(lane < 2 * width * x, total, moved)
    return total


def split_kernel(
    p_hbm, c_hbm, owner_hbm, m_hbm, t_hbm,
    pt_ref, keep_ref, send_ref, edge_ref, side_ref, metric_ref,
    p_ref, c_ref, owner_ref, t_ref, sems,
):
    fields, _, cols = p_ref.shape
    rows = t_ref.shape[0]
    levels = p_ref.shape[1] // rows
    half = rows // 2
    member = lax.axis_index("member")
    members = owner_ref.shape[0]
    first = lax.rem(member, 2) == 0
    copies = [
        pltpu.make_async_copy(owner_hbm, owner_ref, sems.at[0]),
        pltpu.make_async_copy(m_hbm, metric_ref.at[pl.ds(0, rows), :], sems.at[1]),
        pltpu.make_async_copy(t_hbm, t_ref, sems.at[2]),
    ]
    for f in range(fields):
        copies.append(pltpu.make_async_copy(p_hbm.at[f], p_ref.at[f], sems.at[3 + 2 * f]))
        copies.append(pltpu.make_async_copy(c_hbm.at[f], c_ref.at[f], sems.at[4 + 2 * f]))
    for copy in copies:
        copy.start()
    for copy in copies[:3]:
        copy.wait()
    metric_ref[pl.ds(rows, rows), :] = t_ref[...].astype(jnp.float32)
    level = lax.broadcasted_iota(jnp.int32, (levels, cols), 0)
    columns = []
    for x in range(rows):
        scale = jnp.broadcast_to(metric_ref[pl.ds(x, 1), :], (levels, cols))
        ground = jnp.broadcast_to(metric_ref[pl.ds(rows + x, 1), :], (levels, cols))
        columns.append(jnp.where(level == 0, scale, ground))
    side_ref[2 * fields] = edges_of(columns, STEPS)
    weight = jnp.float32(0.0)
    for rank in range(members):
        per_rank = 2.0 * (members - rank) / (members * (members + 1.0))
        weight = weight + jnp.where(owner_ref[rank] == member, per_rank, 0.0)
    for f in range(fields):
        copies[3 + 2 * f].wait()
        copies[4 + 2 * f].wait()
        states, parts = [], []
        for x in range(rows):
            state = p_ref[f, pl.ds(x, levels, stride=rows), :]
            analysis = c_ref[f, pl.ds(x, levels, stride=rows), :]
            pt_ref[x * fields + f] = state
            states.append(state)
            parts.append(weight * analysis - state * (1.0 / members))
        for r in range(half):
            keep_ref[r * fields + f] = jnp.where(first, parts[r], parts[rows - 1 - r])
            send_ref[r * fields + f] = jnp.where(first, parts[rows - 1 - r], parts[r])
        edge_ref[f] = edges_of(parts, STEPS)
        side_ref[f] = edge_ref[f]
        side_ref[fields + f] = edges_of(states, STEPS)


def has_neighbours(axis, size):
    place = lax.axis_index(axis)
    return place > 0, place < size - 1


def coefficients(level, scale, ground):
    scale = jnp.broadcast_to(scale, level.shape)
    ground = jnp.broadcast_to(ground, level.shape)
    mask = (level.astype(jnp.float32) >= ground).astype(jnp.float32)
    return (
        mask * (1.0 - 6.0 * integration_step * diffusion),
        mask * (integration_step * diffusion),
        mask * (scale * (0.5 * integration_step)),
    )


def updated(level, coefs, cur, dx, sx, dy, sy):
    levels = level.shape[0]
    new = []
    for f, here in enumerate(cur):
        advected = cur[0] * dx[f] + cur[1] * dy[f]
        if f == 0:
            advected = advected + dx[2]
        elif f == 1:
            advected = advected + dy[2]
        elif f == 2:
            advected = advected + (dx[0] + dy[1])
        upper = jnp.where(level < levels - 1, turn(here, -1, 0), 0.0)
        lower = jnp.where(level > 0, turn(here, 1, 0), 0.0)
        total = (sx[f] + sy[f]) + (upper + lower)
        new.append(coefs[0] * here + coefs[1] * total - coefs[2] * advected)
    return new


def row_step(level, lane, coefs, before, cur, after, beyond, spot):
    cols = lane.shape[1]
    dx, sx, dy, sy = [], [], [], []
    for f, here in enumerate(cur):
        outer = turn(beyond[f], -spot)
        north = jnp.where(lane == cols - 1, outer, turn(here, -1))
        south = jnp.where(lane == 0, outer, turn(here, 1))
        dx.append(after[f] - before[f])
        sx.append(after[f] + before[f])
        dy.append(north - south)
        sy.append(north + south)
    return updated(level, coefs, cur, dx, sx, dy, sy)


def strip_step(level, coefs, here, group):
    dx, sx, dy, sy = [], [], [], []
    for tile in here:
        east, west = turn(tile, -group), turn(tile, group)
        north, south = turn(tile, -1), turn(tile, 1)
        dx.append(east - west)
        sx.append(east + west)
        dy.append(north - south)
        sy.append(north + south)
    return updated(level, coefs, here, dx, sx, dy, sy)


def outside_columns(lane, width, strips, has_left):
    place = lax.rem(lane, 2 * width)
    if len(strips) == 2:
        return [jnp.where(place == width - 1, a, turn(b, -2)) for a, b in zip(*strips)]
    before = jnp.logical_and(place == width - 1, has_left)
    after = jnp.logical_and(place == width - 2, jnp.logical_not(has_left))
    return [jnp.where(before, a, jnp.where(after, turn(a, -2), 0.0)) for a in strips[0]]


def strips_of(early, own, beside, has_left):
    if len(beside) == 2:
        return [jnp.where(early, beside[0], own), jnp.where(early, own, beside[1])]
    return [jnp.where(early == has_left, beside[0], own)]


def join_kernel(
    sizes, n_sides, pt_ref, mine_ref, edge_ref, other_ref, metric_ref, side_ref, *refs
):
    near, (start_ref, beside_ref, first_ref, second_ref) = refs[:n_sides], refs[n_sides:]
    rows, cols = metric_ref.shape[0] // 2, metric_ref.shape[1]
    levels = pt_ref.shape[1]
    fields = pt_ref.shape[0] // rows
    wide = STEPS
    parity = lax.rem(lax.axis_index("member"), 2)
    has_left, has_right = has_neighbours("dy", sizes[2])
    lane = lanes_of((levels, cols))
    early = lax.rem(lane, 2 * wide) < wide
    quarter = 2 * wide * wide
    sides = beside_ref.shape[0] // (fields + 1)

    for r in range(wide):
        for f in range(fields):
            mine, other = mine_ref[r * fields + f], other_ref[r * fields + f]
            low, high = jnp.where(parity == 0, mine, other), jnp.where(parity == 0, other, mine)
            start_ref[r * fields + f] = pt_ref[r * fields + f] + low
            end = 2 * wide - 1 - r
            start_ref[end * fields + f] = pt_ref[(rows - 1 - r) * fields + f] + high

    def ends_of(strips, up):
        if sides == 1:
            packed = None
            for f in range(fields):
                moved = turn(strips[f][0], jnp.where(up, quarter, 0) + f * quarter)
                packed = moved if f == 0 else jnp.where(lane < f * quarter, packed, moved)
            return [packed, strips[fields][0]]
        return [
            jnp.where(
                lane < quarter,
                a,
                jnp.where(
                    lane < 2 * quarter,
                    turn(b, quarter),
                    jnp.where(lane < cols - quarter, turn(b, -quarter), a),
                ),
            )
            for a, b in strips
        ]

    strips = []
    for f in range(fields + 1):
        beside = []
        for side in range(sides):
            if f < fields:
                k = side * fields + f
                value = near[side][fields + f] + (edge_ref[k] + other_ref[wide * fields + k])
            else:
                value = near[side][2 * fields]
            if sides == 2:
                value = jnp.where((has_left, has_right)[side], value, 0.0 if f < fields else OUTSIDE)
            beside.append(value)
            beside_ref[side * (fields + 1) + f] = value
        if f < fields:
            own = None
            for k in range(2 * wide):
                x = k if k < wide else rows - 2 * wide + k
                moved = turn(start_ref[k * fields + f], 2 * wide * x + wide)
                own = moved if own is None else jnp.where(lane < 2 * wide * x, own, moved)
        else:
            own = side_ref[2 * fields]
        strips.append(strips_of(early, own, beside, has_left))
    scale, ground = metric_ref[pl.ds(0, rows), :], metric_ref[pl.ds(rows, rows), :]
    tops = jnp.concatenate([scale[rows - wide :], ground[rows - wide :]], axis=0)
    bottoms = jnp.concatenate([scale[:wide], ground[:wide]], axis=0)
    for message, up in ((first_ref, parity == 0), (second_ref, parity == 1)):
        base = jnp.where(up, wide, 0) * fields
        for k in range(wide * fields):
            message[k] = start_ref[base + k]
        message[wide * fields] = jnp.where(up, tops, bottoms)
        for k, end in enumerate(ends_of(strips, up)):
            message[wide * fields + 1 + k] = end


def middle_kernel(
    sizes, pt_ref, outer_ref, mine_ref, other_ref, metric_ref, side_ref, beside_ref,
    strip_ref, saved_ref, done_ref, a_ref, b_ref,
):
    rows, cols = metric_ref.shape[0] // 2, metric_ref.shape[1]
    levels = pt_ref.shape[1]
    fields = pt_ref.shape[0] // rows
    wide = STEPS
    group = 2 * wide
    half = rows // 2
    parity = lax.rem(lax.axis_index("member"), 2)
    lane = lanes_of((levels, cols))
    level = lax.broadcasted_iota(jnp.int32, (levels, cols), 0)
    early = lax.rem(lane, group) < wide
    for r in range(wide):
        for f in range(fields):
            a_ref[r * fields + f] = outer_ref[r * fields + f]
            a_ref[(rows - 1 - r) * fields + f] = outer_ref[(group - 1 - r) * fields + f]
    for r in range(wide, half):
        for f in range(fields):
            k = (r - wide) * fields + f
            mine, other = mine_ref[k], other_ref[k]
            low, high = jnp.where(parity == 0, mine, other), jnp.where(parity == 0, other, mine)
            a_ref[r * fields + f] = pt_ref[r * fields + f] + low
            mirrored = (rows - 1 - r) * fields + f
            a_ref[mirrored] = pt_ref[mirrored] + high
    has_left, _ = has_neighbours("dy", sizes[2])
    sides = beside_ref.shape[0] // (fields + 1)
    strips = [[] for _ in range(sides)]
    for f in range(fields + 1):
        if f < fields:
            own = edges_of([a_ref[x * fields + f] for x in range(rows)], wide)
        else:
            own = side_ref[2 * fields]
        beside = [beside_ref[side * (fields + 1) + f] for side in range(sides)]
        for side, strip in enumerate(strips_of(early, own, beside, has_left)):
            strips[side].append(strip)
            strip_ref[side * (fields + 1) + f] = strip
    strip_coefs = [coefficients(level, side[fields][0:1], side[fields][1:2]) for side in strips]
    strips = [side[:fields] for side in strips]
    coefs = [
        coefficients(level, metric_ref[pl.ds(x, 1), :], metric_ref[pl.ds(rows + x, 1), :])
        for x in range(rows)
    ]
    for number in range(STEPS):
        source, sink = (a_ref, b_ref) if number % 2 == 0 else (b_ref, a_ref)
        beyond = outside_columns(lane, wide, strips, has_left)
        bottom, top = number + 1, rows - 1 - number
        row = lambda x: [source[x * fields + f] for f in range(fields)]
        before, cur = row(bottom - 1), row(bottom)
        for x in range(bottom, top):
            after = row(x + 1)
            new = row_step(
                level, lane, coefs[x], before, cur, after, beyond, group * x + wide - 1
            )
            edge = {bottom: 0, bottom + 1: 1, top - 2: 2, top - 1: 3}.get(x)
            for f in range(fields):
                if number == STEPS - 1:
                    done_ref[(x - wide) * fields + f] = new[f]
                else:
                    sink[x * fields + f] = new[f]
                    if edge is not None:
                        saved_ref[(4 * number + edge) * fields + f] = new[f]
            before, cur = cur, after
        if number < STEPS - 1:
            strips = [
                strip_step(level, coef, tiles, group) for coef, tiles in zip(strip_coefs, strips)
            ]


def outer_kernel(
    sizes, outer_ref, strip_ref, saved_ref, done_ref, metric_ref, first_ref, second_ref,
    out_hbm, out_ref, sems,
):
    rows, cols = metric_ref.shape[0] // 2, metric_ref.shape[1]
    levels = outer_ref.shape[1]
    wide = STEPS
    group = 2 * wide
    fields = outer_ref.shape[0] // group
    half = rows // 2
    even = lax.rem(lax.axis_index("member"), 2) == 0
    has_low, has_high = has_neighbours("dx", sizes[1])
    lane = lanes_of((levels, cols))
    level = lax.broadcasted_iota(jnp.int32, (levels, cols), 0)
    quarter = group * wide

    def low(k, empty=0.0):
        return jnp.where(has_low, jnp.where(even, first_ref[k], second_ref[k]), empty)

    def high(k, empty=0.0):
        return jnp.where(has_high, jnp.where(even, second_ref[k], first_ref[k]), empty)

    has_left, _ = has_neighbours("dy", sizes[2])
    sides = strip_ref.shape[0] // (fields + 1)

    def stretched(is_low, side, f):
        mine = strip_ref[side * (fields + 1) + f]
        empty = 0.0 if f < fields else OUTSIDE
        if sides == 1 and f < fields:
            k, by = 0, (-f if is_low else -1 - f)
        else:
            k, by = min(f, 1) if sides == 1 else f, ((1, 2) if is_low else (-1, 2))[side]
        theirs = turn((low if is_low else high)(wide * fields + 1 + k, empty), by * quarter)
        if is_low:
            return jnp.where(lane < quarter, theirs, turn(mine, quarter))
        return jnp.where(lane < cols - quarter, turn(mine, -quarter), theirs)

    beyond = {}
    for is_low in (True, False):
        strips = [[stretched(is_low, side, f) for f in range(fields + 1)] for side in range(sides)]
        coefs = [coefficients(level, side[fields][0:1], side[fields][1:2]) for side in strips]
        strips = [side[:fields] for side in strips]
        for number in range(STEPS):
            beyond[is_low, number] = outside_columns(lane, wide, strips, has_left)
            if number < STEPS - 1:
                strips = [strip_step(level, c, tiles, group) for c, tiles in zip(coefs, strips)]

    for x in range(wide, rows - wide):
        for f in range(fields):
            out_ref[f, pl.ds(x, levels, stride=rows), :] = done_ref[(x - wide) * fields + f]

    def saved(number, edge):
        return [saved_ref[(4 * (number - 1) + edge) * fields + f] for f in range(fields)]

    def finish(is_low):
        metric = wide * fields
        halo = low(metric, OUTSIDE) if is_low else high(metric, OUTSIDE)
        coefs, state = {}, {}
        for r in range(wide):
            message = [(low if is_low else high)(r * fields + f) for f in range(fields)]
            state[r - wide if is_low else rows + r] = message
            coefs[r - wide if is_low else rows + r] = coefficients(
                level, halo[r : r + 1], halo[wide + r : wide + r + 1]
            )
            x = r if is_low else rows - wide + r
            k = r if is_low else wide + r
            state[x] = [outer_ref[k * fields + f] for f in range(fields)]
            coefs[x] = coefficients(
                level, metric_ref[pl.ds(x, 1), :], metric_ref[pl.ds(rows + x, 1), :]
            )
        for number in range(STEPS):
            if number > 0:
                if is_low:
                    state[number], state[number + 1] = saved(number, 0), saved(number, 1)
                else:
                    state[rows - 2 - number], state[rows - 1 - number] = saved(number, 2), saved(number, 3)
            bottom = number + 1 - wide if is_low else rows - 1 - number
            new = {}
            for x in range(bottom, bottom + wide):
                spot = group * (x + (wide if is_low else -wide)) + wide - 1
                new[x] = row_step(
                    level, lane, coefs[x], state[x - 1], state[x], state[x + 1],
                    beyond[is_low, number], spot,
                )
            state = new
        for x, tiles in state.items():
            for f in range(fields):
                out_ref[f, pl.ds(x, levels, stride=rows), :] = tiles[f]

    copies = []
    for n, is_low in enumerate((True, False)):
        finish(is_low)
        part = pl.ds(n * half, half)
        source = out_ref.reshape(fields * levels, rows, cols)
        copies.append(
            pltpu.make_async_copy(source.at[:, part, :], out_hbm.at[:, part, :], sems.at[n])
        )
        copies[-1].start()
    for copy in copies:
        copy.wait()


def on_device(perturbed_states, control, owner, map_factor, terrain):
    _, fields, levels, rows, cols = perturbed_states.shape
    sizes = tuple(lax.axis_size(axis) for axis in AXES)
    members, along = sizes[0], sizes[2]
    half = rows // 2
    tile = (levels, cols)

    def tiles(count):
        return jax.ShapeDtypeStruct((count, *tile), jnp.float32)

    def room(count):
        return pltpu.VMEM((count, *tile), jnp.float32)

    flat = (fields, levels * rows, cols)
    states, keep, give, edge, side, metric = pl.pallas_call(
        split_kernel,
        out_shape=(
            tiles(rows * fields),
            tiles(half * fields),
            tiles(half * fields),
            tiles(fields),
            tiles(2 * fields + 1),
            jax.ShapeDtypeStruct((2 * rows, cols), jnp.float32),
        ),
        in_specs=[HBM] * 5,
        out_specs=(VMEM,) * 6,
        scratch_shapes=[
            pltpu.VMEM(flat, jnp.float32),
            pltpu.VMEM(flat, jnp.float32),
            pltpu.SMEM(owner.shape, jnp.int32),
            pltpu.VMEM((rows, cols), jnp.int32),
            pltpu.SemaphoreType.DMA((2 * fields + 3,)),
        ],
        compiler_params=MODEST,
        name="split",
    )(
        *(
            pltpu.with_memory_space_constraint(value, pltpu.HBM)
            for value in (
                perturbed_states.reshape(flat), control.reshape(flat), owner, map_factor, terrain
            )
        )
    )

    def over_members(value, bit):
        return send(value, lambda k, i, j: (k ^ bit, i, j))

    def over_chips(value):
        bit = 2
        while bit < members:
            value = value + over_members(value, bit)
            bit *= 2
        return value

    given = over_members(give, 1)
    def from_beside(value, step, bit):
        return send(value, lambda k, i, j: (k ^ bit, i, (j + step) % along))

    steps = (1, -1) if along > 2 else (1,)
    near = [from_beside(side, step, 0) for step in steps]
    edges = []
    for step, n in zip(steps, near):
        total = n[:fields]
        for bit in range(2, members, 2):
            total = total + from_beside(edge, step, bit)
        edges.append(total)
    edges = jnp.concatenate(edges, axis=0)
    cut = STEPS * fields
    outer = over_chips(keep[:cut] + given[:cut])
    inner = over_chips(keep + given)[cut:]

    other = over_members(jnp.concatenate([outer, edges], axis=0), 1)
    count = cut + (3 if along == 2 else fields + 2)
    start, beside, first, second = pl.pallas_call(
        functools.partial(join_kernel, sizes, len(near)),
        out_shape=(tiles(2 * cut), tiles(len(near) * (fields + 1)), tiles(count), tiles(count)),
        in_specs=[VMEM] * (6 + len(near)),
        out_specs=(VMEM,) * 4,
        compiler_params=MODEST,
        name="join",
    )(states, outer, edges, other, metric, side, *near)
    first_in = send(first, loop_target(sizes[1], True))
    second_in = send(second, loop_target(sizes[1], False))
    inner, _ = lax.optimization_barrier((inner, first))
    other = over_members(inner, 1)
    strips, saved, done = pl.pallas_call(
        functools.partial(middle_kernel, sizes),
        out_shape=(
            tiles(len(near) * (fields + 1)),
            tiles(4 * (STEPS - 1) * fields),
            tiles((rows - 2 * STEPS) * fields),
        ),
        in_specs=[VMEM] * 7,
        out_specs=(VMEM,) * 3,
        scratch_shapes=[room(rows * fields), room(rows * fields)],
        compiler_params=MODEST,
        cost_estimate=pl.CostEstimate(
            flops=30 * rows * fields * levels * cols * STEPS, bytes_accessed=2**20, transcendentals=0
        ),
        name="middle",
    )(states, start, inner, other, metric, side, beside)
    out = pl.pallas_call(
        functools.partial(outer_kernel, sizes),
        out_shape=jax.ShapeDtypeStruct((fields * levels, rows, cols), jnp.float32),
        in_specs=[VMEM] * 7,
        out_specs=HBM,
        scratch_shapes=[pltpu.VMEM(flat, jnp.float32), pltpu.SemaphoreType.DMA((2,))],
        compiler_params=MODEST,
        name="outer",
    )(start, strips, saved, done, metric, first_in, second_in)
    return out.reshape(perturbed_states.shape)


def solution(mesh):
    placed = (
        P("member", None, None, "dx", "dy"),
        P("member", None, None, "dx", "dy"),
        P(),
        P("dx", "dy"),
        P("dx", "dy"),
    )
    return jax.shard_map(
        on_device,
        mesh=mesh,
        in_specs=placed,
        out_specs=P("member", None, None, "dx", "dy"),
        check_vma=False,
    )
```

```python
import functools

import jax
import jax.numpy as jnp
from jax import lax
from jax.experimental import pallas as pl
from jax.experimental.pallas import tpu as pltpu
from jax.sharding import PartitionSpec as P

STEPS = 4

integration_step = 0.2
diffusion = 0.1

OUTSIDE = 1.0e6
AXES = ("member", "dx", "dy")
VMEM = pl.BlockSpec(memory_space=pltpu.VMEM)
HBM = pl.BlockSpec(memory_space=pltpu.HBM)
MODEST = pltpu.CompilerParams(vmem_limit_bytes=8 * 2**20)


def send(value, target):
    sizes = [lax.axis_size(axis) for axis in AXES]
    pairs = []
    for member in range(sizes[0]):
        for i in range(sizes[1]):
            for j in range(sizes[2]):
                k, l, m = target(member, i, j)
                pairs.append(
                    (
                        (member * sizes[1] + i) * sizes[2] + j,
                        (k * sizes[1] + l) * sizes[2] + m,
                    )
                )
    return lax.ppermute(value, AXES, pairs)


def loop_target(rows, forward):
    def target(member, i, j):
        step = 1 if (member % 2 == 0) == forward else -1
        if 0 <= i + step < rows:
            return member, i + step, j
        return member ^ 1, i, j

    return target


def lanes_of(shape):
    return lax.broadcasted_iota(jnp.int32, shape, len(shape) - 1)


def turn(tile, by, axis=1):
    size = tile.shape[axis]
    return pltpu.roll(tile, by % size if isinstance(by, int) else lax.rem(by + size, size), axis)


def edges_of(tiles, width):
    lane = lanes_of(tiles[0].shape)
    total = None
    for x, tile in enumerate(tiles):
        moved = turn(tile, 2 * width * x + width)
        total = moved if total is None else jnp.where(lane < 2 * width * x, total, moved)
    return total


def pack_of(fields, along):
    return 2 if along == 2 and fields % 2 == 0 else 1


def packed(edges, early, has_left, along):
    if pack_of(len(edges), along) == 1:
        return edges
    by = jnp.where(has_left, -STEPS, STEPS)
    return [
        jnp.where(early == has_left, turn(b, by), a) for a, b in zip(edges[::2], edges[1::2])
    ]


def unpacked(tiles, fields, has_left, along):
    if pack_of(fields, along) == 1:
        return tiles
    by = jnp.where(has_left, -STEPS, STEPS)
    return [part for tile in tiles for part in (tile, turn(tile, by))]


def split_kernel(
    sizes, p_hbm, c_hbm, owner_hbm, m_hbm, t_hbm,
    pt_ref, keep_ref, send_ref, edge_ref, side_ref, metric_ref,
    p_ref, c_ref, owner_ref, t_ref, sems,
):
    fields, _, cols = p_ref.shape
    rows = t_ref.shape[0]
    levels = p_ref.shape[1] // rows
    half = rows // 2
    member = lax.axis_index("member")
    members = owner_ref.shape[0]
    first = lax.rem(member, 2) == 0
    copies = [
        pltpu.make_async_copy(owner_hbm, owner_ref, sems.at[0]),
        pltpu.make_async_copy(m_hbm, metric_ref.at[pl.ds(0, rows), :], sems.at[1]),
        pltpu.make_async_copy(t_hbm, t_ref, sems.at[2]),
    ]
    for f in range(fields):
        copies.append(pltpu.make_async_copy(p_hbm.at[f], p_ref.at[f], sems.at[3 + 2 * f]))
        copies.append(pltpu.make_async_copy(c_hbm.at[f], c_ref.at[f], sems.at[4 + 2 * f]))
    for copy in copies:
        copy.start()
    for copy in copies[:3]:
        copy.wait()
    metric_ref[pl.ds(rows, rows), :] = t_ref[...].astype(jnp.float32)
    level = lax.broadcasted_iota(jnp.int32, (levels, cols), 0)
    columns = []
    for x in range(rows):
        scale = jnp.broadcast_to(metric_ref[pl.ds(x, 1), :], (levels, cols))
        ground = jnp.broadcast_to(metric_ref[pl.ds(rows + x, 1), :], (levels, cols))
        columns.append(jnp.where(level == 0, scale, ground))
    side_ref[side_ref.shape[0] - 1] = edges_of(columns, STEPS)
    part_edges, state_edges = [], []
    weight = jnp.float32(0.0)
    for rank in range(members):
        per_rank = 2.0 * (members - rank) / (members * (members + 1.0))
        weight = weight + jnp.where(owner_ref[rank] == member, per_rank, 0.0)
    for f in range(fields):
        copies[3 + 2 * f].wait()
        copies[4 + 2 * f].wait()
        states, parts = [], []
        for x in range(rows):
            state = p_ref[f, pl.ds(x, levels, stride=rows), :]
            analysis = c_ref[f, pl.ds(x, levels, stride=rows), :]
            pt_ref[x * fields + f] = state
            states.append(state)
            parts.append(weight * analysis - state * (1.0 / members))
        for r in range(half):
            keep_ref[r * fields + f] = jnp.where(first, parts[r], parts[rows - 1 - r])
            send_ref[r * fields + f] = jnp.where(first, parts[rows - 1 - r], parts[r])
        part_edges.append(edges_of(parts, STEPS))
        state_edges.append(edges_of(states, STEPS))
    early = lax.rem(lanes_of((levels, cols)), 2 * STEPS) < STEPS
    has_left, _ = has_neighbours("dy", sizes[2])
    for k, edge in enumerate(packed(part_edges, early, has_left, sizes[2])):
        edge_ref[k] = edge
        side_ref[k] = edge
    for k, edge in enumerate(packed(state_edges, early, has_left, sizes[2])):
        side_ref[edge_ref.shape[0] + k] = edge


def has_neighbours(axis, size):
    place = lax.axis_index(axis)
    return place > 0, place < size - 1


def coefficients(level, scale, ground):
    scale = jnp.broadcast_to(scale, level.shape)
    ground = jnp.broadcast_to(ground, level.shape)
    mask = (level.astype(jnp.float32) >= ground).astype(jnp.float32)
    return (
        mask * (1.0 - 6.0 * integration_step * diffusion),
        mask * (integration_step * diffusion),
        mask * (scale * (0.5 * integration_step)),
    )


def updated(level, coefs, cur, dx, sx, dy, sy):
    levels = level.shape[0]
    new = []
    for f, here in enumerate(cur):
        advected = cur[0] * dx[f] + cur[1] * dy[f]
        if f == 0:
            advected = advected + dx[2]
        elif f == 1:
            advected = advected + dy[2]
        elif f == 2:
            advected = advected + (dx[0] + dy[1])
        upper = jnp.where(level < levels - 1, turn(here, -1, 0), 0.0)
        lower = jnp.where(level > 0, turn(here, 1, 0), 0.0)
        total = (sx[f] + sy[f]) + (upper + lower)
        new.append(coefs[0] * here + coefs[1] * total - coefs[2] * advected)
    return new


def row_step(level, lane, coefs, before, cur, after, beyond, spot):
    cols = lane.shape[1]
    dx, sx, dy, sy = [], [], [], []
    for f, here in enumerate(cur):
        outer = turn(beyond[f], -spot)
        north = jnp.where(lane == cols - 1, outer, turn(here, -1))
        south = jnp.where(lane == 0, outer, turn(here, 1))
        dx.append(after[f] - before[f])
        sx.append(after[f] + before[f])
        dy.append(north - south)
        sy.append(north + south)
    return updated(level, coefs, cur, dx, sx, dy, sy)


def strip_step(level, coefs, here, group):
    dx, sx, dy, sy = [], [], [], []
    for tile in here:
        east, west = turn(tile, -group), turn(tile, group)
        north, south = turn(tile, -1), turn(tile, 1)
        dx.append(east - west)
        sx.append(east + west)
        dy.append(north - south)
        sy.append(north + south)
    return updated(level, coefs, here, dx, sx, dy, sy)


def outside_columns(lane, width, strips, has_left):
    place = lax.rem(lane, 2 * width)
    if len(strips) == 2:
        return [jnp.where(place == width - 1, a, turn(b, -2)) for a, b in zip(*strips)]
    before = jnp.logical_and(place == width - 1, has_left)
    after = jnp.logical_and(place == width - 2, jnp.logical_not(has_left))
    return [jnp.where(before, a, jnp.where(after, turn(a, -2), 0.0)) for a in strips[0]]


def strips_of(early, own, beside, has_left):
    if len(beside) == 2:
        return [jnp.where(early, beside[0], own), jnp.where(early, own, beside[1])]
    return [jnp.where(early == has_left, beside[0], own)]


def join_kernel(
    sizes, n_sides, pt_ref, mine_ref, edge_ref, other_ref, metric_ref, side_ref, *refs
):
    near, (start_ref, beside_ref, first_ref, second_ref) = refs[:n_sides], refs[n_sides:]
    rows, cols = metric_ref.shape[0] // 2, metric_ref.shape[1]
    levels = pt_ref.shape[1]
    fields = pt_ref.shape[0] // rows
    wide = STEPS
    parity = lax.rem(lax.axis_index("member"), 2)
    has_left, has_right = has_neighbours("dy", sizes[2])
    lane = lanes_of((levels, cols))
    early = lax.rem(lane, 2 * wide) < wide
    quarter = 2 * wide * wide
    sides = beside_ref.shape[0] // (fields + 1)

    for r in range(wide):
        for f in range(fields):
            mine, other = mine_ref[r * fields + f], other_ref[r * fields + f]
            low, high = jnp.where(parity == 0, mine, other), jnp.where(parity == 0, other, mine)
            start_ref[r * fields + f] = pt_ref[r * fields + f] + low
            end = 2 * wide - 1 - r
            start_ref[end * fields + f] = pt_ref[(rows - 1 - r) * fields + f] + high

    def ends_of(strips, up):
        if sides == 1:
            packed = None
            for f in range(fields):
                moved = turn(strips[f][0], jnp.where(up, quarter, 0) + f * quarter)
                packed = moved if f == 0 else jnp.where(lane < f * quarter, packed, moved)
            return [packed, strips[fields][0]]
        return [
            jnp.where(
                lane < quarter,
                a,
                jnp.where(
                    lane < 2 * quarter,
                    turn(b, quarter),
                    jnp.where(lane < cols - quarter, turn(b, -quarter), a),
                ),
            )
            for a, b in strips
        ]

    per_side = edge_ref.shape[0] // sides
    sums = [
        unpacked(
            [
                near[side][per_side + k]
                + (edge_ref[side * per_side + k] + other_ref[wide * fields + side * per_side + k])
                for k in range(per_side)
            ],
            fields, has_left, sizes[2],
        )
        for side in range(sides)
    ]
    strips = []
    for f in range(fields + 1):
        beside = []
        for side in range(sides):
            value = sums[side][f] if f < fields else near[side][2 * per_side]
            if sides == 2:
                value = jnp.where((has_left, has_right)[side], value, 0.0 if f < fields else OUTSIDE)
            beside.append(value)
            beside_ref[side * (fields + 1) + f] = value
        if f < fields:
            own = None
            for k in range(2 * wide):
                x = k if k < wide else rows - 2 * wide + k
                moved = turn(start_ref[k * fields + f], 2 * wide * x + wide)
                own = moved if own is None else jnp.where(lane < 2 * wide * x, own, moved)
        else:
            own = side_ref[side_ref.shape[0] - 1]
        strips.append(strips_of(early, own, beside, has_left))
    scale, ground = metric_ref[pl.ds(0, rows), :], metric_ref[pl.ds(rows, rows), :]
    tops = jnp.concatenate([scale[rows - wide :], ground[rows - wide :]], axis=0)
    bottoms = jnp.concatenate([scale[:wide], ground[:wide]], axis=0)
    for message, up in ((first_ref, parity == 0), (second_ref, parity == 1)):
        base = jnp.where(up, wide, 0) * fields
        for k in range(wide * fields):
            message[k] = start_ref[base + k]
        message[wide * fields] = jnp.where(up, tops, bottoms)
        for k, end in enumerate(ends_of(strips, up)):
            message[wide * fields + 1 + k] = end


def middle_kernel(
    sizes, pt_ref, outer_ref, mine_ref, other_ref, metric_ref, side_ref, beside_ref,
    strip_ref, saved_ref, done_ref, a_ref, b_ref,
):
    rows, cols = metric_ref.shape[0] // 2, metric_ref.shape[1]
    levels = pt_ref.shape[1]
    fields = pt_ref.shape[0] // rows
    wide = STEPS
    group = 2 * wide
    half = rows // 2
    parity = lax.rem(lax.axis_index("member"), 2)
    lane = lanes_of((levels, cols))
    level = lax.broadcasted_iota(jnp.int32, (levels, cols), 0)
    early = lax.rem(lane, group) < wide
    for r in range(wide):
        for f in range(fields):
            a_ref[r * fields + f] = outer_ref[r * fields + f]
            a_ref[(rows - 1 - r) * fields + f] = outer_ref[(group - 1 - r) * fields + f]
    for r in range(wide, half):
        for f in range(fields):
            k = (r - wide) * fields + f
            mine, other = mine_ref[k], other_ref[k]
            low, high = jnp.where(parity == 0, mine, other), jnp.where(parity == 0, other, mine)
            a_ref[r * fields + f] = pt_ref[r * fields + f] + low
            mirrored = (rows - 1 - r) * fields + f
            a_ref[mirrored] = pt_ref[mirrored] + high
    has_left, _ = has_neighbours("dy", sizes[2])
    sides = beside_ref.shape[0] // (fields + 1)
    strips = [[] for _ in range(sides)]
    for f in range(fields + 1):
        if f < fields:
            own = edges_of([a_ref[x * fields + f] for x in range(rows)], wide)
        else:
            own = side_ref[side_ref.shape[0] - 1]
        beside = [beside_ref[side * (fields + 1) + f] for side in range(sides)]
        for side, strip in enumerate(strips_of(early, own, beside, has_left)):
            strips[side].append(strip)
            strip_ref[side * (fields + 1) + f] = strip
    strip_coefs = [coefficients(level, side[fields][0:1], side[fields][1:2]) for side in strips]
    strips = [side[:fields] for side in strips]
    coefs = [
        coefficients(level, metric_ref[pl.ds(x, 1), :], metric_ref[pl.ds(rows + x, 1), :])
        for x in range(rows)
    ]
    for number in range(STEPS):
        source, sink = (a_ref, b_ref) if number % 2 == 0 else (b_ref, a_ref)
        beyond = outside_columns(lane, wide, strips, has_left)
        bottom, top = number + 1, rows - 1 - number
        row = lambda x: [source[x * fields + f] for f in range(fields)]
        before, cur = row(bottom - 1), row(bottom)
        for x in range(bottom, top):
            after = row(x + 1)
            new = row_step(
                level, lane, coefs[x], before, cur, after, beyond, group * x + wide - 1
            )
            edge = {bottom: 0, bottom + 1: 1, top - 2: 2, top - 1: 3}.get(x)
            for f in range(fields):
                if number == STEPS - 1:
                    done_ref[(x - wide) * fields + f] = new[f]
                else:
                    sink[x * fields + f] = new[f]
                    if edge is not None:
                        saved_ref[(4 * number + edge) * fields + f] = new[f]
            before, cur = cur, after
        if number < STEPS - 1:
            strips = [
                strip_step(level, coef, tiles, group) for coef, tiles in zip(strip_coefs, strips)
            ]


def outer_kernel(
    sizes, outer_ref, strip_ref, saved_ref, done_ref, metric_ref, first_ref, second_ref,
    out_hbm, out_ref, sems,
):
    rows, cols = metric_ref.shape[0] // 2, metric_ref.shape[1]
    levels = outer_ref.shape[1]
    wide = STEPS
    group = 2 * wide
    fields = outer_ref.shape[0] // group
    half = rows // 2
    even = lax.rem(lax.axis_index("member"), 2) == 0
    has_low, has_high = has_neighbours("dx", sizes[1])
    lane = lanes_of((levels, cols))
    level = lax.broadcasted_iota(jnp.int32, (levels, cols), 0)
    quarter = group * wide

    def low(k, empty=0.0):
        return jnp.where(has_low, jnp.where(even, first_ref[k], second_ref[k]), empty)

    def high(k, empty=0.0):
        return jnp.where(has_high, jnp.where(even, second_ref[k], first_ref[k]), empty)

    has_left, _ = has_neighbours("dy", sizes[2])
    sides = strip_ref.shape[0] // (fields + 1)

    def stretched(is_low, side, f):
        mine = strip_ref[side * (fields + 1) + f]
        empty = 0.0 if f < fields else OUTSIDE
        if sides == 1 and f < fields:
            k, by = 0, (-f if is_low else -1 - f)
        else:
            k, by = min(f, 1) if sides == 1 else f, ((1, 2) if is_low else (-1, 2))[side]
        theirs = turn((low if is_low else high)(wide * fields + 1 + k, empty), by * quarter)
        if is_low:
            return jnp.where(lane < quarter, theirs, turn(mine, quarter))
        return jnp.where(lane < cols - quarter, turn(mine, -quarter), theirs)

    beyond = {}
    for is_low in (True, False):
        strips = [[stretched(is_low, side, f) for f in range(fields + 1)] for side in range(sides)]
        coefs = [coefficients(level, side[fields][0:1], side[fields][1:2]) for side in strips]
        strips = [side[:fields] for side in strips]
        for number in range(STEPS):
            beyond[is_low, number] = outside_columns(lane, wide, strips, has_left)
            if number < STEPS - 1:
                strips = [strip_step(level, c, tiles, group) for c, tiles in zip(coefs, strips)]

    for x in range(wide, rows - wide):
        for f in range(fields):
            out_ref[f, pl.ds(x, levels, stride=rows), :] = done_ref[(x - wide) * fields + f]

    def saved(number, edge):
        return [saved_ref[(4 * (number - 1) + edge) * fields + f] for f in range(fields)]

    def finish(is_low):
        metric = wide * fields
        halo = low(metric, OUTSIDE) if is_low else high(metric, OUTSIDE)
        coefs, state = {}, {}
        for r in range(wide):
            message = [(low if is_low else high)(r * fields + f) for f in range(fields)]
            state[r - wide if is_low else rows + r] = message
            coefs[r - wide if is_low else rows + r] = coefficients(
                level, halo[r : r + 1], halo[wide + r : wide + r + 1]
            )
            x = r if is_low else rows - wide + r
            k = r if is_low else wide + r
            state[x] = [outer_ref[k * fields + f] for f in range(fields)]
            coefs[x] = coefficients(
                level, metric_ref[pl.ds(x, 1), :], metric_ref[pl.ds(rows + x, 1), :]
            )
        for number in range(STEPS):
            if number > 0:
                if is_low:
                    state[number], state[number + 1] = saved(number, 0), saved(number, 1)
                else:
                    state[rows - 2 - number], state[rows - 1 - number] = saved(number, 2), saved(number, 3)
            bottom = number + 1 - wide if is_low else rows - 1 - number
            new = {}
            for x in range(bottom, bottom + wide):
                spot = group * (x + (wide if is_low else -wide)) + wide - 1
                new[x] = row_step(
                    level, lane, coefs[x], state[x - 1], state[x], state[x + 1],
                    beyond[is_low, number], spot,
                )
            state = new
        for x, tiles in state.items():
            for f in range(fields):
                out_ref[f, pl.ds(x, levels, stride=rows), :] = tiles[f]

    copies = []
    for n, is_low in enumerate((True, False)):
        finish(is_low)
        part = pl.ds(n * half, half)
        source = out_ref.reshape(fields * levels, rows, cols)
        copies.append(
            pltpu.make_async_copy(source.at[:, part, :], out_hbm.at[:, part, :], sems.at[n])
        )
        copies[-1].start()
    for copy in copies:
        copy.wait()


def pair_kernel(keep_ref, given_ref, outer_ref, inner_ref):
    count, skip = outer_ref.shape[0], keep_ref.shape[0] - inner_ref.shape[0]
    for k in range(keep_ref.shape[0]):
        total = keep_ref[k] + given_ref[k]
        if k < count:
            outer_ref[k] = total
        if k >= skip:
            inner_ref[k - skip] = total


def on_device(perturbed_states, control, owner, map_factor, terrain):
    _, fields, levels, rows, cols = perturbed_states.shape
    sizes = tuple(lax.axis_size(axis) for axis in AXES)
    members, along = sizes[0], sizes[2]
    half = rows // 2
    n_edges = fields // pack_of(fields, along)
    tile = (levels, cols)

    def tiles(count):
        return jax.ShapeDtypeStruct((count, *tile), jnp.float32)

    def room(count):
        return pltpu.VMEM((count, *tile), jnp.float32)

    flat = (fields, levels * rows, cols)
    states, keep, give, edge, side, metric = pl.pallas_call(
        functools.partial(split_kernel, sizes),
        out_shape=(
            tiles(rows * fields),
            tiles(half * fields),
            tiles(half * fields),
            tiles(n_edges),
            tiles(2 * n_edges + 1),
            jax.ShapeDtypeStruct((2 * rows, cols), jnp.float32),
        ),
        in_specs=[HBM] * 5,
        out_specs=(VMEM,) * 6,
        scratch_shapes=[
            pltpu.VMEM(flat, jnp.float32),
            pltpu.VMEM(flat, jnp.float32),
            pltpu.SMEM(owner.shape, jnp.int32),
            pltpu.VMEM((rows, cols), jnp.int32),
            pltpu.SemaphoreType.DMA((2 * fields + 3,)),
        ],
        compiler_params=MODEST,
        name="split",
    )(
        *(
            pltpu.with_memory_space_constraint(value, pltpu.HBM)
            for value in (
                perturbed_states.reshape(flat), control.reshape(flat), owner, map_factor, terrain
            )
        )
    )

    def over_members(value, bit):
        return send(value, lambda k, i, j: (k ^ bit, i, j))

    def over_chips(value):
        bit = 2
        while bit < members:
            value = value + over_members(value, bit)
            bit *= 2
        return value

    given = over_members(give, 1)
    def from_beside(value, step, bit):
        return send(value, lambda k, i, j: (k ^ bit, i, (j + step) % along))

    steps = (1, -1) if along > 2 else (1,)
    near = [from_beside(side, step, 0) for step in steps]
    edges = []
    for step, n in zip(steps, near):
        total = n[:n_edges]
        for bit in range(2, members, 2):
            total = total + from_beside(edge, step, bit)
        edges.append(total)
    edges = jnp.concatenate(edges, axis=0)
    cut = STEPS * fields
    outer, inner = pl.pallas_call(
        pair_kernel,
        out_shape=(tiles(cut), tiles(half * fields - cut + fields)),
        in_specs=[VMEM] * 2,
        out_specs=(VMEM,) * 2,
        compiler_params=MODEST,
        name="pair",
    )(keep, given)
    outer = over_chips(outer)
    inner = over_chips(inner)[fields:]

    other = over_members(jnp.concatenate([outer, edges], axis=0), 1)
    count = cut + (3 if along == 2 else fields + 2)
    start, beside, first, second = pl.pallas_call(
        functools.partial(join_kernel, sizes, len(near)),
        out_shape=(tiles(2 * cut), tiles(len(near) * (fields + 1)), tiles(count), tiles(count)),
        in_specs=[VMEM] * (6 + len(near)),
        out_specs=(VMEM,) * 4,
        compiler_params=MODEST,
        name="join",
    )(states, outer, edges, other, metric, side, *near)
    first_in = send(first, loop_target(sizes[1], True))
    second_in = send(second, loop_target(sizes[1], False))
    inner, _ = lax.optimization_barrier((inner, first))
    other = over_members(inner, 1)
    strips, saved, done = pl.pallas_call(
        functools.partial(middle_kernel, sizes),
        out_shape=(
            tiles(len(near) * (fields + 1)),
            tiles(4 * (STEPS - 1) * fields),
            tiles((rows - 2 * STEPS) * fields),
        ),
        in_specs=[VMEM] * 7,
        out_specs=(VMEM,) * 3,
        scratch_shapes=[room(rows * fields), room(rows * fields)],
        compiler_params=MODEST,
        cost_estimate=pl.CostEstimate(
            flops=30 * rows * fields * levels * cols * STEPS, bytes_accessed=2**20, transcendentals=0
        ),
        name="middle",
    )(states, start, inner, other, metric, side, beside)
    out = pl.pallas_call(
        functools.partial(outer_kernel, sizes),
        out_shape=jax.ShapeDtypeStruct((fields * levels, rows, cols), jnp.float32),
        in_specs=[VMEM] * 7,
        out_specs=HBM,
        scratch_shapes=[pltpu.VMEM(flat, jnp.float32), pltpu.SemaphoreType.DMA((2,))],
        compiler_params=MODEST,
        name="outer",
    )(start, strips, saved, done, metric, first_in, second_in)
    return out.reshape(perturbed_states.shape)


def solution(mesh):
    placed = (
        P("member", None, None, "dx", "dy"),
        P("member", None, None, "dx", "dy"),
        P(),
        P("dx", "dy"),
        P("dx", "dy"),
    )
    return jax.shard_map(
        on_device,
        mesh=mesh,
        in_specs=placed,
        out_specs=P("member", None, None, "dx", "dy"),
        check_vma=False,
    )
```

```python
import functools

import jax
import jax.numpy as jnp
from jax import lax
from jax.experimental import pallas as pl
from jax.experimental.pallas import tpu as pltpu
from jax.sharding import PartitionSpec as P

STEPS = 4

integration_step = 0.2
diffusion = 0.1

OUTSIDE = 1.0e6
AXES = ("member", "dx", "dy")
VMEM = pl.BlockSpec(memory_space=pltpu.VMEM)
HBM = pl.BlockSpec(memory_space=pltpu.HBM)
MODEST = pltpu.CompilerParams(vmem_limit_bytes=8 * 2**20)


def send(value, target):
    sizes = [lax.axis_size(axis) for axis in AXES]
    pairs = []
    for member in range(sizes[0]):
        for i in range(sizes[1]):
            for j in range(sizes[2]):
                k, l, m = target(member, i, j)
                pairs.append(
                    (
                        (member * sizes[1] + i) * sizes[2] + j,
                        (k * sizes[1] + l) * sizes[2] + m,
                    )
                )
    return lax.ppermute(value, AXES, pairs)


def loop_target(rows, forward):
    def target(member, i, j):
        step = 1 if (member % 2 == 0) == forward else -1
        if 0 <= i + step < rows:
            return member, i + step, j
        return member ^ 1, i, j

    return target


def lanes_of(shape):
    return lax.broadcasted_iota(jnp.int32, shape, len(shape) - 1)


def turn(tile, by, axis=1):
    size = tile.shape[axis]
    return pltpu.roll(tile, by % size if isinstance(by, int) else lax.rem(by + size, size), axis)


def edges_of(tiles, width):
    lane = lanes_of(tiles[0].shape)
    total = None
    for x, tile in enumerate(tiles):
        moved = turn(tile, 2 * width * x + width)
        total = moved if total is None else jnp.where(lane < 2 * width * x, total, moved)
    return total


def pack_of(fields, along):
    return 2 if along == 2 and fields % 2 == 0 else 1


def packed(edges, early, has_left, along):
    if pack_of(len(edges), along) == 1:
        return edges
    by = jnp.where(has_left, -STEPS, STEPS)
    return [
        jnp.where(early == has_left, turn(b, by), a) for a, b in zip(edges[::2], edges[1::2])
    ]


def unpacked(tiles, fields, has_left, along):
    if pack_of(fields, along) == 1:
        return tiles
    by = jnp.where(has_left, -STEPS, STEPS)
    return [part for tile in tiles for part in (tile, turn(tile, by))]


def split_kernel(
    sizes, p_hbm, c_hbm, owner_hbm, m_hbm, t_hbm,
    pt_ref, keep_ref, send_ref, edge_ref, side_ref, metric_ref,
    p_ref, c_ref, owner_ref, t_ref, sems,
):
    fields, _, cols = p_ref.shape
    rows = t_ref.shape[0]
    levels = p_ref.shape[1] // rows
    half = rows // 2
    member = lax.axis_index("member")
    members = owner_ref.shape[0]
    first = lax.rem(member, 2) == 0
    copies = [
        pltpu.make_async_copy(owner_hbm, owner_ref, sems.at[0]),
        pltpu.make_async_copy(m_hbm, metric_ref.at[pl.ds(0, rows), :], sems.at[1]),
        pltpu.make_async_copy(t_hbm, t_ref, sems.at[2]),
    ]
    together = 2 if fields % 2 == 0 else 1
    for n in range(fields // together):
        some = pl.ds(n * together, together)
        copies.append(pltpu.make_async_copy(p_hbm.at[some], p_ref.at[some], sems.at[3 + 2 * n]))
        copies.append(pltpu.make_async_copy(c_hbm.at[some], c_ref.at[some], sems.at[4 + 2 * n]))
    for copy in copies:
        copy.start()
    for copy in copies[:3]:
        copy.wait()
    metric_ref[pl.ds(rows, rows), :] = t_ref[...].astype(jnp.float32)
    level = lax.broadcasted_iota(jnp.int32, (levels, cols), 0)
    columns = []
    for x in range(rows):
        scale = jnp.broadcast_to(metric_ref[pl.ds(x, 1), :], (levels, cols))
        ground = jnp.broadcast_to(metric_ref[pl.ds(rows + x, 1), :], (levels, cols))
        columns.append(jnp.where(level == 0, scale, ground))
    side_ref[side_ref.shape[0] - 1] = edges_of(columns, STEPS)
    part_edges, state_edges = [], []
    weight = jnp.float32(0.0)
    for rank in range(members):
        per_rank = 2.0 * (members - rank) / (members * (members + 1.0))
        weight = weight + jnp.where(owner_ref[rank] == member, per_rank, 0.0)
    for f in range(fields):
        if f % together == 0:
            copies[3 + 2 * (f // together)].wait()
            copies[4 + 2 * (f // together)].wait()
        states, parts = [], []
        for x in range(rows):
            state = p_ref[f, pl.ds(x, levels, stride=rows), :]
            analysis = c_ref[f, pl.ds(x, levels, stride=rows), :]
            pt_ref[x * fields + f] = state
            states.append(state)
            parts.append(weight * analysis - state * (1.0 / members))
        for r in range(half):
            keep_ref[r * fields + f] = jnp.where(first, parts[r], parts[rows - 1 - r])
            send_ref[r * fields + f] = jnp.where(first, parts[rows - 1 - r], parts[r])
        part_edges.append(edges_of(parts, STEPS))
        state_edges.append(edges_of(states, STEPS))
    early = lax.rem(lanes_of((levels, cols)), 2 * STEPS) < STEPS
    has_left, _ = has_neighbours("dy", sizes[2])
    for k, edge in enumerate(packed(part_edges, early, has_left, sizes[2])):
        edge_ref[k] = edge
        side_ref[k] = edge
    for k, edge in enumerate(packed(state_edges, early, has_left, sizes[2])):
        side_ref[edge_ref.shape[0] + k] = edge


def has_neighbours(axis, size):
    place = lax.axis_index(axis)
    return place > 0, place < size - 1


def coefficients(level, scale, ground):
    scale = jnp.broadcast_to(scale, level.shape)
    ground = jnp.broadcast_to(ground, level.shape)
    mask = (level.astype(jnp.float32) >= ground).astype(jnp.float32)
    return (
        mask * (1.0 - 6.0 * integration_step * diffusion),
        mask * (integration_step * diffusion),
        mask * (scale * (0.5 * integration_step)),
    )


def updated(level, coefs, cur, dx, sx, dy, sy):
    levels = level.shape[0]
    new = []
    for f, here in enumerate(cur):
        advected = cur[0] * dx[f] + cur[1] * dy[f]
        if f == 0:
            advected = advected + dx[2]
        elif f == 1:
            advected = advected + dy[2]
        elif f == 2:
            advected = advected + (dx[0] + dy[1])
        upper = jnp.where(level < levels - 1, turn(here, -1, 0), 0.0)
        lower = jnp.where(level > 0, turn(here, 1, 0), 0.0)
        total = (sx[f] + sy[f]) + (upper + lower)
        new.append(coefs[0] * here + coefs[1] * total - coefs[2] * advected)
    return new


def row_step(level, lane, coefs, before, cur, after, beyond, spot):
    cols = lane.shape[1]
    dx, sx, dy, sy = [], [], [], []
    for f, here in enumerate(cur):
        outer = turn(beyond[f], -spot)
        north = jnp.where(lane == cols - 1, outer, turn(here, -1))
        south = jnp.where(lane == 0, outer, turn(here, 1))
        dx.append(after[f] - before[f])
        sx.append(after[f] + before[f])
        dy.append(north - south)
        sy.append(north + south)
    return updated(level, coefs, cur, dx, sx, dy, sy)


def strip_step(level, coefs, here, group):
    dx, sx, dy, sy = [], [], [], []
    for tile in here:
        east, west = turn(tile, -group), turn(tile, group)
        north, south = turn(tile, -1), turn(tile, 1)
        dx.append(east - west)
        sx.append(east + west)
        dy.append(north - south)
        sy.append(north + south)
    return updated(level, coefs, here, dx, sx, dy, sy)


def outside_columns(lane, width, strips, has_left):
    place = lax.rem(lane, 2 * width)
    if len(strips) == 2:
        return [jnp.where(place == width - 1, a, turn(b, -2)) for a, b in zip(*strips)]
    before = jnp.logical_and(place == width - 1, has_left)
    after = jnp.logical_and(place == width - 2, jnp.logical_not(has_left))
    return [jnp.where(before, a, jnp.where(after, turn(a, -2), 0.0)) for a in strips[0]]


def strips_of(early, own, beside, has_left):
    if len(beside) == 2:
        return [jnp.where(early, beside[0], own), jnp.where(early, own, beside[1])]
    return [jnp.where(early == has_left, beside[0], own)]


def join_kernel(
    sizes, n_sides, pt_ref, mine_ref, edge_ref, other_ref, metric_ref, side_ref, *refs
):
    near, (start_ref, beside_ref, first_ref, second_ref) = refs[:n_sides], refs[n_sides:]
    rows, cols = metric_ref.shape[0] // 2, metric_ref.shape[1]
    levels = pt_ref.shape[1]
    fields = pt_ref.shape[0] // rows
    wide = STEPS
    parity = lax.rem(lax.axis_index("member"), 2)
    has_left, has_right = has_neighbours("dy", sizes[2])
    lane = lanes_of((levels, cols))
    early = lax.rem(lane, 2 * wide) < wide
    quarter = 2 * wide * wide
    sides = beside_ref.shape[0] // (fields + 1)

    for r in range(wide):
        for f in range(fields):
            mine, other = mine_ref[r * fields + f], other_ref[r * fields + f]
            low, high = jnp.where(parity == 0, mine, other), jnp.where(parity == 0, other, mine)
            start_ref[r * fields + f] = pt_ref[r * fields + f] + low
            end = 2 * wide - 1 - r
            start_ref[end * fields + f] = pt_ref[(rows - 1 - r) * fields + f] + high

    def ends_of(strips, up):
        if sides == 1:
            packed = None
            for f in range(fields):
                moved = turn(strips[f][0], jnp.where(up, quarter, 0) + f * quarter)
                packed = moved if f == 0 else jnp.where(lane < f * quarter, packed, moved)
            return [packed, strips[fields][0]]
        return [
            jnp.where(
                lane < quarter,
                a,
                jnp.where(
                    lane < 2 * quarter,
                    turn(b, quarter),
                    jnp.where(lane < cols - quarter, turn(b, -quarter), a),
                ),
            )
            for a, b in strips
        ]

    per_side = edge_ref.shape[0] // sides
    sums = [
        unpacked(
            [
                near[side][per_side + k]
                + (edge_ref[side * per_side + k] + other_ref[wide * fields + side * per_side + k])
                for k in range(per_side)
            ],
            fields, has_left, sizes[2],
        )
        for side in range(sides)
    ]
    strips = []
    for f in range(fields + 1):
        beside = []
        for side in range(sides):
            value = sums[side][f] if f < fields else near[side][2 * per_side]
            if sides == 2:
                value = jnp.where((has_left, has_right)[side], value, 0.0 if f < fields else OUTSIDE)
            beside.append(value)
            beside_ref[side * (fields + 1) + f] = value
        if f < fields:
            own = None
            for k in range(2 * wide):
                x = k if k < wide else rows - 2 * wide + k
                moved = turn(start_ref[k * fields + f], 2 * wide * x + wide)
                own = moved if own is None else jnp.where(lane < 2 * wide * x, own, moved)
        else:
            own = side_ref[side_ref.shape[0] - 1]
        strips.append(strips_of(early, own, beside, has_left))
    scale, ground = metric_ref[pl.ds(0, rows), :], metric_ref[pl.ds(rows, rows), :]
    tops = jnp.concatenate([scale[rows - wide :], ground[rows - wide :]], axis=0)
    bottoms = jnp.concatenate([scale[:wide], ground[:wide]], axis=0)
    for message, up in ((first_ref, parity == 0), (second_ref, parity == 1)):
        base = jnp.where(up, wide, 0) * fields
        for k in range(wide * fields):
            message[k] = start_ref[base + k]
        message[wide * fields] = jnp.where(up, tops, bottoms)
        for k, end in enumerate(ends_of(strips, up)):
            message[wide * fields + 1 + k] = end


def middle_kernel(
    sizes, pt_ref, outer_ref, mine_ref, other_ref, metric_ref, side_ref, beside_ref,
    strip_ref, saved_ref, done_ref, a_ref, b_ref,
):
    rows, cols = metric_ref.shape[0] // 2, metric_ref.shape[1]
    levels = pt_ref.shape[1]
    fields = pt_ref.shape[0] // rows
    wide = STEPS
    group = 2 * wide
    half = rows // 2
    parity = lax.rem(lax.axis_index("member"), 2)
    lane = lanes_of((levels, cols))
    level = lax.broadcasted_iota(jnp.int32, (levels, cols), 0)
    early = lax.rem(lane, group) < wide
    for r in range(wide):
        for f in range(fields):
            a_ref[r * fields + f] = outer_ref[r * fields + f]
            a_ref[(rows - 1 - r) * fields + f] = outer_ref[(group - 1 - r) * fields + f]
    for r in range(wide, half):
        for f in range(fields):
            k = (r - wide) * fields + f
            mine, other = mine_ref[k], other_ref[k]
            low, high = jnp.where(parity == 0, mine, other), jnp.where(parity == 0, other, mine)
            a_ref[r * fields + f] = pt_ref[r * fields + f] + low
            mirrored = (rows - 1 - r) * fields + f
            a_ref[mirrored] = pt_ref[mirrored] + high
    has_left, _ = has_neighbours("dy", sizes[2])
    sides = beside_ref.shape[0] // (fields + 1)
    strips = [[] for _ in range(sides)]
    for f in range(fields + 1):
        if f < fields:
            own = edges_of([a_ref[x * fields + f] for x in range(rows)], wide)
        else:
            own = side_ref[side_ref.shape[0] - 1]
        beside = [beside_ref[side * (fields + 1) + f] for side in range(sides)]
        for side, strip in enumerate(strips_of(early, own, beside, has_left)):
            strips[side].append(strip)
            strip_ref[side * (fields + 1) + f] = strip
    strip_coefs = [coefficients(level, side[fields][0:1], side[fields][1:2]) for side in strips]
    strips = [side[:fields] for side in strips]
    coefs = [
        coefficients(level, metric_ref[pl.ds(x, 1), :], metric_ref[pl.ds(rows + x, 1), :])
        for x in range(rows)
    ]
    for number in range(STEPS):
        source, sink = (a_ref, b_ref) if number % 2 == 0 else (b_ref, a_ref)
        beyond = outside_columns(lane, wide, strips, has_left)
        bottom, top = number + 1, rows - 1 - number
        row = lambda x: [source[x * fields + f] for f in range(fields)]
        before, cur = row(bottom - 1), row(bottom)
        for x in range(bottom, top):
            after = row(x + 1)
            new = row_step(
                level, lane, coefs[x], before, cur, after, beyond, group * x + wide - 1
            )
            edge = {bottom: 0, bottom + 1: 1, top - 2: 2, top - 1: 3}.get(x)
            for f in range(fields):
                if number == STEPS - 1:
                    done_ref[(x - wide) * fields + f] = new[f]
                else:
                    sink[x * fields + f] = new[f]
                    if edge is not None:
                        saved_ref[(4 * number + edge) * fields + f] = new[f]
            before, cur = cur, after
        if number < STEPS - 1:
            strips = [
                strip_step(level, coef, tiles, group) for coef, tiles in zip(strip_coefs, strips)
            ]


def outer_kernel(
    sizes, outer_ref, strip_ref, saved_ref, done_ref, metric_ref, first_ref, second_ref,
    out_hbm, out_ref, sems,
):
    rows, cols = metric_ref.shape[0] // 2, metric_ref.shape[1]
    levels = outer_ref.shape[1]
    wide = STEPS
    group = 2 * wide
    fields = outer_ref.shape[0] // group
    half = rows // 2
    even = lax.rem(lax.axis_index("member"), 2) == 0
    has_low, has_high = has_neighbours("dx", sizes[1])
    lane = lanes_of((levels, cols))
    level = lax.broadcasted_iota(jnp.int32, (levels, cols), 0)
    quarter = group * wide

    def low(k, empty=0.0):
        return jnp.where(has_low, jnp.where(even, first_ref[k], second_ref[k]), empty)

    def high(k, empty=0.0):
        return jnp.where(has_high, jnp.where(even, second_ref[k], first_ref[k]), empty)

    has_left, _ = has_neighbours("dy", sizes[2])
    sides = strip_ref.shape[0] // (fields + 1)

    def stretched(is_low, side, f):
        mine = strip_ref[side * (fields + 1) + f]
        empty = 0.0 if f < fields else OUTSIDE
        if sides == 1 and f < fields:
            k, by = 0, (-f if is_low else -1 - f)
        else:
            k, by = min(f, 1) if sides == 1 else f, ((1, 2) if is_low else (-1, 2))[side]
        theirs = turn((low if is_low else high)(wide * fields + 1 + k, empty), by * quarter)
        if is_low:
            return jnp.where(lane < quarter, theirs, turn(mine, quarter))
        return jnp.where(lane < cols - quarter, turn(mine, -quarter), theirs)

    beyond = {}
    for is_low in (True, False):
        strips = [[stretched(is_low, side, f) for f in range(fields + 1)] for side in range(sides)]
        coefs = [coefficients(level, side[fields][0:1], side[fields][1:2]) for side in strips]
        strips = [side[:fields] for side in strips]
        for number in range(STEPS):
            beyond[is_low, number] = outside_columns(lane, wide, strips, has_left)
            if number < STEPS - 1:
                strips = [strip_step(level, c, tiles, group) for c, tiles in zip(coefs, strips)]

    for x in range(wide, rows - wide):
        for f in range(fields):
            out_ref[f, pl.ds(x, levels, stride=rows), :] = done_ref[(x - wide) * fields + f]

    def saved(number, edge):
        return [saved_ref[(4 * (number - 1) + edge) * fields + f] for f in range(fields)]

    def prepare(is_low):
        metric = wide * fields
        halo = low(metric, OUTSIDE) if is_low else high(metric, OUTSIDE)
        coefs, state = {}, {}
        for r in range(wide):
            message = [(low if is_low else high)(r * fields + f) for f in range(fields)]
            state[r - wide if is_low else rows + r] = message
            coefs[r - wide if is_low else rows + r] = coefficients(
                level, halo[r : r + 1], halo[wide + r : wide + r + 1]
            )
            x = r if is_low else rows - wide + r
            k = r if is_low else wide + r
            state[x] = [outer_ref[k * fields + f] for f in range(fields)]
            coefs[x] = coefficients(
                level, metric_ref[pl.ds(x, 1), :], metric_ref[pl.ds(rows + x, 1), :]
            )
        return state, coefs

    def advanced(is_low, number, state, coefs):
        if number > 0:
            if is_low:
                state[number], state[number + 1] = saved(number, 0), saved(number, 1)
            else:
                state[rows - 2 - number], state[rows - 1 - number] = saved(number, 2), saved(number, 3)
        bottom = number + 1 - wide if is_low else rows - 1 - number
        new = {}
        for x in range(bottom, bottom + wide):
            spot = group * (x + (wide if is_low else -wide)) + wide - 1
            new[x] = row_step(
                level, lane, coefs[x], state[x - 1], state[x], state[x + 1],
                beyond[is_low, number], spot,
            )
        return new

    parts = {is_low: prepare(is_low) for is_low in (True, False)}
    for number in range(STEPS):
        for is_low, (state, coefs) in parts.items():
            parts[is_low] = advanced(is_low, number, state, coefs), coefs
    for state, _ in parts.values():
        for x, tiles in state.items():
            for f in range(fields):
                out_ref[f, pl.ds(x, levels, stride=rows), :] = tiles[f]

    copies = []
    for n, is_low in enumerate((True, False)):
        part = pl.ds(n * half, half)
        source = out_ref.reshape(fields * levels, rows, cols)
        copies.append(
            pltpu.make_async_copy(source.at[:, part, :], out_hbm.at[:, part, :], sems.at[n])
        )
        copies[-1].start()
    for copy in copies:
        copy.wait()


def pair_kernel(keep_ref, given_ref, outer_ref, inner_ref):
    count, skip = outer_ref.shape[0], keep_ref.shape[0] - inner_ref.shape[0]
    for k in range(keep_ref.shape[0]):
        total = keep_ref[k] + given_ref[k]
        if k < count:
            outer_ref[k] = total
        if k >= skip:
            inner_ref[k - skip] = total


def on_device(perturbed_states, control, owner, map_factor, terrain):
    _, fields, levels, rows, cols = perturbed_states.shape
    sizes = tuple(lax.axis_size(axis) for axis in AXES)
    members, along = sizes[0], sizes[2]
    half = rows // 2
    n_edges = fields // pack_of(fields, along)
    tile = (levels, cols)

    def tiles(count):
        return jax.ShapeDtypeStruct((count, *tile), jnp.float32)

    def room(count):
        return pltpu.VMEM((count, *tile), jnp.float32)

    flat = (fields, levels * rows, cols)
    states, keep, give, edge, side, metric = pl.pallas_call(
        functools.partial(split_kernel, sizes),
        out_shape=(
            tiles(rows * fields),
            tiles(half * fields),
            tiles(half * fields),
            tiles(n_edges),
            tiles(2 * n_edges + 1),
            jax.ShapeDtypeStruct((2 * rows, cols), jnp.float32),
        ),
        in_specs=[HBM] * 5,
        out_specs=(VMEM,) * 6,
        scratch_shapes=[
            pltpu.VMEM(flat, jnp.float32),
            pltpu.VMEM(flat, jnp.float32),
            pltpu.SMEM(owner.shape, jnp.int32),
            pltpu.VMEM((rows, cols), jnp.int32),
            pltpu.SemaphoreType.DMA((2 * fields + 3,)),
        ],
        compiler_params=MODEST,
        name="split",
    )(
        *(
            pltpu.with_memory_space_constraint(value, pltpu.HBM)
            for value in (
                perturbed_states.reshape(flat), control.reshape(flat), owner, map_factor, terrain
            )
        )
    )

    def over_members(value, bit):
        return send(value, lambda k, i, j: (k ^ bit, i, j))

    def over_chips(value):
        bit = 2
        while bit < members:
            value = value + over_members(value, bit)
            bit *= 2
        return value

    given = over_members(give, 1)
    def from_beside(value, step, bit):
        return send(value, lambda k, i, j: (k ^ bit, i, (j + step) % along))

    steps = (1, -1) if along > 2 else (1,)
    near = [from_beside(side, step, 0) for step in steps]
    edges = []
    for step, n in zip(steps, near):
        total = n[:n_edges]
        for bit in range(2, members, 2):
            total = total + from_beside(edge, step, bit)
        edges.append(total)
    edges = jnp.concatenate(edges, axis=0)
    cut = STEPS * fields
    outer, inner = pl.pallas_call(
        pair_kernel,
        out_shape=(tiles(cut), tiles(half * fields - cut + fields)),
        in_specs=[VMEM] * 2,
        out_specs=(VMEM,) * 2,
        compiler_params=MODEST,
        name="pair",
    )(keep, given)
    outer = over_chips(outer)
    inner = over_chips(inner)[fields:]

    other = over_members(jnp.concatenate([outer, edges], axis=0), 1)
    count = cut + (3 if along == 2 else fields + 2)
    start, beside, first, second = pl.pallas_call(
        functools.partial(join_kernel, sizes, len(near)),
        out_shape=(tiles(2 * cut), tiles(len(near) * (fields + 1)), tiles(count), tiles(count)),
        in_specs=[VMEM] * (6 + len(near)),
        out_specs=(VMEM,) * 4,
        compiler_params=MODEST,
        name="join",
    )(states, outer, edges, other, metric, side, *near)
    first_in = send(first, loop_target(sizes[1], True))
    second_in = send(second, loop_target(sizes[1], False))
    inner, _ = lax.optimization_barrier((inner, first))
    other = over_members(inner, 1)
    strips, saved, done = pl.pallas_call(
        functools.partial(middle_kernel, sizes),
        out_shape=(
            tiles(len(near) * (fields + 1)),
            tiles(4 * (STEPS - 1) * fields),
            tiles((rows - 2 * STEPS) * fields),
        ),
        in_specs=[VMEM] * 7,
        out_specs=(VMEM,) * 3,
        scratch_shapes=[room(rows * fields), room(rows * fields)],
        compiler_params=MODEST,
        cost_estimate=pl.CostEstimate(
            flops=30 * rows * fields * levels * cols * STEPS, bytes_accessed=2**20, transcendentals=0
        ),
        name="middle",
    )(states, start, inner, other, metric, side, beside)
    out = pl.pallas_call(
        functools.partial(outer_kernel, sizes),
        out_shape=jax.ShapeDtypeStruct((fields * levels, rows, cols), jnp.float32),
        in_specs=[VMEM] * 7,
        out_specs=HBM,
        scratch_shapes=[pltpu.VMEM(flat, jnp.float32), pltpu.SemaphoreType.DMA((2,))],
        compiler_params=MODEST,
        name="outer",
    )(start, strips, saved, done, metric, first_in, second_in)
    return out.reshape(perturbed_states.shape)


def solution(mesh):
    placed = (
        P("member", None, None, "dx", "dy"),
        P("member", None, None, "dx", "dy"),
        P(),
        P("dx", "dy"),
        P("dx", "dy"),
    )
    return jax.shard_map(
        on_device,
        mesh=mesh,
        in_specs=placed,
        out_specs=P("member", None, None, "dx", "dy"),
        check_vma=False,
    )
```

```python
import functools

import jax
import jax.numpy as jnp
from jax import lax
from jax.experimental import pallas as pl
from jax.experimental.pallas import tpu as pltpu
from jax.sharding import PartitionSpec as P

STEPS = 4

integration_step = 0.2
diffusion = 0.1

OUTSIDE = 1.0e6
AXES = ("member", "dx", "dy")
VMEM = pl.BlockSpec(memory_space=pltpu.VMEM)
HBM = pl.BlockSpec(memory_space=pltpu.HBM)
MODEST = pltpu.CompilerParams(vmem_limit_bytes=8 * 2**20)


def send(value, target):
    sizes = [lax.axis_size(axis) for axis in AXES]
    pairs = []
    for member in range(sizes[0]):
        for i in range(sizes[1]):
            for j in range(sizes[2]):
                k, l, m = target(member, i, j)
                pairs.append(
                    (
                        (member * sizes[1] + i) * sizes[2] + j,
                        (k * sizes[1] + l) * sizes[2] + m,
                    )
                )
    return lax.ppermute(value, AXES, pairs)


def loop_target(rows, forward):
    def target(member, i, j):
        step = 1 if (member % 2 == 0) == forward else -1
        if 0 <= i + step < rows:
            return member, i + step, j
        return member ^ 1, i, j

    return target


def lanes_of(shape):
    return lax.broadcasted_iota(jnp.int32, shape, len(shape) - 1)


def turn(tile, by, axis=1):
    size = tile.shape[axis]
    return pltpu.roll(tile, by % size if isinstance(by, int) else lax.rem(by + size, size), axis)


def edges_of(tiles, width):
    lane = lanes_of(tiles[0].shape)
    total = None
    for x, tile in enumerate(tiles):
        moved = turn(tile, 2 * width * x + width)
        total = moved if total is None else jnp.where(lane < 2 * width * x, total, moved)
    return total


def pack_of(fields, along):
    return 2 if along == 2 and fields % 2 == 0 else 1


def packed(edges, early, has_left, along):
    if pack_of(len(edges), along) == 1:
        return edges
    by = jnp.where(has_left, -STEPS, STEPS)
    return [
        jnp.where(early == has_left, turn(b, by), a) for a, b in zip(edges[::2], edges[1::2])
    ]


def unpacked(tiles, fields, has_left, along):
    if pack_of(fields, along) == 1:
        return tiles
    by = jnp.where(has_left, -STEPS, STEPS)
    return [part for tile in tiles for part in (tile, turn(tile, by))]


def split_kernel(
    sizes, p_hbm, c_hbm, owner_hbm, m_hbm, t_hbm,
    pt_ref, keep_ref, send_ref, edge_ref, side_ref, metric_ref,
    p_ref, c_ref, owner_ref, t_ref, sems,
):
    fields, _, cols = p_ref.shape
    rows = t_ref.shape[0]
    levels = p_ref.shape[1] // rows
    half = rows // 2
    member = lax.axis_index("member")
    members = owner_ref.shape[0]
    first = lax.rem(member, 2) == 0
    copies = [
        pltpu.make_async_copy(owner_hbm, owner_ref, sems.at[0]),
        pltpu.make_async_copy(m_hbm, metric_ref.at[pl.ds(0, rows), :], sems.at[1]),
        pltpu.make_async_copy(t_hbm, t_ref, sems.at[2]),
    ]
    together = 2 if fields % 2 == 0 else 1
    for n in range(fields // together):
        some = pl.ds(n * together, together)
        copies.append(pltpu.make_async_copy(p_hbm.at[some], p_ref.at[some], sems.at[3 + 2 * n]))
        copies.append(pltpu.make_async_copy(c_hbm.at[some], c_ref.at[some], sems.at[4 + 2 * n]))
    for copy in copies:
        copy.start()
    for copy in copies[:3]:
        copy.wait()
    metric_ref[pl.ds(rows, rows), :] = t_ref[...].astype(jnp.float32)
    level = lax.broadcasted_iota(jnp.int32, (levels, cols), 0)
    columns = []
    for x in range(rows):
        scale = jnp.broadcast_to(metric_ref[pl.ds(x, 1), :], (levels, cols))
        ground = jnp.broadcast_to(metric_ref[pl.ds(rows + x, 1), :], (levels, cols))
        columns.append(jnp.where(level == 0, scale, ground))
    side_ref[side_ref.shape[0] - 1] = edges_of(columns, STEPS)
    part_edges, state_edges = [], []
    weight = jnp.float32(0.0)
    for rank in range(members):
        per_rank = 2.0 * (members - rank) / (members * (members + 1.0))
        weight = weight + jnp.where(owner_ref[rank] == member, per_rank, 0.0)
    for f in range(fields):
        if f % together == 0:
            copies[3 + 2 * (f // together)].wait()
            copies[4 + 2 * (f // together)].wait()
        states, parts = [], []
        for x in range(rows):
            state = p_ref[f, pl.ds(x, levels, stride=rows), :]
            analysis = c_ref[f, pl.ds(x, levels, stride=rows), :]
            pt_ref[x * fields + f] = state
            states.append(state)
            parts.append(weight * analysis - state * (1.0 / members))
        for r in range(half):
            keep_ref[r * fields + f] = jnp.where(first, parts[r], parts[rows - 1 - r])
            send_ref[r * fields + f] = jnp.where(first, parts[rows - 1 - r], parts[r])
        part_edges.append(edges_of(parts, STEPS))
        state_edges.append(edges_of(states, STEPS))
    early = lax.rem(lanes_of((levels, cols)), 2 * STEPS) < STEPS
    has_left, _ = has_neighbours("dy", sizes[2])
    for k, edge in enumerate(packed(part_edges, early, has_left, sizes[2])):
        edge_ref[k] = edge
        side_ref[k] = edge
    for k, edge in enumerate(packed(state_edges, early, has_left, sizes[2])):
        side_ref[edge_ref.shape[0] + k] = edge


def has_neighbours(axis, size):
    place = lax.axis_index(axis)
    return place > 0, place < size - 1


def coefficients(level, scale, ground):
    scale = jnp.broadcast_to(scale, level.shape)
    ground = jnp.broadcast_to(ground, level.shape)
    mask = (level.astype(jnp.float32) >= ground).astype(jnp.float32)
    return (
        mask * (1.0 - 6.0 * integration_step * diffusion),
        mask * (integration_step * diffusion),
        mask * (scale * (0.5 * integration_step)),
    )


def updated(level, coefs, cur, dx, sx, dy, sy):
    levels = level.shape[0]
    new = []
    for f, here in enumerate(cur):
        advected = cur[0] * dx[f] + cur[1] * dy[f]
        if f == 0:
            advected = advected + dx[2]
        elif f == 1:
            advected = advected + dy[2]
        elif f == 2:
            advected = advected + (dx[0] + dy[1])
        upper = jnp.where(level < levels - 1, turn(here, -1, 0), 0.0)
        lower = jnp.where(level > 0, turn(here, 1, 0), 0.0)
        total = (sx[f] + sy[f]) + (upper + lower)
        new.append(coefs[0] * here + coefs[1] * total - coefs[2] * advected)
    return new


def row_step(level, lane, coefs, before, cur, after, beyond, spot):
    cols = lane.shape[1]
    dx, sx, dy, sy = [], [], [], []
    for f, here in enumerate(cur):
        outer = turn(beyond[f], -spot)
        north = jnp.where(lane == cols - 1, outer, turn(here, -1))
        south = jnp.where(lane == 0, outer, turn(here, 1))
        dx.append(after[f] - before[f])
        sx.append(after[f] + before[f])
        dy.append(north - south)
        sy.append(north + south)
    return updated(level, coefs, cur, dx, sx, dy, sy)


def strip_step(level, coefs, here, group):
    dx, sx, dy, sy = [], [], [], []
    for tile in here:
        east, west = turn(tile, -group), turn(tile, group)
        north, south = turn(tile, -1), turn(tile, 1)
        dx.append(east - west)
        sx.append(east + west)
        dy.append(north - south)
        sy.append(north + south)
    return updated(level, coefs, here, dx, sx, dy, sy)


def outside_columns(lane, width, strips, has_left):
    place = lax.rem(lane, 2 * width)
    if len(strips) == 2:
        return [jnp.where(place == width - 1, a, turn(b, -2)) for a, b in zip(*strips)]
    before = jnp.logical_and(place == width - 1, has_left)
    after = jnp.logical_and(place == width - 2, jnp.logical_not(has_left))
    return [jnp.where(before, a, jnp.where(after, turn(a, -2), 0.0)) for a in strips[0]]


def strips_of(early, own, beside, has_left):
    if len(beside) == 2:
        return [jnp.where(early, beside[0], own), jnp.where(early, own, beside[1])]
    return [jnp.where(early == has_left, beside[0], own)]


def metric_rows(metric_ref, wide, up):
    rows = metric_ref.shape[0] // 2
    scale, ground = metric_ref[pl.ds(0, rows), :], metric_ref[pl.ds(rows, rows), :]
    tops = jnp.concatenate([scale[rows - wide :], ground[rows - wide :]], axis=0)
    bottoms = jnp.concatenate([scale[:wide], ground[:wide]], axis=0)
    return jnp.where(up, tops, bottoms)


def besides(sizes, fields, near, edge_ref, other_ref, sides):
    has_left, has_right = has_neighbours("dy", sizes[2])
    per_side = edge_ref.shape[0] // sides
    by_side = []
    for side in range(sides):
        own, other = (
            [ref[side * per_side + k] for k in range(per_side)] for ref in (edge_ref, other_ref)
        )
        tiles = [near[side][per_side + k] + (own[k] + other[k]) for k in range(per_side)]
        tiles = unpacked(tiles, fields, has_left, sizes[2]) + [near[side][2 * per_side]]
        if sides == 2:
            here = (has_left, has_right)[side]
            empty = [0.0] * fields + [OUTSIDE]
            tiles = [jnp.where(here, tile, e) for tile, e in zip(tiles, empty)]
        by_side.append(tiles)
    return [list(pair) for pair in zip(*by_side)]


def ends_of(strips, up, quarter):
    lane = lanes_of(strips[0][0].shape)
    cols = lane.shape[1]
    fields = len(strips) - 1
    if len(strips[0]) == 1:
        packed = None
        for f in range(fields):
            moved = turn(strips[f][0], jnp.where(up, quarter, 0) + f * quarter)
            packed = moved if f == 0 else jnp.where(lane < f * quarter, packed, moved)
        return [packed, strips[fields][0]]
    return [
        jnp.where(
            lane < quarter,
            a,
            jnp.where(
                lane < 2 * quarter,
                turn(b, quarter),
                jnp.where(lane < cols - quarter, turn(b, -quarter), a),
            ),
        )
        for a, b in strips
    ]


def near_kernel(
    sizes, n_sides, pt_ref, sum_ref, metric_ref, edge_ref, other_ref, side_ref, *refs
):
    near, (message_ref,) = refs[:n_sides], refs[n_sides:]
    rows = metric_ref.shape[0] // 2
    fields = pt_ref.shape[0] // rows
    wide = STEPS
    even = lax.rem(lax.axis_index("member"), 2) == 0
    has_left, _ = has_neighbours("dy", sizes[2])
    lane = lanes_of(pt_ref.shape[1:])
    early = lax.rem(lane, 2 * wide) < wide
    values = besides(sizes, fields, near, edge_ref, other_ref, n_sides)
    strips = []
    for f in range(fields):
        own = None
        for r in range(wide):
            x = jnp.where(even, r, rows - 1 - r)
            place = jnp.where(even, r, wide - 1 - r) * fields
            tile = pt_ref[x * fields + f] + sum_ref[r * fields + f]
            message_ref[place + f] = tile
            moved = turn(tile, 2 * wide * x + wide)
            own = moved if own is None else jnp.where(lane // (2 * wide) == x, moved, own)
        strips.append(strips_of(early, own, values[f], has_left))
    strips.append(strips_of(early, side_ref[side_ref.shape[0] - 1], values[fields], has_left))
    up = jnp.logical_not(even)
    message_ref[wide * fields] = metric_rows(metric_ref, wide, up)
    for k, end in enumerate(ends_of(strips, up, 2 * wide * wide)):
        message_ref[wide * fields + 1 + k] = end


def join_kernel(
    sizes, n_sides, pt_ref, mine_ref, theirs_ref, edge_ref, other_ref, metric_ref, side_ref, *refs
):
    near, (start_ref, beside_ref, first_ref) = refs[:n_sides], refs[n_sides:]
    rows, cols = metric_ref.shape[0] // 2, metric_ref.shape[1]
    levels = pt_ref.shape[1]
    fields = pt_ref.shape[0] // rows
    wide = STEPS
    parity = lax.rem(lax.axis_index("member"), 2)
    has_left, has_right = has_neighbours("dy", sizes[2])
    lane = lanes_of((levels, cols))
    early = lax.rem(lane, 2 * wide) < wide
    quarter = 2 * wide * wide
    sides = beside_ref.shape[0] // (fields + 1)

    for r in range(wide):
        for f in range(fields):
            mine, other = mine_ref[r * fields + f], theirs_ref[r * fields + f]
            low, high = jnp.where(parity == 0, mine, other), jnp.where(parity == 0, other, mine)
            start_ref[r * fields + f] = pt_ref[r * fields + f] + low
            end = 2 * wide - 1 - r
            start_ref[end * fields + f] = pt_ref[(rows - 1 - r) * fields + f] + high

    strips = []
    values = besides(sizes, fields, near, edge_ref, other_ref, sides)
    for f, beside in enumerate(values):
        for side in range(sides):
            beside_ref[side * (fields + 1) + f] = beside[side]
        if f < fields:
            own = None
            for k in range(2 * wide):
                x = k if k < wide else rows - 2 * wide + k
                moved = turn(start_ref[k * fields + f], 2 * wide * x + wide)
                own = moved if own is None else jnp.where(lane < 2 * wide * x, own, moved)
        else:
            own = side_ref[side_ref.shape[0] - 1]
        strips.append(strips_of(early, own, beside, has_left))
    up = parity == 0
    base = jnp.where(up, wide, 0) * fields
    for k in range(wide * fields):
        first_ref[k] = start_ref[base + k]
    first_ref[wide * fields] = metric_rows(metric_ref, wide, up)
    for k, end in enumerate(ends_of(strips, up, quarter)):
        first_ref[wide * fields + 1 + k] = end


def middle_kernel(
    sizes, pt_ref, outer_ref, mine_ref, other_ref, metric_ref, side_ref, beside_ref,
    strip_ref, saved_ref, done_ref, a_ref, b_ref,
):
    rows, cols = metric_ref.shape[0] // 2, metric_ref.shape[1]
    levels = pt_ref.shape[1]
    fields = pt_ref.shape[0] // rows
    wide = STEPS
    group = 2 * wide
    half = rows // 2
    parity = lax.rem(lax.axis_index("member"), 2)
    lane = lanes_of((levels, cols))
    level = lax.broadcasted_iota(jnp.int32, (levels, cols), 0)
    early = lax.rem(lane, group) < wide
    for r in range(wide):
        for f in range(fields):
            a_ref[r * fields + f] = outer_ref[r * fields + f]
            a_ref[(rows - 1 - r) * fields + f] = outer_ref[(group - 1 - r) * fields + f]
    for r in range(wide, half):
        for f in range(fields):
            k = (r - wide) * fields + f
            mine, other = mine_ref[k], other_ref[k]
            low, high = jnp.where(parity == 0, mine, other), jnp.where(parity == 0, other, mine)
            a_ref[r * fields + f] = pt_ref[r * fields + f] + low
            mirrored = (rows - 1 - r) * fields + f
            a_ref[mirrored] = pt_ref[mirrored] + high
    has_left, _ = has_neighbours("dy", sizes[2])
    sides = beside_ref.shape[0] // (fields + 1)
    strips = [[] for _ in range(sides)]
    for f in range(fields + 1):
        if f < fields:
            own = edges_of([a_ref[x * fields + f] for x in range(rows)], wide)
        else:
            own = side_ref[side_ref.shape[0] - 1]
        beside = [beside_ref[side * (fields + 1) + f] for side in range(sides)]
        for side, strip in enumerate(strips_of(early, own, beside, has_left)):
            strips[side].append(strip)
            strip_ref[side * (fields + 1) + f] = strip
    strip_coefs = [coefficients(level, side[fields][0:1], side[fields][1:2]) for side in strips]
    strips = [side[:fields] for side in strips]
    coefs = [
        coefficients(level, metric_ref[pl.ds(x, 1), :], metric_ref[pl.ds(rows + x, 1), :])
        for x in range(rows)
    ]
    for number in range(STEPS):
        source, sink = (a_ref, b_ref) if number % 2 == 0 else (b_ref, a_ref)
        beyond = outside_columns(lane, wide, strips, has_left)
        bottom, top = number + 1, rows - 1 - number
        row = lambda x: [source[x * fields + f] for f in range(fields)]
        before, cur = row(bottom - 1), row(bottom)
        for x in range(bottom, top):
            after = row(x + 1)
            new = row_step(
                level, lane, coefs[x], before, cur, after, beyond, group * x + wide - 1
            )
            edge = {bottom: 0, bottom + 1: 1, top - 2: 2, top - 1: 3}.get(x)
            for f in range(fields):
                if number == STEPS - 1:
                    done_ref[(x - wide) * fields + f] = new[f]
                else:
                    sink[x * fields + f] = new[f]
                    if edge is not None:
                        saved_ref[(4 * number + edge) * fields + f] = new[f]
            before, cur = cur, after
        if number < STEPS - 1:
            strips = [
                strip_step(level, coef, tiles, group) for coef, tiles in zip(strip_coefs, strips)
            ]


def outer_kernel(
    sizes, outer_ref, strip_ref, saved_ref, done_ref, metric_ref, first_ref, second_ref,
    out_hbm, out_ref, sems,
):
    rows, cols = metric_ref.shape[0] // 2, metric_ref.shape[1]
    levels = outer_ref.shape[1]
    wide = STEPS
    group = 2 * wide
    fields = outer_ref.shape[0] // group
    half = rows // 2
    even = lax.rem(lax.axis_index("member"), 2) == 0
    has_low, has_high = has_neighbours("dx", sizes[1])
    lane = lanes_of((levels, cols))
    level = lax.broadcasted_iota(jnp.int32, (levels, cols), 0)
    quarter = group * wide

    def low(k, empty=0.0):
        return jnp.where(has_low, jnp.where(even, first_ref[k], second_ref[k]), empty)

    def high(k, empty=0.0):
        return jnp.where(has_high, jnp.where(even, second_ref[k], first_ref[k]), empty)

    has_left, _ = has_neighbours("dy", sizes[2])
    sides = strip_ref.shape[0] // (fields + 1)

    def stretched(is_low, side, f):
        mine = strip_ref[side * (fields + 1) + f]
        empty = 0.0 if f < fields else OUTSIDE
        if sides == 1 and f < fields:
            k, by = 0, (-f if is_low else -1 - f)
        else:
            k, by = min(f, 1) if sides == 1 else f, ((1, 2) if is_low else (-1, 2))[side]
        theirs = turn((low if is_low else high)(wide * fields + 1 + k, empty), by * quarter)
        if is_low:
            return jnp.where(lane < quarter, theirs, turn(mine, quarter))
        return jnp.where(lane < cols - quarter, turn(mine, -quarter), theirs)

    beyond = {}
    for is_low in (True, False):
        strips = [[stretched(is_low, side, f) for f in range(fields + 1)] for side in range(sides)]
        coefs = [coefficients(level, side[fields][0:1], side[fields][1:2]) for side in strips]
        strips = [side[:fields] for side in strips]
        for number in range(STEPS):
            beyond[is_low, number] = outside_columns(lane, wide, strips, has_left)
            if number < STEPS - 1:
                strips = [strip_step(level, c, tiles, group) for c, tiles in zip(coefs, strips)]

    for x in range(wide, rows - wide):
        for f in range(fields):
            out_ref[f, pl.ds(x, levels, stride=rows), :] = done_ref[(x - wide) * fields + f]

    def saved(number, edge):
        return [saved_ref[(4 * (number - 1) + edge) * fields + f] for f in range(fields)]

    def prepare(is_low):
        metric = wide * fields
        halo = low(metric, OUTSIDE) if is_low else high(metric, OUTSIDE)
        coefs, state = {}, {}
        for r in range(wide):
            message = [(low if is_low else high)(r * fields + f) for f in range(fields)]
            state[r - wide if is_low else rows + r] = message
            coefs[r - wide if is_low else rows + r] = coefficients(
                level, halo[r : r + 1], halo[wide + r : wide + r + 1]
            )
            x = r if is_low else rows - wide + r
            k = r if is_low else wide + r
            state[x] = [outer_ref[k * fields + f] for f in range(fields)]
            coefs[x] = coefficients(
                level, metric_ref[pl.ds(x, 1), :], metric_ref[pl.ds(rows + x, 1), :]
            )
        return state, coefs

    def advanced(is_low, number, state, coefs):
        if number > 0:
            if is_low:
                state[number], state[number + 1] = saved(number, 0), saved(number, 1)
            else:
                state[rows - 2 - number], state[rows - 1 - number] = saved(number, 2), saved(number, 3)
        bottom = number + 1 - wide if is_low else rows - 1 - number
        new = {}
        for x in range(bottom, bottom + wide):
            spot = group * (x + (wide if is_low else -wide)) + wide - 1
            new[x] = row_step(
                level, lane, coefs[x], state[x - 1], state[x], state[x + 1],
                beyond[is_low, number], spot,
            )
        return new

    parts = {is_low: prepare(is_low) for is_low in (True, False)}
    for number in range(STEPS):
        for is_low, (state, coefs) in parts.items():
            parts[is_low] = advanced(is_low, number, state, coefs), coefs
    for state, _ in parts.values():
        for x, tiles in state.items():
            for f in range(fields):
                out_ref[f, pl.ds(x, levels, stride=rows), :] = tiles[f]

    copies = []
    for n, is_low in enumerate((True, False)):
        part = pl.ds(n * half, half)
        source = out_ref.reshape(fields * levels, rows, cols)
        copies.append(
            pltpu.make_async_copy(source.at[:, part, :], out_hbm.at[:, part, :], sems.at[n])
        )
        copies[-1].start()
    for copy in copies:
        copy.wait()


def pair_kernel(keep_ref, given_ref, outer_ref, inner_ref):
    count, skip = outer_ref.shape[0], keep_ref.shape[0] - inner_ref.shape[0]
    for k in range(keep_ref.shape[0]):
        total = keep_ref[k] + given_ref[k]
        if k < count:
            outer_ref[k] = total
        if k >= skip:
            inner_ref[k - skip] = total


def on_device(perturbed_states, control, owner, map_factor, terrain):
    _, fields, levels, rows, cols = perturbed_states.shape
    sizes = tuple(lax.axis_size(axis) for axis in AXES)
    members, along = sizes[0], sizes[2]
    half = rows // 2
    n_edges = fields // pack_of(fields, along)
    tile = (levels, cols)

    def tiles(count):
        return jax.ShapeDtypeStruct((count, *tile), jnp.float32)

    def room(count):
        return pltpu.VMEM((count, *tile), jnp.float32)

    flat = (fields, levels * rows, cols)
    states, keep, give, edge, side, metric = pl.pallas_call(
        functools.partial(split_kernel, sizes),
        out_shape=(
            tiles(rows * fields),
            tiles(half * fields),
            tiles(half * fields),
            tiles(n_edges),
            tiles(2 * n_edges + 1),
            jax.ShapeDtypeStruct((2 * rows, cols), jnp.float32),
        ),
        in_specs=[HBM] * 5,
        out_specs=(VMEM,) * 6,
        scratch_shapes=[
            pltpu.VMEM(flat, jnp.float32),
            pltpu.VMEM(flat, jnp.float32),
            pltpu.SMEM(owner.shape, jnp.int32),
            pltpu.VMEM((rows, cols), jnp.int32),
            pltpu.SemaphoreType.DMA((2 * fields + 3,)),
        ],
        compiler_params=MODEST,
        name="split",
    )(
        *(
            pltpu.with_memory_space_constraint(value, pltpu.HBM)
            for value in (
                perturbed_states.reshape(flat), control.reshape(flat), owner, map_factor, terrain
            )
        )
    )

    def over_members(value, bit):
        return send(value, lambda k, i, j: (k ^ bit, i, j))

    def over_chips(value):
        bit = 2
        while bit < members:
            value = value + over_members(value, bit)
            bit *= 2
        return value

    given = over_members(give, 1)
    def from_beside(value, step, bit):
        return send(value, lambda k, i, j: (k ^ bit, i, (j + step) % along))

    steps = (1, -1) if along > 2 else (1,)
    near = [from_beside(side, step, 0) for step in steps]
    edges = []
    for step, n in zip(steps, near):
        total = n[:n_edges]
        for bit in range(2, members, 2):
            total = total + from_beside(edge, step, bit)
        edges.append(total)
    edges = jnp.concatenate(edges, axis=0)
    cut = STEPS * fields
    outer, inner = pl.pallas_call(
        pair_kernel,
        out_shape=(tiles(cut), tiles(half * fields - cut + 1)),
        in_specs=[VMEM] * 2,
        out_specs=(VMEM,) * 2,
        compiler_params=MODEST,
        name="pair",
    )(keep, given)
    outer = over_chips(outer)
    inner = over_chips(inner)[1:]

    other_edges = over_members(edges, 1)
    outer, other_edges = lax.optimization_barrier((outer, other_edges))
    n_ends = 2 if along == 2 else fields + 1
    message = pl.pallas_call(
        functools.partial(near_kernel, sizes, len(near)),
        out_shape=tiles(cut + 1 + n_ends),
        in_specs=[VMEM] * (6 + len(near)),
        out_specs=VMEM,
        compiler_params=MODEST,
        name="near",
    )(states, outer, metric, edges, other_edges, side, *near)
    second_in = send(message, loop_target(sizes[1], False))
    other = over_members(outer, 1)
    start, beside, first = pl.pallas_call(
        functools.partial(join_kernel, sizes, len(near)),
        out_shape=(tiles(2 * cut), tiles(len(near) * (fields + 1)), tiles(cut + 1 + n_ends)),
        in_specs=[VMEM] * (7 + len(near)),
        out_specs=(VMEM,) * 3,
        compiler_params=MODEST,
        name="join",
    )(states, outer, other, edges, other_edges, metric, side, *near)
    first_in = send(first, loop_target(sizes[1], True))
    inner, _ = lax.optimization_barrier((inner, first))
    other = over_members(inner, 1)
    strips, saved, done = pl.pallas_call(
        functools.partial(middle_kernel, sizes),
        out_shape=(
            tiles(len(near) * (fields + 1)),
            tiles(4 * (STEPS - 1) * fields),
            tiles((rows - 2 * STEPS) * fields),
        ),
        in_specs=[VMEM] * 7,
        out_specs=(VMEM,) * 3,
        scratch_shapes=[room(rows * fields), room(rows * fields)],
        compiler_params=MODEST,
        cost_estimate=pl.CostEstimate(
            flops=30 * rows * fields * levels * cols * STEPS, bytes_accessed=2**20, transcendentals=0
        ),
        name="middle",
    )(states, start, inner, other, metric, side, beside)
    out = pl.pallas_call(
        functools.partial(outer_kernel, sizes),
        out_shape=jax.ShapeDtypeStruct((fields * levels, rows, cols), jnp.float32),
        in_specs=[VMEM] * 7,
        out_specs=HBM,
        scratch_shapes=[pltpu.VMEM(flat, jnp.float32), pltpu.SemaphoreType.DMA((2,))],
        compiler_params=MODEST,
        name="outer",
    )(start, strips, saved, done, metric, first_in, second_in)
    return out.reshape(perturbed_states.shape)


def solution(mesh):
    placed = (
        P("member", None, None, "dx", "dy"),
        P("member", None, None, "dx", "dy"),
        P(),
        P("dx", "dy"),
        P("dx", "dy"),
    )
    return jax.shard_map(
        on_device,
        mesh=mesh,
        in_specs=placed,
        out_specs=P("member", None, None, "dx", "dy"),
        check_vma=False,
    )
```

```python
import functools

import jax
import jax.numpy as jnp
from jax import lax
from jax.experimental import pallas as pl
from jax.experimental.pallas import tpu as pltpu
from jax.sharding import PartitionSpec as P

STEPS = 4

integration_step = 0.2
diffusion = 0.1

OUTSIDE = 1.0e6
AXES = ("member", "dx", "dy")
VMEM = pl.BlockSpec(memory_space=pltpu.VMEM)
HBM = pl.BlockSpec(memory_space=pltpu.HBM)
MODEST = pltpu.CompilerParams(vmem_limit_bytes=8 * 2**20)


def send(value, target):
    sizes = [lax.axis_size(axis) for axis in AXES]
    pairs = []
    for member in range(sizes[0]):
        for i in range(sizes[1]):
            for j in range(sizes[2]):
                k, l, m = target(member, i, j)
                pairs.append(
                    (
                        (member * sizes[1] + i) * sizes[2] + j,
                        (k * sizes[1] + l) * sizes[2] + m,
                    )
                )
    return lax.ppermute(value, AXES, pairs)


def loop_target(rows, forward):
    def target(member, i, j):
        step = 1 if (member % 2 == 0) == forward else -1
        if 0 <= i + step < rows:
            return member, i + step, j
        return member ^ 1, i, j

    return target


def lanes_of(shape):
    return lax.broadcasted_iota(jnp.int32, shape, len(shape) - 1)


def turn(tile, by, axis=1):
    size = tile.shape[axis]
    return pltpu.roll(tile, by % size if isinstance(by, int) else lax.rem(by + size, size), axis)


def edges_of(tiles, width):
    lane = lanes_of(tiles[0].shape)
    total = None
    for x, tile in enumerate(tiles):
        moved = turn(tile, 2 * width * x + width)
        total = moved if total is None else jnp.where(lane < 2 * width * x, total, moved)
    return total


def pack_of(fields, along):
    return 2 if along == 2 and fields % 2 == 0 else 1


def packed(edges, early, has_left, along):
    if pack_of(len(edges), along) == 1:
        return edges
    by = jnp.where(has_left, -STEPS, STEPS)
    return [
        jnp.where(early == has_left, turn(b, by), a) for a, b in zip(edges[::2], edges[1::2])
    ]


def unpacked(tiles, fields, has_left, along):
    if pack_of(fields, along) == 1:
        return tiles
    by = jnp.where(has_left, -STEPS, STEPS)
    return [part for tile in tiles for part in (tile, turn(tile, by))]


def split_kernel(
    sizes, p_hbm, c_hbm, owner_hbm, m_hbm, t_hbm,
    pt_ref, keep_ref, send_ref, edge_ref, side_ref, metric_ref,
    p_ref, c_ref, owner_ref, t_ref, sems,
):
    fields, _, cols = p_ref.shape
    rows = t_ref.shape[0]
    levels = p_ref.shape[1] // rows
    half = rows // 2
    member = lax.axis_index("member")
    members = owner_ref.shape[0]
    first = lax.rem(member, 2) == 0
    copies = [
        pltpu.make_async_copy(owner_hbm, owner_ref, sems.at[0]),
        pltpu.make_async_copy(m_hbm, metric_ref.at[pl.ds(0, rows), :], sems.at[1]),
        pltpu.make_async_copy(t_hbm, t_ref, sems.at[2]),
    ]
    together = 2 if fields % 2 == 0 else 1
    for n in range(fields // together):
        some = pl.ds(n * together, together)
        copies.append(pltpu.make_async_copy(p_hbm.at[some], p_ref.at[some], sems.at[3 + 2 * n]))
        copies.append(pltpu.make_async_copy(c_hbm.at[some], c_ref.at[some], sems.at[4 + 2 * n]))
    for copy in copies:
        copy.start()
    for copy in copies[:3]:
        copy.wait()
    metric_ref[pl.ds(rows, rows), :] = t_ref[...].astype(jnp.float32)
    level = lax.broadcasted_iota(jnp.int32, (levels, cols), 0)
    columns = []
    for x in range(rows):
        scale = jnp.broadcast_to(metric_ref[pl.ds(x, 1), :], (levels, cols))
        ground = jnp.broadcast_to(metric_ref[pl.ds(rows + x, 1), :], (levels, cols))
        columns.append(jnp.where(level == 0, scale, ground))
    side_ref[side_ref.shape[0] - 1] = edges_of(columns, STEPS)
    part_edges, state_edges = [], []
    weight = jnp.float32(0.0)
    for rank in range(members):
        per_rank = 2.0 * (members - rank) / (members * (members + 1.0))
        weight = weight + jnp.where(owner_ref[rank] == member, per_rank, 0.0)
    for f in range(fields):
        if f % together == 0:
            copies[3 + 2 * (f // together)].wait()
            copies[4 + 2 * (f // together)].wait()
        states, parts = [], []
        for x in range(rows):
            state = p_ref[f, pl.ds(x, levels, stride=rows), :]
            analysis = c_ref[f, pl.ds(x, levels, stride=rows), :]
            pt_ref[x * fields + f] = state
            states.append(state)
            parts.append(weight * analysis - state * (1.0 / members))
        for r in range(half):
            keep_ref[r * fields + f] = jnp.where(first, parts[r], parts[rows - 1 - r])
            send_ref[r * fields + f] = jnp.where(first, parts[rows - 1 - r], parts[r])
        part_edges.append(edges_of(parts, STEPS))
        state_edges.append(edges_of(states, STEPS))
    early = lax.rem(lanes_of((levels, cols)), 2 * STEPS) < STEPS
    has_left, _ = has_neighbours("dy", sizes[2])
    for k, edge in enumerate(packed(part_edges, early, has_left, sizes[2])):
        edge_ref[k] = edge
        side_ref[k] = edge
    for k, edge in enumerate(packed(state_edges, early, has_left, sizes[2])):
        side_ref[edge_ref.shape[0] + k] = edge


def has_neighbours(axis, size):
    place = lax.axis_index(axis)
    return place > 0, place < size - 1


def coefficients(level, scale, ground):
    scale = jnp.broadcast_to(scale, level.shape)
    ground = jnp.broadcast_to(ground, level.shape)
    mask = (level.astype(jnp.float32) >= ground).astype(jnp.float32)
    return (
        mask * (1.0 - 6.0 * integration_step * diffusion),
        mask * (integration_step * diffusion),
        mask * (scale * (0.5 * integration_step)),
    )


def updated(level, coefs, cur, dx, sx, dy, sy):
    levels = level.shape[0]
    new = []
    for f, here in enumerate(cur):
        advected = cur[0] * dx[f] + cur[1] * dy[f]
        if f == 0:
            advected = advected + dx[2]
        elif f == 1:
            advected = advected + dy[2]
        elif f == 2:
            advected = advected + (dx[0] + dy[1])
        upper = jnp.where(level < levels - 1, turn(here, -1, 0), 0.0)
        lower = jnp.where(level > 0, turn(here, 1, 0), 0.0)
        total = (sx[f] + sy[f]) + (upper + lower)
        new.append(coefs[0] * here + coefs[1] * total - coefs[2] * advected)
    return new


def row_step(level, lane, coefs, before, cur, after, beyond, spot):
    cols = lane.shape[1]
    dx, sx, dy, sy = [], [], [], []
    for f, here in enumerate(cur):
        outer = turn(beyond[f], -spot)
        north = jnp.where(lane == cols - 1, outer, turn(here, -1))
        south = jnp.where(lane == 0, outer, turn(here, 1))
        dx.append(after[f] - before[f])
        sx.append(after[f] + before[f])
        dy.append(north - south)
        sy.append(north + south)
    return updated(level, coefs, cur, dx, sx, dy, sy)


def strip_step(level, coefs, here, group):
    dx, sx, dy, sy = [], [], [], []
    for tile in here:
        east, west = turn(tile, -group), turn(tile, group)
        north, south = turn(tile, -1), turn(tile, 1)
        dx.append(east - west)
        sx.append(east + west)
        dy.append(north - south)
        sy.append(north + south)
    return updated(level, coefs, here, dx, sx, dy, sy)


def outside_columns(lane, width, strips, has_left):
    place = lax.rem(lane, 2 * width)
    if len(strips) == 2:
        return [jnp.where(place == width - 1, a, turn(b, -2)) for a, b in zip(*strips)]
    before = jnp.logical_and(place == width - 1, has_left)
    after = jnp.logical_and(place == width - 2, jnp.logical_not(has_left))
    return [jnp.where(before, a, jnp.where(after, turn(a, -2), 0.0)) for a in strips[0]]


def strips_of(early, own, beside, has_left):
    if len(beside) == 2:
        return [jnp.where(early, beside[0], own), jnp.where(early, own, beside[1])]
    return [jnp.where(early == has_left, beside[0], own)]


def metric_rows(metric_ref, wide, up):
    rows = metric_ref.shape[0] // 2
    scale, ground = metric_ref[pl.ds(0, rows), :], metric_ref[pl.ds(rows, rows), :]
    tops = jnp.concatenate([scale[rows - wide :], ground[rows - wide :]], axis=0)
    bottoms = jnp.concatenate([scale[:wide], ground[:wide]], axis=0)
    return jnp.where(up, tops, bottoms)


def besides(sizes, fields, near, edge_ref, other_ref, sides):
    has_left, has_right = has_neighbours("dy", sizes[2])
    per_side = edge_ref.shape[0] // sides
    by_side = []
    for side in range(sides):
        own, other = (
            [ref[side * per_side + k] for k in range(per_side)] for ref in (edge_ref, other_ref)
        )
        tiles = [near[side][per_side + k] + (own[k] + other[k]) for k in range(per_side)]
        tiles = unpacked(tiles, fields, has_left, sizes[2]) + [near[side][2 * per_side]]
        if sides == 2:
            here = (has_left, has_right)[side]
            empty = [0.0] * fields + [OUTSIDE]
            tiles = [jnp.where(here, tile, e) for tile, e in zip(tiles, empty)]
        by_side.append(tiles)
    return [list(pair) for pair in zip(*by_side)]


def ends_of(strips, up, quarter):
    lane = lanes_of(strips[0][0].shape)
    cols = lane.shape[1]
    fields = len(strips) - 1
    if len(strips[0]) == 1:
        packed = None
        for f in range(fields):
            moved = turn(strips[f][0], jnp.where(up, quarter, 0) + f * quarter)
            packed = moved if f == 0 else jnp.where(lane < f * quarter, packed, moved)
        return [packed, strips[fields][0]]
    return [
        jnp.where(
            lane < quarter,
            a,
            jnp.where(
                lane < 2 * quarter,
                turn(b, quarter),
                jnp.where(lane < cols - quarter, turn(b, -quarter), a),
            ),
        )
        for a, b in strips
    ]


def near_kernel(
    sizes, n_sides, pt_ref, sum_ref, metric_ref, edge_ref, other_ref, side_ref, *refs
):
    near, (message_ref,) = refs[:n_sides], refs[n_sides:]
    rows = metric_ref.shape[0] // 2
    fields = pt_ref.shape[0] // rows
    wide = STEPS
    even = lax.rem(lax.axis_index("member"), 2) == 0
    has_left, _ = has_neighbours("dy", sizes[2])
    lane = lanes_of(pt_ref.shape[1:])
    early = lax.rem(lane, 2 * wide) < wide
    values = besides(sizes, fields, near, edge_ref, other_ref, n_sides)
    strips = []
    for f in range(fields):
        own = None
        for r in range(wide):
            x = jnp.where(even, r, rows - 1 - r)
            place = jnp.where(even, r, wide - 1 - r) * fields
            tile = pt_ref[x * fields + f] + sum_ref[r * fields + f]
            message_ref[place + f] = tile
            moved = turn(tile, 2 * wide * x + wide)
            own = moved if own is None else jnp.where(lane // (2 * wide) == x, moved, own)
        strips.append(strips_of(early, own, values[f], has_left))
    strips.append(strips_of(early, side_ref[side_ref.shape[0] - 1], values[fields], has_left))
    up = jnp.logical_not(even)
    message_ref[wide * fields] = metric_rows(metric_ref, wide, up)
    for k, end in enumerate(ends_of(strips, up, 2 * wide * wide)):
        message_ref[wide * fields + 1 + k] = end


def join_kernel(
    sizes, n_sides, pt_ref, mine_ref, theirs_ref, edge_ref, other_ref, metric_ref, side_ref, *refs
):
    near, (start_ref, beside_ref, first_ref) = refs[:n_sides], refs[n_sides:]
    rows, cols = metric_ref.shape[0] // 2, metric_ref.shape[1]
    levels = pt_ref.shape[1]
    fields = pt_ref.shape[0] // rows
    wide = STEPS
    parity = lax.rem(lax.axis_index("member"), 2)
    has_left, has_right = has_neighbours("dy", sizes[2])
    lane = lanes_of((levels, cols))
    early = lax.rem(lane, 2 * wide) < wide
    quarter = 2 * wide * wide
    sides = beside_ref.shape[0] // (fields + 1)

    for r in range(wide):
        for f in range(fields):
            mine, other = mine_ref[r * fields + f], theirs_ref[r * fields + f]
            low, high = jnp.where(parity == 0, mine, other), jnp.where(parity == 0, other, mine)
            start_ref[r * fields + f] = pt_ref[r * fields + f] + low
            end = 2 * wide - 1 - r
            start_ref[end * fields + f] = pt_ref[(rows - 1 - r) * fields + f] + high

    strips = []
    values = besides(sizes, fields, near, edge_ref, other_ref, sides)
    for f, beside in enumerate(values):
        for side in range(sides):
            beside_ref[side * (fields + 1) + f] = beside[side]
        if f < fields:
            own = None
            for k in range(2 * wide):
                x = k if k < wide else rows - 2 * wide + k
                moved = turn(start_ref[k * fields + f], 2 * wide * x + wide)
                own = moved if own is None else jnp.where(lane < 2 * wide * x, own, moved)
        else:
            own = side_ref[side_ref.shape[0] - 1]
        strips.append(strips_of(early, own, beside, has_left))
    up = parity == 0
    base = jnp.where(up, wide, 0) * fields
    for k in range(wide * fields):
        first_ref[k] = start_ref[base + k]
    first_ref[wide * fields] = metric_rows(metric_ref, wide, up)
    for k, end in enumerate(ends_of(strips, up, quarter)):
        first_ref[wide * fields + 1 + k] = end


def middle_kernel(
    sizes, pt_ref, outer_ref, mine_ref, other_ref, metric_ref, side_ref, beside_ref,
    strip_ref, saved_ref, done_ref, a_ref, b_ref,
):
    rows, cols = metric_ref.shape[0] // 2, metric_ref.shape[1]
    levels = pt_ref.shape[1]
    fields = pt_ref.shape[0] // rows
    wide = STEPS
    group = 2 * wide
    half = rows // 2
    parity = lax.rem(lax.axis_index("member"), 2)
    lane = lanes_of((levels, cols))
    level = lax.broadcasted_iota(jnp.int32, (levels, cols), 0)
    early = lax.rem(lane, group) < wide
    for r in range(wide):
        for f in range(fields):
            a_ref[r * fields + f] = outer_ref[r * fields + f]
            a_ref[(rows - 1 - r) * fields + f] = outer_ref[(group - 1 - r) * fields + f]
    for r in range(wide, half):
        for f in range(fields):
            k = (r - wide) * fields + f
            mine, other = mine_ref[k], other_ref[k]
            low, high = jnp.where(parity == 0, mine, other), jnp.where(parity == 0, other, mine)
            a_ref[r * fields + f] = pt_ref[r * fields + f] + low
            mirrored = (rows - 1 - r) * fields + f
            a_ref[mirrored] = pt_ref[mirrored] + high
    has_left, _ = has_neighbours("dy", sizes[2])
    sides = beside_ref.shape[0] // (fields + 1)
    strips = [[] for _ in range(sides)]
    for f in range(fields + 1):
        if f < fields:
            own = edges_of([a_ref[x * fields + f] for x in range(rows)], wide)
        else:
            own = side_ref[side_ref.shape[0] - 1]
        beside = [beside_ref[side * (fields + 1) + f] for side in range(sides)]
        for side, strip in enumerate(strips_of(early, own, beside, has_left)):
            strips[side].append(strip)
            strip_ref[side * (fields + 1) + f] = strip
    strip_coefs = [coefficients(level, side[fields][0:1], side[fields][1:2]) for side in strips]
    strips = [side[:fields] for side in strips]
    coefs = [
        coefficients(level, metric_ref[pl.ds(x, 1), :], metric_ref[pl.ds(rows + x, 1), :])
        for x in range(rows)
    ]
    for number in range(STEPS):
        source, sink = (a_ref, b_ref) if number % 2 == 0 else (b_ref, a_ref)
        beyond = outside_columns(lane, wide, strips, has_left)
        bottom, top = number + 1, rows - 1 - number
        row = lambda x: [source[x * fields + f] for f in range(fields)]
        before, cur = row(bottom - 1), row(bottom)
        for x in range(bottom, top):
            after = row(x + 1)
            new = row_step(
                level, lane, coefs[x], before, cur, after, beyond, group * x + wide - 1
            )
            edge = {bottom: 0, bottom + 1: 1, top - 2: 2, top - 1: 3}.get(x)
            for f in range(fields):
                if number == STEPS - 1:
                    done_ref[(x - wide) * fields + f] = new[f]
                else:
                    sink[x * fields + f] = new[f]
                    if edge is not None:
                        saved_ref[(4 * number + edge) * fields + f] = new[f]
            before, cur = cur, after
        if number < STEPS - 1:
            strips = [
                strip_step(level, coef, tiles, group) for coef, tiles in zip(strip_coefs, strips)
            ]


def outer_kernel(
    sizes, outer_ref, strip_ref, saved_ref, done_ref, metric_ref, first_ref, second_ref,
    out_hbm, out_ref, sems,
):
    rows, cols = metric_ref.shape[0] // 2, metric_ref.shape[1]
    levels = outer_ref.shape[1]
    wide = STEPS
    group = 2 * wide
    fields = outer_ref.shape[0] // group
    half = rows // 2
    even = lax.rem(lax.axis_index("member"), 2) == 0
    has_low, has_high = has_neighbours("dx", sizes[1])
    lane = lanes_of((levels, cols))
    level = lax.broadcasted_iota(jnp.int32, (levels, cols), 0)
    quarter = group * wide

    def low(k, empty=0.0):
        return jnp.where(has_low, jnp.where(even, first_ref[k], second_ref[k]), empty)

    def high(k, empty=0.0):
        return jnp.where(has_high, jnp.where(even, second_ref[k], first_ref[k]), empty)

    has_left, _ = has_neighbours("dy", sizes[2])
    sides = strip_ref.shape[0] // (fields + 1)

    def stretched(is_low, side, f):
        mine = strip_ref[side * (fields + 1) + f]
        empty = 0.0 if f < fields else OUTSIDE
        if sides == 1 and f < fields:
            k, by = 0, (-f if is_low else -1 - f)
        else:
            k, by = min(f, 1) if sides == 1 else f, ((1, 2) if is_low else (-1, 2))[side]
        theirs = turn((low if is_low else high)(wide * fields + 1 + k, empty), by * quarter)
        if is_low:
            return jnp.where(lane < quarter, theirs, turn(mine, quarter))
        return jnp.where(lane < cols - quarter, turn(mine, -quarter), theirs)

    beyond = {}
    for is_low in (True, False):
        strips = [[stretched(is_low, side, f) for f in range(fields + 1)] for side in range(sides)]
        coefs = [coefficients(level, side[fields][0:1], side[fields][1:2]) for side in strips]
        strips = [side[:fields] for side in strips]
        for number in range(STEPS):
            beyond[is_low, number] = outside_columns(lane, wide, strips, has_left)
            if number < STEPS - 1:
                strips = [strip_step(level, c, tiles, group) for c, tiles in zip(coefs, strips)]

    for x in range(wide, rows - wide):
        for f in range(fields):
            out_ref[f, pl.ds(x, levels, stride=rows), :] = done_ref[(x - wide) * fields + f]

    def saved(number, edge):
        return [saved_ref[(4 * (number - 1) + edge) * fields + f] for f in range(fields)]

    def prepare(is_low):
        metric = wide * fields
        halo = low(metric, OUTSIDE) if is_low else high(metric, OUTSIDE)
        coefs, state = {}, {}
        for r in range(wide):
            message = [(low if is_low else high)(r * fields + f) for f in range(fields)]
            state[r - wide if is_low else rows + r] = message
            coefs[r - wide if is_low else rows + r] = coefficients(
                level, halo[r : r + 1], halo[wide + r : wide + r + 1]
            )
            x = r if is_low else rows - wide + r
            k = r if is_low else wide + r
            state[x] = [outer_ref[k * fields + f] for f in range(fields)]
            coefs[x] = coefficients(
                level, metric_ref[pl.ds(x, 1), :], metric_ref[pl.ds(rows + x, 1), :]
            )
        return state, coefs

    def advanced(is_low, number, state, coefs):
        if number > 0:
            if is_low:
                state[number], state[number + 1] = saved(number, 0), saved(number, 1)
            else:
                state[rows - 2 - number], state[rows - 1 - number] = saved(number, 2), saved(number, 3)
        bottom = number + 1 - wide if is_low else rows - 1 - number
        new = {}
        for x in range(bottom, bottom + wide):
            spot = group * (x + (wide if is_low else -wide)) + wide - 1
            new[x] = row_step(
                level, lane, coefs[x], state[x - 1], state[x], state[x + 1],
                beyond[is_low, number], spot,
            )
        return new

    parts = {is_low: prepare(is_low) for is_low in (True, False)}
    for number in range(STEPS):
        for is_low, (state, coefs) in parts.items():
            parts[is_low] = advanced(is_low, number, state, coefs), coefs
    for state, _ in parts.values():
        for x, tiles in state.items():
            for f in range(fields):
                out_ref[f, pl.ds(x, levels, stride=rows), :] = tiles[f]

    copies = []
    for n, is_low in enumerate((True, False)):
        part = pl.ds(n * half, half)
        source = out_ref.reshape(fields * levels, rows, cols)
        copies.append(
            pltpu.make_async_copy(source.at[:, part, :], out_hbm.at[:, part, :], sems.at[n])
        )
        copies[-1].start()
    for copy in copies:
        copy.wait()


def pair_kernel(keep_ref, given_ref, outer_ref, inner_ref):
    count, skip = outer_ref.shape[0], keep_ref.shape[0] - inner_ref.shape[0]
    for k in range(keep_ref.shape[0]):
        total = keep_ref[k] + given_ref[k]
        if k < count:
            outer_ref[k] = total
        if k >= skip:
            inner_ref[k - skip] = total


def on_device(perturbed_states, control, owner, map_factor, terrain):
    _, fields, levels, rows, cols = perturbed_states.shape
    sizes = tuple(lax.axis_size(axis) for axis in AXES)
    members, along = sizes[0], sizes[2]
    half = rows // 2
    n_edges = fields // pack_of(fields, along)
    tile = (levels, cols)

    def tiles(count):
        return jax.ShapeDtypeStruct((count, *tile), jnp.float32)

    def room(count):
        return pltpu.VMEM((count, *tile), jnp.float32)

    flat = (fields, levels * rows, cols)
    states, keep, give, edge, side, metric = pl.pallas_call(
        functools.partial(split_kernel, sizes),
        out_shape=(
            tiles(rows * fields),
            tiles(half * fields),
            tiles(half * fields),
            tiles(n_edges),
            tiles(2 * n_edges + 1),
            jax.ShapeDtypeStruct((2 * rows, cols), jnp.float32),
        ),
        in_specs=[HBM] * 5,
        out_specs=(VMEM,) * 6,
        scratch_shapes=[
            pltpu.VMEM(flat, jnp.float32),
            pltpu.VMEM(flat, jnp.float32),
            pltpu.SMEM(owner.shape, jnp.int32),
            pltpu.VMEM((rows, cols), jnp.int32),
            pltpu.SemaphoreType.DMA((2 * fields + 3,)),
        ],
        compiler_params=MODEST,
        name="split",
    )(
        *(
            pltpu.with_memory_space_constraint(value, pltpu.HBM)
            for value in (
                perturbed_states.reshape(flat), control.reshape(flat), owner, map_factor, terrain
            )
        )
    )

    def over_members(value, bit):
        return send(value, lambda k, i, j: (k ^ bit, i, j))

    def over_chips(value):
        bit = 2
        while bit < members:
            value = value + over_members(value, bit)
            bit *= 2
        return value

    given = over_members(give, 1)
    def from_beside(value, step, bit):
        return send(value, lambda k, i, j: (k ^ bit, i, (j + step) % along))

    steps = (1, -1) if along > 2 else (1,)
    near = [from_beside(side, step, 0) for step in steps]
    edges = []
    for step, n in zip(steps, near):
        total = n[:n_edges]
        for bit in range(2, members, 2):
            total = total + from_beside(edge, step, bit)
        edges.append(total)
    edges = jnp.concatenate(edges, axis=0)
    cut = STEPS * fields
    outer, inner = pl.pallas_call(
        pair_kernel,
        out_shape=(tiles(cut), tiles(half * fields - cut + 1)),
        in_specs=[VMEM] * 2,
        out_specs=(VMEM,) * 2,
        compiler_params=MODEST,
        name="pair",
    )(keep, given)
    outer = over_chips(outer)
    inner = over_chips(inner)[1:]

    other_edges = over_members(edges, 1)
    outer, other_edges = lax.optimization_barrier((outer, other_edges))
    n_ends = 2 if along == 2 else fields + 1
    message = pl.pallas_call(
        functools.partial(near_kernel, sizes, len(near)),
        out_shape=tiles(cut + 1 + n_ends),
        in_specs=[VMEM] * (6 + len(near)),
        out_specs=VMEM,
        compiler_params=MODEST,
        name="near",
    )(states, outer, metric, edges, other_edges, side, *near)
    second_in = send(message, loop_target(sizes[1], False))
    other = over_members(outer, 1)
    start, beside, first = pl.pallas_call(
        functools.partial(join_kernel, sizes, len(near)),
        out_shape=(tiles(2 * cut), tiles(len(near) * (fields + 1)), tiles(cut + 1 + n_ends)),
        in_specs=[VMEM] * (7 + len(near)),
        out_specs=(VMEM,) * 3,
        compiler_params=MODEST,
        name="join",
    )(states, outer, other, edges, other_edges, metric, side, *near)
    first_in = send(first, loop_target(sizes[1], True))
    other = over_members(inner, 1)
    strips, saved, done = pl.pallas_call(
        functools.partial(middle_kernel, sizes),
        out_shape=(
            tiles(len(near) * (fields + 1)),
            tiles(4 * (STEPS - 1) * fields),
            tiles((rows - 2 * STEPS) * fields),
        ),
        in_specs=[VMEM] * 7,
        out_specs=(VMEM,) * 3,
        scratch_shapes=[room(rows * fields), room(rows * fields)],
        compiler_params=MODEST,
        cost_estimate=pl.CostEstimate(
            flops=30 * rows * fields * levels * cols * STEPS, bytes_accessed=2**20, transcendentals=0
        ),
        name="middle",
    )(states, start, inner, other, metric, side, beside)
    out = pl.pallas_call(
        functools.partial(outer_kernel, sizes),
        out_shape=jax.ShapeDtypeStruct((fields * levels, rows, cols), jnp.float32),
        in_specs=[VMEM] * 7,
        out_specs=HBM,
        scratch_shapes=[pltpu.VMEM(flat, jnp.float32), pltpu.SemaphoreType.DMA((2,))],
        compiler_params=MODEST,
        name="outer",
    )(start, strips, saved, done, metric, first_in, second_in)
    return out.reshape(perturbed_states.shape)


def solution(mesh):
    placed = (
        P("member", None, None, "dx", "dy"),
        P("member", None, None, "dx", "dy"),
        P(),
        P("dx", "dy"),
        P("dx", "dy"),
    )
    return jax.shard_map(
        on_device,
        mesh=mesh,
        in_specs=placed,
        out_specs=P("member", None, None, "dx", "dy"),
        check_vma=False,
    )
```

```python
import functools

import jax
import jax.numpy as jnp
from jax import lax
from jax.experimental import pallas as pl
from jax.experimental.pallas import tpu as pltpu
from jax.sharding import PartitionSpec as P

STEPS = 4

integration_step = 0.2
diffusion = 0.1

OUTSIDE = 1.0e6
AXES = ("member", "dx", "dy")
VMEM = pl.BlockSpec(memory_space=pltpu.VMEM)
HBM = pl.BlockSpec(memory_space=pltpu.HBM)
MODEST = pltpu.CompilerParams(vmem_limit_bytes=8 * 2**20)


def send(value, target):
    sizes = [lax.axis_size(axis) for axis in AXES]
    pairs = []
    for member in range(sizes[0]):
        for i in range(sizes[1]):
            for j in range(sizes[2]):
                k, l, m = target(member, i, j)
                pairs.append(
                    (
                        (member * sizes[1] + i) * sizes[2] + j,
                        (k * sizes[1] + l) * sizes[2] + m,
                    )
                )
    return lax.ppermute(value, AXES, pairs)


def loop_target(rows, forward):
    def target(member, i, j):
        step = 1 if (member % 2 == 0) == forward else -1
        if 0 <= i + step < rows:
            return member, i + step, j
        return member ^ 1, i, j

    return target


def lanes_of(shape):
    return lax.broadcasted_iota(jnp.int32, shape, len(shape) - 1)


def turn(tile, by, axis=1):
    size = tile.shape[axis]
    return pltpu.roll(tile, by % size if isinstance(by, int) else lax.rem(by + size, size), axis)


def edges_of(tiles, width):
    lane = lanes_of(tiles[0].shape)
    total = None
    for x, tile in enumerate(tiles):
        moved = turn(tile, 2 * width * x + width)
        total = moved if total is None else jnp.where(lane < 2 * width * x, total, moved)
    return total


def pack_of(fields, along):
    return 2 if along == 2 and fields % 2 == 0 else 1


def packed(edges, early, has_left, along):
    if pack_of(len(edges), along) == 1:
        return edges
    by = jnp.where(has_left, -STEPS, STEPS)
    return [
        jnp.where(early == has_left, turn(b, by), a) for a, b in zip(edges[::2], edges[1::2])
    ]


def unpacked(tiles, fields, has_left, along):
    if pack_of(fields, along) == 1:
        return tiles
    by = jnp.where(has_left, -STEPS, STEPS)
    return [part for tile in tiles for part in (tile, turn(tile, by))]


def split_kernel(
    sizes, p_hbm, c_hbm, owner_hbm, m_hbm, t_hbm,
    pt_ref, keep_ref, send_ref, edge_ref, side_ref, metric_ref,
    p_ref, c_ref, owner_ref, t_ref, sems,
):
    fields, _, cols = p_ref.shape
    rows = t_ref.shape[0]
    levels = p_ref.shape[1] // rows
    half = rows // 2
    member = lax.axis_index("member")
    members = owner_ref.shape[0]
    first = lax.rem(member, 2) == 0
    copies = [
        pltpu.make_async_copy(owner_hbm, owner_ref, sems.at[0]),
        pltpu.make_async_copy(m_hbm, metric_ref.at[pl.ds(0, rows), :], sems.at[1]),
        pltpu.make_async_copy(t_hbm, t_ref, sems.at[2]),
    ]
    together = 2 if fields % 2 == 0 else 1
    for n in range(fields // together):
        some = pl.ds(n * together, together)
        copies.append(pltpu.make_async_copy(p_hbm.at[some], p_ref.at[some], sems.at[3 + 2 * n]))
        copies.append(pltpu.make_async_copy(c_hbm.at[some], c_ref.at[some], sems.at[4 + 2 * n]))
    for copy in copies:
        copy.start()
    for copy in copies[:3]:
        copy.wait()
    metric_ref[pl.ds(rows, rows), :] = t_ref[...].astype(jnp.float32)
    level = lax.broadcasted_iota(jnp.int32, (levels, cols), 0)
    columns = []
    for x in range(rows):
        scale = jnp.broadcast_to(metric_ref[pl.ds(x, 1), :], (levels, cols))
        ground = jnp.broadcast_to(metric_ref[pl.ds(rows + x, 1), :], (levels, cols))
        columns.append(jnp.where(level == 0, scale, ground))
    side_ref[side_ref.shape[0] - 1] = edges_of(columns, STEPS)
    part_edges, state_edges = [], []
    weight = jnp.float32(0.0)
    for rank in range(members):
        per_rank = 2.0 * (members - rank) / (members * (members + 1.0))
        weight = weight + jnp.where(owner_ref[rank] == member, per_rank, 0.0)
    for f in range(fields):
        if f % together == 0:
            copies[3 + 2 * (f // together)].wait()
            copies[4 + 2 * (f // together)].wait()
        states, parts = [], []
        for x in range(rows):
            state = p_ref[f, pl.ds(x, levels, stride=rows), :]
            analysis = c_ref[f, pl.ds(x, levels, stride=rows), :]
            pt_ref[x * fields + f] = state
            states.append(state)
            parts.append(weight * analysis - state * (1.0 / members))
        for r in range(half):
            keep_ref[r * fields + f] = jnp.where(first, parts[r], parts[rows - 1 - r])
            send_ref[r * fields + f] = jnp.where(first, parts[rows - 1 - r], parts[r])
        part_edges.append(edges_of(parts, STEPS))
        state_edges.append(edges_of(states, STEPS))
    early = lax.rem(lanes_of((levels, cols)), 2 * STEPS) < STEPS
    has_left, _ = has_neighbours("dy", sizes[2])
    for k, edge in enumerate(packed(part_edges, early, has_left, sizes[2])):
        edge_ref[k] = edge
        side_ref[k] = edge
    for k, edge in enumerate(packed(state_edges, early, has_left, sizes[2])):
        side_ref[edge_ref.shape[0] + k] = edge


def has_neighbours(axis, size):
    place = lax.axis_index(axis)
    return place > 0, place < size - 1


def coefficients(level, scale, ground):
    scale = jnp.broadcast_to(scale, level.shape)
    ground = jnp.broadcast_to(ground, level.shape)
    mask = (level.astype(jnp.float32) >= ground).astype(jnp.float32)
    return (
        mask * (1.0 - 6.0 * integration_step * diffusion),
        mask * (integration_step * diffusion),
        mask * (scale * (0.5 * integration_step)),
    )


def updated(level, coefs, cur, dx, sx, dy, sy):
    levels = level.shape[0]
    new = []
    for f, here in enumerate(cur):
        advected = cur[0] * dx[f] + cur[1] * dy[f]
        if f == 0:
            advected = advected + dx[2]
        elif f == 1:
            advected = advected + dy[2]
        elif f == 2:
            advected = advected + (dx[0] + dy[1])
        upper = jnp.where(level < levels - 1, turn(here, -1, 0), 0.0)
        lower = jnp.where(level > 0, turn(here, 1, 0), 0.0)
        total = (sx[f] + sy[f]) + (upper + lower)
        new.append(coefs[0] * here + coefs[1] * total - coefs[2] * advected)
    return new


def row_step(level, lane, coefs, before, cur, after, beyond, spot):
    cols = lane.shape[1]
    dx, sx, dy, sy = [], [], [], []
    for f, here in enumerate(cur):
        outer = turn(beyond[f], -spot)
        north = jnp.where(lane == cols - 1, outer, turn(here, -1))
        south = jnp.where(lane == 0, outer, turn(here, 1))
        dx.append(after[f] - before[f])
        sx.append(after[f] + before[f])
        dy.append(north - south)
        sy.append(north + south)
    return updated(level, coefs, cur, dx, sx, dy, sy)


def strip_step(level, coefs, here, group):
    dx, sx, dy, sy = [], [], [], []
    for tile in here:
        east, west = turn(tile, -group), turn(tile, group)
        north, south = turn(tile, -1), turn(tile, 1)
        dx.append(east - west)
        sx.append(east + west)
        dy.append(north - south)
        sy.append(north + south)
    return updated(level, coefs, here, dx, sx, dy, sy)


def outside_columns(lane, width, strips, has_left):
    place = lax.rem(lane, 2 * width)
    if len(strips) == 2:
        return [jnp.where(place == width - 1, a, turn(b, -2)) for a, b in zip(*strips)]
    before = jnp.logical_and(place == width - 1, has_left)
    after = jnp.logical_and(place == width - 2, jnp.logical_not(has_left))
    return [jnp.where(before, a, jnp.where(after, turn(a, -2), 0.0)) for a in strips[0]]


def strips_of(early, own, beside, has_left):
    if len(beside) == 2:
        return [jnp.where(early, beside[0], own), jnp.where(early, own, beside[1])]
    return [jnp.where(early == has_left, beside[0], own)]


def metric_rows(metric_ref, wide, up):
    rows = metric_ref.shape[0] // 2
    scale, ground = metric_ref[pl.ds(0, rows), :], metric_ref[pl.ds(rows, rows), :]
    tops = jnp.concatenate([scale[rows - wide :], ground[rows - wide :]], axis=0)
    bottoms = jnp.concatenate([scale[:wide], ground[:wide]], axis=0)
    return jnp.where(up, tops, bottoms)


def besides(sizes, fields, near, edge_ref, other_ref, sides):
    has_left, has_right = has_neighbours("dy", sizes[2])
    per_side = edge_ref.shape[0] // sides
    by_side = []
    for side in range(sides):
        own, other = (
            [ref[side * per_side + k] for k in range(per_side)] for ref in (edge_ref, other_ref)
        )
        tiles = [near[side][per_side + k] + (own[k] + other[k]) for k in range(per_side)]
        tiles = unpacked(tiles, fields, has_left, sizes[2]) + [near[side][2 * per_side]]
        if sides == 2:
            here = (has_left, has_right)[side]
            empty = [0.0] * fields + [OUTSIDE]
            tiles = [jnp.where(here, tile, e) for tile, e in zip(tiles, empty)]
        by_side.append(tiles)
    return [list(pair) for pair in zip(*by_side)]


def ends_of(strips, up, quarter):
    lane = lanes_of(strips[0][0].shape)
    cols = lane.shape[1]
    fields = len(strips) - 1
    if len(strips[0]) == 1:
        packed = None
        for f in range(fields):
            moved = turn(strips[f][0], jnp.where(up, quarter, 0) + f * quarter)
            packed = moved if f == 0 else jnp.where(lane < f * quarter, packed, moved)
        return [packed, strips[fields][0]]
    return [
        jnp.where(
            lane < quarter,
            a,
            jnp.where(
                lane < 2 * quarter,
                turn(b, quarter),
                jnp.where(lane < cols - quarter, turn(b, -quarter), a),
            ),
        )
        for a, b in strips
    ]


def near_kernel(
    sizes, n_sides, pt_ref, sum_ref, metric_ref, edge_ref, other_ref, side_ref, *refs
):
    near, (message_ref,) = refs[:n_sides], refs[n_sides:]
    rows = metric_ref.shape[0] // 2
    fields = pt_ref.shape[0] // rows
    wide = STEPS
    even = lax.rem(lax.axis_index("member"), 2) == 0
    has_left, _ = has_neighbours("dy", sizes[2])
    lane = lanes_of(pt_ref.shape[1:])
    early = lax.rem(lane, 2 * wide) < wide
    values = besides(sizes, fields, near, edge_ref, other_ref, n_sides)
    strips = []
    for f in range(fields):
        own = None
        for r in range(wide):
            x = jnp.where(even, r, rows - 1 - r)
            place = jnp.where(even, r, wide - 1 - r) * fields
            tile = pt_ref[x * fields + f] + sum_ref[r * fields + f]
            message_ref[place + f] = tile
            moved = turn(tile, 2 * wide * x + wide)
            own = moved if own is None else jnp.where(lane // (2 * wide) == x, moved, own)
        strips.append(strips_of(early, own, values[f], has_left))
    strips.append(strips_of(early, side_ref[side_ref.shape[0] - 1], values[fields], has_left))
    up = jnp.logical_not(even)
    message_ref[wide * fields] = metric_rows(metric_ref, wide, up)
    for k, end in enumerate(ends_of(strips, up, 2 * wide * wide)):
        message_ref[wide * fields + 1 + k] = end


def join_kernel(
    sizes, n_sides, pt_ref, mine_ref, theirs_ref, edge_ref, other_ref, metric_ref, side_ref, *refs
):
    near, (start_ref, beside_ref, first_ref) = refs[:n_sides], refs[n_sides:]
    rows, cols = metric_ref.shape[0] // 2, metric_ref.shape[1]
    levels = pt_ref.shape[1]
    fields = pt_ref.shape[0] // rows
    wide = STEPS
    parity = lax.rem(lax.axis_index("member"), 2)
    has_left, has_right = has_neighbours("dy", sizes[2])
    lane = lanes_of((levels, cols))
    early = lax.rem(lane, 2 * wide) < wide
    quarter = 2 * wide * wide
    sides = beside_ref.shape[0] // (fields + 1)

    for r in range(wide):
        for f in range(fields):
            mine, other = mine_ref[r * fields + f], theirs_ref[r * fields + f]
            low, high = jnp.where(parity == 0, mine, other), jnp.where(parity == 0, other, mine)
            start_ref[r * fields + f] = pt_ref[r * fields + f] + low
            end = 2 * wide - 1 - r
            start_ref[end * fields + f] = pt_ref[(rows - 1 - r) * fields + f] + high

    strips = []
    values = besides(sizes, fields, near, edge_ref, other_ref, sides)
    for f, beside in enumerate(values):
        for side in range(sides):
            beside_ref[side * (fields + 1) + f] = beside[side]
        if f < fields:
            own = None
            for k in range(2 * wide):
                x = k if k < wide else rows - 2 * wide + k
                moved = turn(start_ref[k * fields + f], 2 * wide * x + wide)
                own = moved if own is None else jnp.where(lane < 2 * wide * x, own, moved)
        else:
            own = side_ref[side_ref.shape[0] - 1]
        strips.append(strips_of(early, own, beside, has_left))
    up = parity == 0
    base = jnp.where(up, wide, 0) * fields
    for k in range(wide * fields):
        first_ref[k] = start_ref[base + k]
    first_ref[wide * fields] = metric_rows(metric_ref, wide, up)
    for k, end in enumerate(ends_of(strips, up, quarter)):
        first_ref[wide * fields + 1 + k] = end


def middle_kernel(
    sizes, pt_ref, outer_ref, mine_ref, other_ref, metric_ref, side_ref, beside_ref,
    strip_ref, saved_ref, done_ref, a_ref, b_ref,
):
    rows, cols = metric_ref.shape[0] // 2, metric_ref.shape[1]
    levels = pt_ref.shape[1]
    fields = pt_ref.shape[0] // rows
    wide = STEPS
    group = 2 * wide
    half = rows // 2
    parity = lax.rem(lax.axis_index("member"), 2)
    lane = lanes_of((levels, cols))
    level = lax.broadcasted_iota(jnp.int32, (levels, cols), 0)
    early = lax.rem(lane, group) < wide
    for r in range(wide):
        for f in range(fields):
            a_ref[r * fields + f] = outer_ref[r * fields + f]
            a_ref[(rows - 1 - r) * fields + f] = outer_ref[(group - 1 - r) * fields + f]
    for r in range(wide, half):
        for f in range(fields):
            k = (r - wide) * fields + f
            mine, other = mine_ref[k], other_ref[k]
            low, high = jnp.where(parity == 0, mine, other), jnp.where(parity == 0, other, mine)
            a_ref[r * fields + f] = pt_ref[r * fields + f] + low
            mirrored = (rows - 1 - r) * fields + f
            a_ref[mirrored] = pt_ref[mirrored] + high
    has_left, _ = has_neighbours("dy", sizes[2])
    sides = beside_ref.shape[0] // (fields + 1)
    strips = [[] for _ in range(sides)]
    for f in range(fields + 1):
        if f < fields:
            own = edges_of([a_ref[x * fields + f] for x in range(rows)], wide)
        else:
            own = side_ref[side_ref.shape[0] - 1]
        beside = [beside_ref[side * (fields + 1) + f] for side in range(sides)]
        for side, strip in enumerate(strips_of(early, own, beside, has_left)):
            strips[side].append(strip)
            strip_ref[side * (fields + 1) + f] = strip
    strip_coefs = [coefficients(level, side[fields][0:1], side[fields][1:2]) for side in strips]
    strips = [side[:fields] for side in strips]
    coefs = [
        coefficients(level, metric_ref[pl.ds(x, 1), :], metric_ref[pl.ds(rows + x, 1), :])
        for x in range(rows)
    ]
    for number in range(STEPS):
        source, sink = (a_ref, b_ref) if number % 2 == 0 else (b_ref, a_ref)
        beyond = outside_columns(lane, wide, strips, has_left)
        bottom, top = number + 1, rows - 1 - number
        row = lambda x: [source[x * fields + f] for f in range(fields)]
        before, cur = row(bottom - 1), row(bottom)
        for x in range(bottom, top):
            after = row(x + 1)
            new = row_step(
                level, lane, coefs[x], before, cur, after, beyond, group * x + wide - 1
            )
            edge = {bottom: 0, bottom + 1: 1, top - 2: 2, top - 1: 3}.get(x)
            for f in range(fields):
                if number == STEPS - 1:
                    done_ref[(x - wide) * fields + f] = new[f]
                else:
                    sink[x * fields + f] = new[f]
                    if edge is not None:
                        saved_ref[(4 * number + edge) * fields + f] = new[f]
            before, cur = cur, after
        if number < STEPS - 1:
            strips = [
                strip_step(level, coef, tiles, group) for coef, tiles in zip(strip_coefs, strips)
            ]


def outer_kernel(
    sizes, outer_ref, strip_ref, saved_ref, done_ref, metric_ref, first_ref, second_ref,
    out_hbm, out_ref, sems,
):
    rows, cols = metric_ref.shape[0] // 2, metric_ref.shape[1]
    levels = outer_ref.shape[1]
    wide = STEPS
    group = 2 * wide
    fields = outer_ref.shape[0] // group
    half = rows // 2
    even = lax.rem(lax.axis_index("member"), 2) == 0
    has_low, has_high = has_neighbours("dx", sizes[1])
    lane = lanes_of((levels, cols))
    level = lax.broadcasted_iota(jnp.int32, (levels, cols), 0)
    quarter = group * wide

    def low(k, empty=0.0):
        return jnp.where(has_low, jnp.where(even, first_ref[k], second_ref[k]), empty)

    def high(k, empty=0.0):
        return jnp.where(has_high, jnp.where(even, second_ref[k], first_ref[k]), empty)

    has_left, _ = has_neighbours("dy", sizes[2])
    sides = strip_ref.shape[0] // (fields + 1)

    def stretched(is_low, side, f):
        mine = strip_ref[side * (fields + 1) + f]
        empty = 0.0 if f < fields else OUTSIDE
        if sides == 1 and f < fields:
            k, by = 0, (-f if is_low else -1 - f)
        else:
            k, by = min(f, 1) if sides == 1 else f, ((1, 2) if is_low else (-1, 2))[side]
        theirs = turn((low if is_low else high)(wide * fields + 1 + k, empty), by * quarter)
        if is_low:
            return jnp.where(lane < quarter, theirs, turn(mine, quarter))
        return jnp.where(lane < cols - quarter, turn(mine, -quarter), theirs)

    beyond = {}
    for is_low in (True, False):
        strips = [[stretched(is_low, side, f) for f in range(fields + 1)] for side in range(sides)]
        coefs = [coefficients(level, side[fields][0:1], side[fields][1:2]) for side in strips]
        strips = [side[:fields] for side in strips]
        for number in range(STEPS):
            beyond[is_low, number] = outside_columns(lane, wide, strips, has_left)
            if number < STEPS - 1:
                strips = [strip_step(level, c, tiles, group) for c, tiles in zip(coefs, strips)]

    for x in range(wide, rows - wide):
        for f in range(fields):
            out_ref[f, pl.ds(x, levels, stride=rows), :] = done_ref[(x - wide) * fields + f]

    def saved(number, edge):
        return [saved_ref[(4 * (number - 1) + edge) * fields + f] for f in range(fields)]

    def prepare(is_low):
        metric = wide * fields
        halo = low(metric, OUTSIDE) if is_low else high(metric, OUTSIDE)
        coefs, state = {}, {}
        for r in range(wide):
            message = [(low if is_low else high)(r * fields + f) for f in range(fields)]
            state[r - wide if is_low else rows + r] = message
            coefs[r - wide if is_low else rows + r] = coefficients(
                level, halo[r : r + 1], halo[wide + r : wide + r + 1]
            )
            x = r if is_low else rows - wide + r
            k = r if is_low else wide + r
            state[x] = [outer_ref[k * fields + f] for f in range(fields)]
            coefs[x] = coefficients(
                level, metric_ref[pl.ds(x, 1), :], metric_ref[pl.ds(rows + x, 1), :]
            )
        return state, coefs

    def advanced(is_low, number, state, coefs):
        if number > 0:
            if is_low:
                state[number], state[number + 1] = saved(number, 0), saved(number, 1)
            else:
                state[rows - 2 - number], state[rows - 1 - number] = saved(number, 2), saved(number, 3)
        bottom = number + 1 - wide if is_low else rows - 1 - number
        new = {}
        for x in range(bottom, bottom + wide):
            spot = group * (x + (wide if is_low else -wide)) + wide - 1
            new[x] = row_step(
                level, lane, coefs[x], state[x - 1], state[x], state[x + 1],
                beyond[is_low, number], spot,
            )
        return new

    parts = {is_low: prepare(is_low) for is_low in (True, False)}
    for number in range(STEPS):
        for is_low, (state, coefs) in parts.items():
            parts[is_low] = advanced(is_low, number, state, coefs), coefs
    for state, _ in parts.values():
        for x, tiles in state.items():
            for f in range(fields):
                out_ref[f, pl.ds(x, levels, stride=rows), :] = tiles[f]

    copies = []
    for n, is_low in enumerate((True, False)):
        part = pl.ds(n * half, half)
        source = out_ref.reshape(fields * levels, rows, cols)
        copies.append(
            pltpu.make_async_copy(source.at[:, part, :], out_hbm.at[:, part, :], sems.at[n])
        )
        copies[-1].start()
    for copy in copies:
        copy.wait()


def pair_kernel(keep_ref, given_ref, outer_ref, inner_ref):
    count, skip = outer_ref.shape[0], keep_ref.shape[0] - inner_ref.shape[0]
    for k in range(keep_ref.shape[0]):
        total = keep_ref[k] + given_ref[k]
        if k < count:
            outer_ref[k] = total
        if k >= skip:
            inner_ref[k - skip] = total


def on_device(perturbed_states, control, owner, map_factor, terrain):
    _, fields, levels, rows, cols = perturbed_states.shape
    sizes = tuple(lax.axis_size(axis) for axis in AXES)
    members, along = sizes[0], sizes[2]
    half = rows // 2
    n_edges = fields // pack_of(fields, along)
    tile = (levels, cols)

    def tiles(count):
        return jax.ShapeDtypeStruct((count, *tile), jnp.float32)

    def room(count):
        return pltpu.VMEM((count, *tile), jnp.float32)

    flat = (fields, levels * rows, cols)
    states, keep, give, edge, side, metric = pl.pallas_call(
        functools.partial(split_kernel, sizes),
        out_shape=(
            tiles(rows * fields),
            tiles(half * fields),
            tiles(half * fields),
            tiles(n_edges),
            tiles(2 * n_edges + 1),
            jax.ShapeDtypeStruct((2 * rows, cols), jnp.float32),
        ),
        in_specs=[HBM] * 5,
        out_specs=(VMEM,) * 6,
        scratch_shapes=[
            pltpu.VMEM(flat, jnp.float32),
            pltpu.VMEM(flat, jnp.float32),
            pltpu.SMEM(owner.shape, jnp.int32),
            pltpu.VMEM((rows, cols), jnp.int32),
            pltpu.SemaphoreType.DMA((2 * fields + 3,)),
        ],
        compiler_params=MODEST,
        name="split",
    )(
        *(
            pltpu.with_memory_space_constraint(value, pltpu.HBM)
            for value in (
                perturbed_states.reshape(flat), control.reshape(flat), owner, map_factor, terrain
            )
        )
    )

    def over_members(value, bit):
        return send(value, lambda k, i, j: (k ^ bit, i, j))

    def over_chips(value):
        bit = 2
        while bit < members:
            value = value + over_members(value, bit)
            bit *= 2
        return value

    given = over_members(give, 1)
    def from_beside(value, step, bit):
        return send(value, lambda k, i, j: (k ^ bit, i, (j + step) % along))

    steps = (1, -1) if along > 2 else (1,)
    near = [from_beside(side, step, 0) for step in steps]
    edges = []
    for step, n in zip(steps, near):
        total = n[:n_edges]
        for bit in range(2, members, 2):
            total = total + from_beside(edge, step, bit)
        edges.append(total)
    edges = jnp.concatenate(edges, axis=0)
    cut = STEPS * fields
    outer, inner = pl.pallas_call(
        pair_kernel,
        out_shape=(tiles(cut), tiles(half * fields - cut + 2)),
        in_specs=[VMEM] * 2,
        out_specs=(VMEM,) * 2,
        compiler_params=MODEST,
        name="pair",
    )(keep, given)
    outer = over_chips(outer)
    inner = over_chips(inner)[2:]

    other_edges = over_members(edges, 1)
    outer, other_edges = lax.optimization_barrier((outer, other_edges))
    n_ends = 2 if along == 2 else fields + 1
    message = pl.pallas_call(
        functools.partial(near_kernel, sizes, len(near)),
        out_shape=tiles(cut + 1 + n_ends),
        in_specs=[VMEM] * (6 + len(near)),
        out_specs=VMEM,
        compiler_params=MODEST,
        name="near",
    )(states, outer, metric, edges, other_edges, side, *near)
    second_in = send(message, loop_target(sizes[1], False))
    other = over_members(outer, 1)
    start, beside, first = pl.pallas_call(
        functools.partial(join_kernel, sizes, len(near)),
        out_shape=(tiles(2 * cut), tiles(len(near) * (fields + 1)), tiles(cut + 1 + n_ends)),
        in_specs=[VMEM] * (7 + len(near)),
        out_specs=(VMEM,) * 3,
        compiler_params=MODEST,
        name="join",
    )(states, outer, other, edges, other_edges, metric, side, *near)
    first_in = send(first, loop_target(sizes[1], True))
    inner, _ = lax.optimization_barrier((inner, first))
    other = over_members(inner, 1)
    strips, saved, done = pl.pallas_call(
        functools.partial(middle_kernel, sizes),
        out_shape=(
            tiles(len(near) * (fields + 1)),
            tiles(4 * (STEPS - 1) * fields),
            tiles((rows - 2 * STEPS) * fields),
        ),
        in_specs=[VMEM] * 7,
        out_specs=(VMEM,) * 3,
        scratch_shapes=[room(rows * fields), room(rows * fields)],
        compiler_params=MODEST,
        cost_estimate=pl.CostEstimate(
            flops=30 * rows * fields * levels * cols * STEPS, bytes_accessed=2**20, transcendentals=0
        ),
        name="middle",
    )(states, start, inner, other, metric, side, beside)
    out = pl.pallas_call(
        functools.partial(outer_kernel, sizes),
        out_shape=jax.ShapeDtypeStruct((fields * levels, rows, cols), jnp.float32),
        in_specs=[VMEM] * 7,
        out_specs=HBM,
        scratch_shapes=[pltpu.VMEM(flat, jnp.float32), pltpu.SemaphoreType.DMA((2,))],
        compiler_params=MODEST,
        name="outer",
    )(start, strips, saved, done, metric, first_in, second_in)
    return out.reshape(perturbed_states.shape)


def solution(mesh):
    placed = (
        P("member", None, None, "dx", "dy"),
        P("member", None, None, "dx", "dy"),
        P(),
        P("dx", "dy"),
        P("dx", "dy"),
    )
    return jax.shard_map(
        on_device,
        mesh=mesh,
        in_specs=placed,
        out_specs=P("member", None, None, "dx", "dy"),
        check_vma=False,
    )
```
